256 devices in a mesh: orb: 16 (over y_lo, z), slab: 16 (over y_hi, x, core).
Axes of the slice: x: 4, y: 4 (y_hi: 2, y_lo: 2; y = y_hi * 2 + y_lo), z: 8, core: 2. Of those that a mesh axis runs over, the one named last changes fastest.
Arguments:
- psi_re: float32 [16, 128, 256, 256], P('orb', 'slab'), may hold values from -6 to 6
- psi_im: float32 [16, 128, 256, 256], P('orb', 'slab'), may hold values from -6 to 6
- v_local: float32 [128, 256, 256], P('slab'), may hold values from -5 to 1
- n_ground: float32 [128, 256, 256], P('slab', 'orb'), may hold values from 1 to 10
Outputs:
- psi_re_out: float32 [16, 128, 256, 256], P('orb', 'slab')
- psi_im_out: float32 [16, 128, 256, 256], P('orb', 'slab')
The draws below stay inside these ranges and needn't reach their ends.
All inputs are finite; a program needn't handle non-finite values.
Results may differ from the reference program's by a relative error of at most 0.0001.
Values sent between devices are 32-bit elements; how exact they have to be, the bound alone decides.
No kernel may reach another device: no remote copies, remote signals or barrier semaphores. Data moves between devices by JAX's collectives and lax.ppermute only.
A program may use at most 128 MiB of HBM per device.

```python
import math
import jax
import jax.numpy as jnp
from jax import lax

NX = 256
NY = 256
NZ = 128
STEPS = 1
ORBS = 16


def orbital_values(key):
    values = jnp.clip(jax.random.normal(key, (ORBS, NZ, NY, NX), jnp.float32), -6.0, 6.0)
    return values


def draw_psi_re(key, part):
    key = jax.random.fold_in(key, 1)
    return orbital_values(key)


def draw_psi_im(key, part):
    key = jax.random.fold_in(key, 2)
    return orbital_values(key)


def draw_n_ground(key, part):
    key = jax.random.fold_in(key, 3)
    values = jax.random.uniform(key, (NZ, NY, NX), jnp.float32, 3.0, 5.0)
    return values


def block_levels(own_key, extent, split, least, top_value):
    level, own = 1.0, jax.random.fold_in(own_key, 6)
    for position, parts in split:
        steps = jnp.exp(jax.random.uniform(jax.random.fold_in(own, position), (parts,), jnp.float32, least / len(split), top_value / len(split)))
        level = level * jnp.repeat(steps, extent[position] // parts).reshape([-1 if axis == position else 1 for axis in range(len(extent))])
    return level


def setup_inputs(seed: int = 0) -> dict:
    streams_of = jax.random.split(jax.random.key(seed), 5)
    psi_re = draw_psi_re(jax.random.fold_in(streams_of[4], 71), 0)
    psi_im = draw_psi_im(jax.random.fold_in(streams_of[4], 71), 0)
    v_local = jnp.clip(-5.0 + 6.0 * jax.random.uniform(streams_of[2], (NZ, NY, NX), jnp.float32) ** block_levels(streams_of[2], (NZ, NY, NX), ((0, 16),), -0.2, 0.2), -5.0, 1.0)
    n_ground = draw_n_ground(jax.random.fold_in(streams_of[4], 71), 0)
    return {"psi_re": psi_re, "psi_im": psi_im, "v_local": v_local, "n_ground": n_ground}


SPACING = 0.5
TIME_STEP = 0.02


def wave_sq(freq_index, length):
    signed = jnp.where(freq_index * 2 <= length, freq_index, freq_index - length)
    wave_number = signed.astype(jnp.float32) * (2.0 * math.pi / (length * SPACING))
    return wave_number * wave_number


def greens_block(z_index, y_index, x_index, z_len, y_len, x_len):
    wave_total = wave_sq(z_index, z_len)[:, None, None] + wave_sq(y_index, y_len)[None, :, None] + wave_sq(x_index, x_len)[None, None, :]
    anchor = (z_index[:, None, None] == 0) & (y_index[None, :, None] == 0) & (x_index[None, None, :] == 0)
    safe = jnp.where(anchor, jnp.float32(1.0), wave_total)
    return jnp.where(anchor, jnp.float32(0.0), (4.0 * math.pi) / safe)


def apply_h(values, potential):
    laplace = (jnp.roll(values, 1, 2) + jnp.roll(values, -1, 2)) + (jnp.roll(values, 1, 1) + jnp.roll(values, -1, 1)) + (jnp.roll(values, -1, 0) + jnp.roll(values, 1, 0)) - 6.0 * values
    return (-0.5 / (SPACING * SPACING)) * laplace + potential * values


def advance(real_part, imag_part, potential):
    first_re = apply_h(real_part, potential)
    first_im = apply_h(imag_part, potential)
    second_re = apply_h(first_re, potential)
    second_im = apply_h(first_im, potential)
    half_sq = 0.5 * TIME_STEP * TIME_STEP
    new_re = real_part + TIME_STEP * first_im - half_sq * second_re
    new_im = imag_part - TIME_STEP * first_re - half_sq * second_im
    return new_re, new_im


def reference(psi_re, psi_im, v_local, n_ground):
    greens = greens_block(jnp.arange(NZ, dtype=jnp.int32), jnp.arange(NY, dtype=jnp.int32), jnp.arange(NX, dtype=jnp.int32), NZ, NY, NX)
    for step_index in range(STEPS):
        density = (2.0 / ORBS) * jnp.sum(psi_re * psi_re + psi_im * psi_im, axis=0) - n_ground
        spectrum = jnp.fft.fftn(density)
        hartree = jnp.real(jnp.fft.ifftn(spectrum * greens)).astype(jnp.float32)
        potential = v_local + hartree
        psi_re, psi_im = lax.map(lambda fields: advance(fields[0], fields[1], potential), (psi_re, psi_im))
    return psi_re, psi_im
```

```python
import functools
import math

import jax
import jax.numpy as jnp
import numpy as np
from jax import lax
from jax.experimental import pallas as pl
from jax.experimental.pallas import tpu as pltpu
from jax.sharding import PartitionSpec as P

SPACING = 0.5
TIME_STEP = 0.02
HALF_SQ = 0.5 * TIME_STEP * TIME_STEP
KINETIC = -0.5 / (SPACING * SPACING)
HIGHEST = lax.Precision.HIGHEST
Z_RING = 8
STRIP = 32
MIB = 1 << 20


def cas_table(length):
    index = np.arange(length)
    angles = (index[:, None] * index[None, :] % length) * (2.0 * math.pi / length)
    return jnp.asarray((np.cos(angles) + np.sin(angles)).astype(np.float32))


def dot(left, right):
    return jnp.dot(left, right, precision=HIGHEST, preferred_element_type=jnp.float32)


def fill_rows(rows_ref, table_ref, offsets, width):
    place = lax.axis_index("orb")
    z = lax.rem(place, Z_RING)
    y = place // Z_RING
    half = width // 2
    for block, offset in enumerate(offsets):
        owner = lax.rem(z + offset, Z_RING)
        for part in range(2):
            side = y if part == 0 else 1 - y
            start = pl.multiple_of(owner * width + side * half, half)
            rows_ref[block * width + part * half : block * width + (part + 1) * half, :] = table_ref[
                pl.ds(start, half), :
            ]


def density_kernel(scale, psi_re, psi_im, ground, table, *rest):
    outs, (rows, rho) = rest[:-2], rest[-2:]
    width = rows.shape[0] // Z_RING
    ground_rows = ground.shape[1]

    @pl.when(pl.program_id(0) == 0)
    def _():
        fill_rows(rows, table, range(Z_RING), width)

    re, im = psi_re[0, 0], psi_im[0, 0]
    rho[...] = scale * (re * re + im * im)
    start = pl.multiple_of(lax.axis_index("orb") * ground_rows, ground_rows)
    own = pl.ds(start, ground_rows)
    rho[own, :] = rho[own, :] - ground[0]
    image = dot(rows[...], rho[...])
    at = 0
    for out in outs:
        out[0] = image[at : at + out.shape[1]]
        at += out.shape[1]


def density_pieces(psi_re, psi_im, n_ground, table, total_orbs):
    _, planes, ny, nx = psi_re.shape
    width = ny // Z_RING
    heights = [width] * 4 + [width // 2] * 2 + [width] * 3
    return pl.pallas_call(
        functools.partial(density_kernel, 2.0 / total_orbs),
        grid=(planes,),
        in_specs=[
            pl.BlockSpec((1, 1, ny, nx), lambda i: (0, i, 0, 0)),
            pl.BlockSpec((1, 1, ny, nx), lambda i: (0, i, 0, 0)),
            pl.BlockSpec((1,) + n_ground.shape[1:], lambda i: (i, 0, 0)),
            pl.BlockSpec((ny, ny), lambda i: (0, 0)),
        ],
        out_specs=[pl.BlockSpec((1, h, nx), lambda i: (i, 0, 0)) for h in heights],
        out_shape=[jax.ShapeDtypeStruct((planes, h, nx), jnp.float32) for h in heights],
        scratch_shapes=[pltpu.VMEM((ny, ny), jnp.float32), pltpu.VMEM((ny, nx), jnp.float32)],
        compiler_params=pltpu.CompilerParams(vmem_limit_bytes=16 * MIB),
        cost_estimate=pl.CostEstimate(flops=12 * planes * ny * ny * nx, bytes_accessed=6 * MIB, transcendentals=0),
        name="density_y",
    )(psi_re, psi_im, n_ground, table)


def wave_sq(freq_index, length):
    signed = jnp.where(freq_index * 2 <= length, freq_index, freq_index - length)
    wave_number = signed.astype(jnp.float32) * (2.0 * math.pi / (length * SPACING))
    return wave_number * wave_number


def solve_kernel(y_len, field, x_table, z_table, out, work):
    nz, nx = field.shape
    planes = out.shape[1] - 2
    place = lax.axis_index("orb")
    width = y_len // Z_RING
    ky = lax.rem(place, Z_RING) * width + (place // Z_RING) * (width // 2) + lax.axis_index("slab")
    z_index = lax.broadcasted_iota(jnp.int32, (nz, nx), 0)
    x_index = lax.broadcasted_iota(jnp.int32, (nz, nx), 1)
    y_index = jnp.full((nz, nx), ky, jnp.int32)
    total = wave_sq(z_index, nz) + wave_sq(y_index, y_len) + wave_sq(x_index, nx)
    anchor = (z_index == 0) & (y_index == 0) & (x_index == 0)
    safe = jnp.where(anchor, jnp.float32(1.0), total)
    greens = jnp.where(anchor, jnp.float32(0.0), (4.0 * math.pi) / safe) * (1.0 / (nz * y_len * nx))
    spectrum = dot(z_table[...], dot(field[...], x_table[...]))
    work[...] = dot(dot(z_table[...], spectrum * greens), x_table[...])
    slabs = out.shape[0]
    for slab in range(slabs):
        first = slab * planes
        out[slab, 0:planes] = work[first : first + planes]
        below = (first - 1) % nz
        above = (first + planes) % nz
        out[slab, planes : planes + 1] = work[below : below + 1]
        out[slab, planes + 1 : planes + 2] = work[above : above + 1]


def solve(field, x_table, z_table, y_len, planes):
    nz, nx = field.shape
    return pl.pallas_call(
        functools.partial(solve_kernel, y_len),
        out_shape=jax.ShapeDtypeStruct((nz // planes, planes + 2, nx), jnp.float32),
        scratch_shapes=[pltpu.VMEM((nz, nx), jnp.float32)],
        compiler_params=pltpu.CompilerParams(vmem_limit_bytes=8 * MIB),
        name="solve_xz",
    )(field, x_table, z_table)


def in_plane(ref, slot, start, rows):
    mid = ref[slot, pl.ds(start, STRIP), :]
    before = ref[slot, pl.ds(pl.multiple_of(lax.rem(start + rows - 8, rows), 8), 8), :]
    after = ref[slot, pl.ds(pl.multiple_of(lax.rem(start + STRIP, rows), 8), 8), :]
    tall = jnp.concatenate([before, mid, after], axis=0)
    height = tall.shape[0]
    columns = mid.shape[1]
    up = pltpu.roll(tall, 1, 0)[8 : 8 + STRIP]
    down = pltpu.roll(tall, height - 1, 0)[8 : 8 + STRIP]
    left = pltpu.roll(mid, 1, 1)
    right = pltpu.roll(mid, columns - 1, 1)
    return mid, (up + down) + (left + right)


def kinetic(ref, below, slot, above, start, rows):
    mid, ring = in_plane(ref, slot, start, rows)
    strip = pl.ds(start, STRIP)
    total = ring + (ref[below, strip, :] + ref[above, strip, :])
    return mid, KINETIC * (total - 6.0 * mid)


def kinetic_kernel(
    planes, psi_re, psi_im, lo_re, lo_im, hi_re, hi_im, t1_re, t1_im, base_re, base_im, field_re, field_im, once_re, once_im
):
    step = pl.program_id(0)
    rows = field_re.shape[1]
    s0, s1, s2 = lax.rem(step + 1, 3), lax.rem(step + 2, 3), lax.rem(step, 3)

    @pl.when(step < 2)
    def _():
        field_re[s2] = lo_re[0]
        field_im[s2] = lo_im[0]

    @pl.when((step >= 2) & (step < planes + 2))
    def _():
        field_re[s2] = psi_re[0, 0]
        field_im[s2] = psi_im[0, 0]

    @pl.when(step >= planes + 2)
    def _():
        field_re[s2] = hi_re[0]
        field_im[s2] = hi_im[0]

    @pl.when(step >= 2)
    def _():
        @pl.loop(0, rows // STRIP)
        def _(index):
            start = pl.multiple_of(index * STRIP, STRIP)
            for field, once in ((field_re, once_re), (field_im, once_im)):
                _, value = kinetic(field, s0, s1, s2, start, rows)
                once[s1, pl.ds(start, STRIP), :] = value

    @pl.when((step >= 3) & (step < planes + 3))
    def _():
        t1_re[0] = once_re[s1]
        t1_im[0] = once_im[s1]

    @pl.when(step >= 4)
    def _():
        @pl.loop(0, rows // STRIP)
        def _(index):
            start = pl.multiple_of(index * STRIP, STRIP)
            strip = pl.ds(start, STRIP)
            first_re, second_re = kinetic(once_re, s2, s0, s1, start, rows)
            first_im, second_im = kinetic(once_im, s2, s0, s1, start, rows)
            base_re[0, strip, :] = field_re[s0, strip, :] + TIME_STEP * first_im - HALF_SQ * second_re
            base_im[0, strip, :] = field_im[s0, strip, :] - TIME_STEP * first_re - HALF_SQ * second_im


def kinetic_parts(psi_re, psi_im, low, high):
    _, planes, ny, nx = psi_re.shape

    def clip(value, top):
        return jnp.clip(value, 0, top)

    plane = (1, ny, nx)
    own = pl.BlockSpec((1, 1, ny, nx), lambda i: (0, clip(i - 2, planes - 1), 0, 0))
    out = jax.ShapeDtypeStruct((planes, ny, nx), jnp.float32)
    return pl.pallas_call(
        functools.partial(kinetic_kernel, planes),
        grid=(planes + 4,),
        in_specs=[
            own,
            own,
            pl.BlockSpec(plane, lambda i: (clip(i, 1), 0, 0)),
            pl.BlockSpec(plane, lambda i: (2 + clip(i, 1), 0, 0)),
            pl.BlockSpec(plane, lambda i: (clip(i - planes - 2, 1), 0, 0)),
            pl.BlockSpec(plane, lambda i: (2 + clip(i - planes - 2, 1), 0, 0)),
        ],
        out_specs=[
            pl.BlockSpec(plane, lambda i: (clip(i - 3, planes - 1), 0, 0)),
            pl.BlockSpec(plane, lambda i: (clip(i - 3, planes - 1), 0, 0)),
            pl.BlockSpec(plane, lambda i: (clip(i - 4, planes - 1), 0, 0)),
            pl.BlockSpec(plane, lambda i: (clip(i - 4, planes - 1), 0, 0)),
        ],
        out_shape=[out] * 4,
        scratch_shapes=[pltpu.VMEM((3, ny, nx), jnp.float32)] * 4,
        compiler_params=pltpu.CompilerParams(vmem_limit_bytes=24 * MIB),
        cost_estimate=pl.CostEstimate(flops=100 * planes * ny * nx, bytes_accessed=14 * MIB, transcendentals=0),
        name="kinetic_parts",
    )(psi_re, psi_im, low, low, high, high)


def update_kernel(planes, blocks, *refs):
    pieces = refs[:blocks]
    (table, v_own, v_lo, v_hi, psi_re, psi_im, lo_re, lo_im, hi_re, hi_im) = refs[blocks : blocks + 10]
    (t1_re, t1_im, base_re, base_im, out_re, out_im, rows, columns, pot, w_re, w_im) = refs[blocks + 10 :]
    step = pl.program_id(0)
    ny = rows.shape[0]
    width = ny // Z_RING
    s0, s1, s2 = lax.rem(step + 1, 3), lax.rem(step + 2, 3), lax.rem(step, 3)

    @pl.when(step == 0)
    def _():
        fill_rows(rows, table, (0, 7, 6, 5, 4, 3, 2, 1), width)
        columns[...] = rows[...].T

    hat = jnp.concatenate([piece[0] for piece in pieces], axis=0)
    hartree = dot(columns[...], hat)

    def place(local, re, im):
        total = local + hartree
        pot[s2] = total
        w_re[s2] = total * re
        w_im[s2] = total * im

    @pl.when(step == 0)
    def _():
        place(v_lo[0], lo_re[0], lo_im[0])

    @pl.when((step >= 1) & (step <= planes))
    def _():
        place(v_own[0], psi_re[0, 0], psi_im[0, 0])

    @pl.when(step == planes + 1)
    def _():
        place(v_hi[0], hi_re[0], hi_im[0])

    @pl.when(step >= 2)
    def _():
        @pl.loop(0, ny // STRIP)
        def _(index):
            start = pl.multiple_of(index * STRIP, STRIP)
            strip = pl.ds(start, STRIP)
            local = pot[s1, strip, :]
            mid_re, kin_re = kinetic(w_re, s0, s1, s2, start, ny)
            mid_im, kin_im = kinetic(w_im, s0, s1, s2, start, ny)
            second_re = kin_re + local * (t1_re[0, strip, :] + mid_re)
            second_im = kin_im + local * (t1_im[0, strip, :] + mid_im)
            out_re[0, 0, strip, :] = base_re[0, strip, :] + TIME_STEP * mid_im - HALF_SQ * second_re
            out_im[0, 0, strip, :] = base_im[0, strip, :] - TIME_STEP * mid_re - HALF_SQ * second_im


def update(pieces, table, v_local, psi_re, psi_im, low, high, parts):
    _, planes, ny, nx = psi_re.shape

    def clip(value):
        return jnp.clip(value, 0, planes - 1)

    def hat_plane(i):
        return jnp.where(i == 0, planes, jnp.where(i == planes + 1, planes + 1, i - 1))

    plane = (1, ny, nx)
    own = pl.BlockSpec((1, 1, ny, nx), lambda i: (0, clip(i - 1), 0, 0))
    late = pl.BlockSpec(plane, lambda i: (clip(i - 2), 0, 0))
    out = pl.BlockSpec((1, 1, ny, nx), lambda i: (0, clip(i - 2), 0, 0))

    def fixed(which):
        return pl.BlockSpec(plane, lambda i: (which, 0, 0))

    return pl.pallas_call(
        functools.partial(update_kernel, planes, len(pieces)),
        grid=(planes + 2,),
        in_specs=[pl.BlockSpec((1,) + piece.shape[1:], lambda i: (hat_plane(i), 0, 0)) for piece in pieces]
        + [
            pl.BlockSpec((ny, ny), lambda i: (0, 0)),
            pl.BlockSpec(plane, lambda i: (clip(i - 1), 0, 0)),
            fixed(4),
            fixed(4),
            own,
            own,
            fixed(1),
            fixed(3),
            fixed(0),
            fixed(2),
            late,
            late,
            late,
            late,
        ],
        out_specs=[out, out],
        out_shape=[jax.ShapeDtypeStruct(psi_re.shape, jnp.float32)] * 2,
        scratch_shapes=[pltpu.VMEM((ny, ny), jnp.float32)] * 2 + [pltpu.VMEM((3, ny, nx), jnp.float32)] * 3,
        compiler_params=pltpu.CompilerParams(vmem_limit_bytes=24 * MIB),
        cost_estimate=pl.CostEstimate(flops=12 * (planes + 2) * ny * ny * nx, bytes_accessed=22 * MIB, transcendentals=0),
        name="update",
    )(*pieces, table, v_local, low, high, psi_re, psi_im, low, low, high, high, *parts)


def ring_pairs(shift):
    return [(y * Z_RING + z, y * Z_RING + (z + shift) % Z_RING) for y in range(2) for z in range(Z_RING)]


def forward(value):
    return lax.ppermute(value, "orb", ring_pairs(1))


def backward(value):
    return lax.ppermute(value, "orb", ring_pairs(-1))


def swap(value):
    return lax.ppermute(value, "orb", [(i, (i + Z_RING) % (2 * Z_RING)) for i in range(2 * Z_RING)])


def sum_over_orb(pieces):
    s0, s1, s2, s3, s4_first, s4_second, s5, s6, s7 = pieces
    half = s4_first.shape[1]
    got_up, got_down = forward(s4_first), backward(s4_second)
    up = jnp.concatenate([s3[:, :half] + got_up, s3[:, half:]], axis=1)
    down = jnp.concatenate([s5[:, :half], s5[:, half:] + got_down], axis=1)
    up, down = forward(up), backward(down)
    up, down = forward(up + s2), backward(down + s6)
    up, down = forward(up + s1), backward(down + s7)
    total = up + down + s0
    return total[:, :half] + swap(total[:, half:])


def gather_over_orb(block):
    half = block.shape[1]
    both = jnp.concatenate([block, swap(block)], axis=1)
    up1, down1 = forward(both), backward(both)
    up2, down2 = forward(up1), backward(down1)
    up3, down3 = forward(up2), backward(down2)
    up4, down4 = forward(up3[:, :half]), backward(down3[:, half:])
    return [both, up1, up2, up3, up4, down4, down3, down2, down1]


def on_device(psi_re, psi_im, v_local, n_ground):
    total_orbs = psi_re.shape[0] * lax.axis_size("orb")
    slabs = lax.axis_size("slab")
    planes, ny, nx = v_local.shape
    nz = planes * slabs
    y_table, x_table, z_table = cas_table(ny), cas_table(nx), cas_table(nz)

    pieces = density_pieces(psi_re, psi_im, n_ground, y_table, total_orbs)

    def edge(first, v_plane):
        return jnp.concatenate(
            [psi_re[0, first : first + 2], psi_im[0, first : first + 2], v_local[v_plane : v_plane + 1]], axis=0
        )

    low = lax.ppermute(edge(planes - 2, planes - 1), "slab", [(i, (i + 1) % slabs) for i in range(slabs)])
    high = lax.ppermute(edge(0, 0), "slab", [((i + 1) % slabs, i) for i in range(slabs)])
    parts = kinetic_parts(psi_re, psi_im, low, high)

    rows = sum_over_orb(pieces)
    pencils = lax.all_to_all(jnp.transpose(rows, (1, 0, 2)), "slab", split_axis=0, concat_axis=0, tiled=True)
    solved = solve(pencils.reshape(nz, nx), x_table, z_table, ny, planes)
    back = lax.all_to_all(solved, "slab", split_axis=0, concat_axis=0, tiled=True)
    hats = gather_over_orb(jnp.transpose(back, (1, 0, 2)))
    new_re, new_im = update(hats, y_table, v_local, psi_re, psi_im, low, high, parts)
    return new_re, new_im


def solution(mesh):
    placed = (
        P("orb", "slab", None, None),
        P("orb", "slab", None, None),
        P("slab", None, None),
        P("slab", "orb", None),
    )
    return jax.shard_map(
        on_device,
        mesh=mesh,
        in_specs=placed,
        out_specs=(P("orb", "slab", None, None), P("orb", "slab", None, None)),
        check_vma=False,
    )
```

```python
import functools
import math

import jax
import jax.numpy as jnp
import numpy as np
from jax import lax
from jax.experimental import pallas as pl
from jax.experimental.pallas import tpu as pltpu
from jax.sharding import Mesh
from jax.sharding import PartitionSpec as P

SPACING = 0.5
TIME_STEP = 0.02
HALF_SQ = 0.5 * TIME_STEP * TIME_STEP
KINETIC = -0.5 / (SPACING * SPACING)
HIGHEST = lax.Precision.HIGHEST
SIDES = 2
STRIP = 32
MIB = 1 << 20
VMEM = pl.BlockSpec(memory_space=pltpu.VMEM)
ANY = pl.BlockSpec(memory_space=pl.ANY)


def cas_table(length):
    index = np.arange(length)
    angles = (index[:, None] * index[None, :] % length) * (2.0 * math.pi / length)
    return jnp.asarray((np.cos(angles) + np.sin(angles)).astype(np.float32))


def dot(left, right):
    return jnp.dot(left, right, precision=HIGHEST, preferred_element_type=jnp.float32)


def shaped(*shape):
    return jax.ShapeDtypeStruct(shape, jnp.float32)


def plane_scratch(*lead, ny, nx):
    return pltpu.VMEM(lead + (ny, nx), jnp.float32)


def cost(planes, weight):
    return pl.CostEstimate(flops=planes * weight, bytes_accessed=planes * MIB // 2, transcendentals=0)


def fill_rows(rows, table):
    ring = lax.axis_size("z")
    width = rows.shape[0] // ring
    z = lax.axis_index("z")
    for offset in range(ring):
        start = pl.multiple_of(lax.rem(z + offset, ring) * width, width)
        rows[offset * width : (offset + 1) * width, :] = table[pl.ds(start, width), :]


def density_kernel(scale, psi_re, psi_im, v_local, ground, y_table, *refs):
    pieces, (near_re, near_im, to_prev, to_next) = refs[:9], refs[9:13]
    table, own_ground, rows, rho, plane_sem, edge_sem, small_sem = refs[13:]
    planes, ny, nx = near_re.shape
    copies = []
    small = [
        pltpu.make_async_copy(y_table, table, small_sem.at[0]),
        pltpu.make_async_copy(ground, own_ground, small_sem.at[1]),
    ]
    for copy in small:
        copy.start()
    for z in range(planes):
        pair = [
            pltpu.make_async_copy(psi_re.at[0, z], near_re.at[z], plane_sem.at[0, z]),
            pltpu.make_async_copy(psi_im.at[0, z], near_im.at[z], plane_sem.at[1, z]),
        ]
        for copy in pair:
            copy.start()
        copies.append(pair)
    edges = []
    for which, (target, first, v_plane) in enumerate(((to_prev, 0, 0), (to_next, planes - 2, planes - 1))):
        edges += [
            pltpu.make_async_copy(psi_re.at[0, pl.ds(first, 2)], target.at[pl.ds(0, 2)], edge_sem.at[which, 0]),
            pltpu.make_async_copy(psi_im.at[0, pl.ds(first, 2)], target.at[pl.ds(2, 2)], edge_sem.at[which, 1]),
            pltpu.make_async_copy(v_local.at[pl.ds(v_plane, 1)], target.at[pl.ds(4, 1)], edge_sem.at[which, 2]),
        ]
    for copy in edges:
        copy.start()
    for copy in small:
        copy.wait()
    fill_rows(rows, table)
    ground_rows = own_ground.shape[1]
    place = lax.axis_index("y") * lax.axis_size("z") + lax.axis_index("z")
    own = pl.ds(pl.multiple_of(place * ground_rows, ground_rows), ground_rows)
    for z in range(planes):
        for copy in copies[z]:
            copy.wait()
        re, im = near_re[z], near_im[z]
        rho[...] = scale * (re * re + im * im)
        rho[own, :] = rho[own, :] - own_ground[z]
        image = dot(rows[...], rho[...])
        at = 0
        for piece in pieces:
            piece[:, z, :] = image[at : at + piece.shape[0]]
            at += piece.shape[0]
    for copy in edges:
        copy.wait()


def density(psi_re, psi_im, v_local, n_ground, y_table, total_orbs):
    planes, ny, nx = v_local.shape
    width = ny // lax.axis_size("z")
    heights = [width] * 4 + [width // 2] * 2 + [width] * 3
    outs = [shaped(h, planes, nx) for h in heights] + [shaped(planes, ny, nx)] * 2 + [shaped(5, ny, nx)] * 2
    far = [pltpu.with_memory_space_constraint(a, pltpu.HBM) for a in (psi_re, psi_im, v_local, n_ground, y_table)]
    result = pl.pallas_call(
        functools.partial(density_kernel, 2.0 / total_orbs),
        in_specs=[ANY] * 5,
        out_specs=[VMEM] * len(outs),
        out_shape=outs,
        scratch_shapes=[
            pltpu.VMEM((ny, ny), jnp.float32),
            pltpu.VMEM(n_ground.shape, jnp.float32),
            pltpu.VMEM((ny, ny), jnp.float32),
            pltpu.VMEM((ny, nx), jnp.float32),
            pltpu.SemaphoreType.DMA((2, planes)),
            pltpu.SemaphoreType.DMA((2, 3)),
            pltpu.SemaphoreType.DMA((2,)),
        ],
        compiler_params=pltpu.CompilerParams(vmem_limit_bytes=24 * MIB),
        name="density_y",
    )(*far)
    return result[:9], result[9], result[10], result[11], result[12]


def wave_sq(freq_index, length):
    signed = jnp.where(freq_index * 2 <= length, freq_index, freq_index - length)
    wave_number = signed.astype(jnp.float32) * (2.0 * math.pi / (length * SPACING))
    return wave_number * wave_number


def solve_kernel(y_len, field, x_table, z_table, out):
    nz, nx = z_table.shape[0], x_table.shape[0]
    half = out.shape[0] // SIDES
    width = y_len // lax.axis_size("z")
    ky = lax.axis_index("z") * width + lax.axis_index("y") * lax.axis_size("slab") + lax.axis_index("slab")
    z_index = lax.broadcasted_iota(jnp.int32, (nz, nx), 0)
    x_index = lax.broadcasted_iota(jnp.int32, (nz, nx), 1)
    y_index = jnp.full((nz, nx), ky, jnp.int32)
    total = wave_sq(z_index, nz) + wave_sq(y_index, y_len) + wave_sq(x_index, nx)
    anchor = (z_index == 0) & (y_index == 0) & (x_index == 0)
    safe = jnp.where(anchor, jnp.float32(1.0), total)
    greens = jnp.where(anchor, jnp.float32(0.0), (4.0 * math.pi) / safe) * (1.0 / (nz * y_len * nx))
    rho = field[0:nz] + field[nz : 2 * nz]
    spectrum = dot(z_table[...], dot(rho, x_table[...]))
    solved = dot(dot(z_table[...], spectrum * greens), x_table[...])
    solved = solved.reshape((half,) + out.shape[1:])
    out[0:half] = solved
    out[half:] = solved


def solve(field, x_table, z_table, y_len, planes):
    rows, nx = field.shape
    return pl.pallas_call(
        functools.partial(solve_kernel, y_len),
        in_specs=[VMEM] * 3,
        out_specs=VMEM,
        out_shape=shaped(rows // planes, planes, nx),
        compiler_params=pltpu.CompilerParams(vmem_limit_bytes=8 * MIB),
        name="solve_xz",
    )(field, x_table, z_table)


def strip_of(plane, start, rows):
    ref, lead = plane
    return ref[lead + (pl.ds(start, rows), slice(None))]


def kinetic(below, plane, above, start):
    ny = plane[0].shape[-2]
    mid = strip_of(plane, start, STRIP)
    before = strip_of(plane, pl.multiple_of(lax.rem(start + ny - 8, ny), 8), 8)
    after = strip_of(plane, pl.multiple_of(lax.rem(start + STRIP, ny), 8), 8)
    tall = jnp.concatenate([before, mid, after], axis=0)
    up = pltpu.roll(tall, 1, 0)[8 : 8 + STRIP]
    down = pltpu.roll(tall, tall.shape[0] - 1, 0)[8 : 8 + STRIP]
    left = pltpu.roll(mid, 1, 1)
    right = pltpu.roll(mid, mid.shape[1] - 1, 1)
    along = strip_of(below, start, STRIP) + strip_of(above, start, STRIP)
    return mid, KINETIC * ((up + down) + (left + right) + along - 6.0 * mid)


def each_strip(ny, body):
    @pl.loop(0, ny // STRIP)
    def _(index):
        body(pl.multiple_of(index * STRIP, STRIP))


def psi_plane(fields, low, high, planes, part, z):
    if z < 0:
        return (low, (2 * part + z + 2,))
    if z >= planes:
        return (high, (2 * part + z - planes,))
    return (fields[part], (z,))


def once_kernel(planes, wanted, with_edges, *refs):
    refs = list(refs)
    fields = [refs.pop(0), refs.pop(0)]
    low, high = (refs.pop(0), refs.pop(0)) if with_edges else (None, None)
    out = refs.pop(0)
    ny = out.shape[-2]
    at = functools.partial(psi_plane, fields, low, high, planes)
    for slot, z in enumerate(wanted):

        def body(start):
            for part in range(2):
                _, value = kinetic(at(part, z - 1), at(part, z), at(part, z + 1), start)
                out[part, slot, pl.ds(start, STRIP), :] = value

        each_strip(ny, body)


def once(near, edges, wanted, name):
    planes, ny, nx = near[0].shape
    return pl.pallas_call(
        functools.partial(once_kernel, planes, wanted, bool(edges)),
        in_specs=[VMEM] * (2 + len(edges)),
        out_specs=VMEM,
        out_shape=shaped(2, len(wanted), ny, nx),
        compiler_params=pltpu.CompilerParams(vmem_limit_bytes=16 * MIB),
        cost_estimate=cost(len(wanted), 100 * ny * nx),
        name=name,
    )(*near, *edges)


def once_plane(groups, refs, part, z):
    for ref, group in zip(refs, groups):
        if z in group:
            return (ref, (part, group.index(z)))


def base_kernel(groups, wanted, re, im, *refs):
    onces, out = refs[:-1], refs[-1]
    ny = out.shape[-2]
    at = functools.partial(once_plane, groups, onces)
    for slot, z in enumerate(wanted):

        def body(start):
            strip = pl.ds(start, STRIP)
            first_re, second_re = kinetic(at(0, z - 1), at(0, z), at(0, z + 1), start)
            first_im, second_im = kinetic(at(1, z - 1), at(1, z), at(1, z + 1), start)
            out[0, slot, strip, :] = re[z, strip, :] + TIME_STEP * first_im - HALF_SQ * second_re
            out[1, slot, strip, :] = im[z, strip, :] - TIME_STEP * first_re - HALF_SQ * second_im

        each_strip(ny, body)


def base(near, onces, groups, wanted, name):
    planes, ny, nx = near[0].shape
    return pl.pallas_call(
        functools.partial(base_kernel, groups, wanted),
        in_specs=[VMEM] * (2 + len(onces)),
        out_specs=VMEM,
        out_shape=shaped(2, len(wanted), ny, nx),
        compiler_params=pltpu.CompilerParams(vmem_limit_bytes=16 * MIB),
        cost_estimate=cost(len(wanted), 100 * ny * nx),
        name=name,
    )(*near, *onces)


def columns_kernel(table, out, rows):
    fill_rows(rows, table)
    out[...] = rows[...].T


def ring_columns(y_table):
    return pl.pallas_call(
        columns_kernel,
        in_specs=[VMEM],
        out_specs=VMEM,
        out_shape=shaped(*y_table.shape),
        scratch_shapes=[pltpu.VMEM(y_table.shape, jnp.float32)],
        name="ring_columns",
    )(y_table)


def potential_plane(v_local, columns, hats, z):
    hat = jnp.concatenate([h[:, z, :] for h in hats], axis=0)
    return v_local[z] + dot(columns[...], hat)


def outer_kernel(v_local, columns, *refs):
    hats, (first, last) = refs[:-2], refs[-2:]
    first[0] = potential_plane(v_local, columns, hats, 0)
    last[0] = potential_plane(v_local, columns, hats, v_local.shape[0] - 1)


def outer_potential(v_local, columns, hats):
    planes, ny, nx = v_local.shape
    return pl.pallas_call(
        outer_kernel,
        in_specs=[VMEM] * (2 + len(hats)),
        out_specs=[VMEM] * 2,
        out_shape=[shaped(1, ny, nx)] * 2,
        compiler_params=pltpu.CompilerParams(vmem_limit_bytes=16 * MIB),
        name="outer_potential",
    )(v_local, columns, *hats)


def update_strip(at_w, at_once, at_base, local, stage, slot, z, start):
    strip = pl.ds(start, STRIP)
    here = strip_of(local, start, STRIP)
    mid_re, kin_re = kinetic(at_w(0, z - 1), at_w(0, z), at_w(0, z + 1), start)
    mid_im, kin_im = kinetic(at_w(1, z - 1), at_w(1, z), at_w(1, z + 1), start)
    second_re = kin_re + here * (strip_of(at_once(0, z), start, STRIP) + mid_re)
    second_im = kin_im + here * (strip_of(at_once(1, z), start, STRIP) + mid_im)
    stage[0, slot, strip, :] = strip_of(at_base(0, z), start, STRIP) + TIME_STEP * mid_im - HALF_SQ * second_re
    stage[1, slot, strip, :] = strip_of(at_base(1, z), start, STRIP) - TIME_STEP * mid_re - HALF_SQ * second_im


def inner_kernel(once_groups, base_groups, hat_count, *refs):
    refs = list(refs)
    v_local, columns, v_first, v_last, re, im = [refs.pop(0) for _ in range(6)]
    hats = [refs.pop(0) for _ in range(hat_count)]
    onces = [refs.pop(0) for _ in once_groups]
    bases = [refs.pop(0) for _ in base_groups]
    out_re, out_im, v_kept, pot, work, stage, sem = refs
    planes, ny, _ = re.shape
    fields = (re, im)

    def at_w(part, z):
        return (work, (part, z))

    copies = []
    for z in range(planes):
        if z == 0:
            here = v_first[0]
        elif z == planes - 1:
            here = v_last[0]
        else:
            here = potential_plane(v_local, columns, hats, z)
            pot[z] = here
        for part in range(2):
            work[part, z] = here * fields[part][z]
        if z >= 2:
            done = z - 1
            each_strip(
                ny,
                lambda start: update_strip(
                    at_w,
                    functools.partial(once_plane, once_groups, onces),
                    functools.partial(once_plane, base_groups, bases),
                    (pot, (done,)),
                    stage,
                    done - 1,
                    done,
                    start,
                ),
            )
            for part, out in enumerate((out_re, out_im)):
                copy = pltpu.make_async_copy(stage.at[part, done - 1], out.at[0, done], sem.at[part, done - 1])
                copy.start()
                copies.append(copy)
    v_kept[0] = pot[1]
    v_kept[1] = pot[planes - 2]
    for copy in copies:
        copy.wait()


def inner_update(v_local, columns, v_first, v_last, near, hats, onces, once_groups, bases, base_groups):
    planes, ny, nx = v_local.shape
    operands = [v_local, columns, v_first, v_last, *near, *hats, *onces, *bases]
    full = shaped(1, planes, ny, nx)
    return pl.pallas_call(
        functools.partial(inner_kernel, once_groups, base_groups, len(hats)),
        in_specs=[VMEM] * len(operands),
        out_specs=[ANY, ANY, VMEM],
        out_shape=[full, full, shaped(2, ny, nx)],
        scratch_shapes=[
            plane_scratch(planes, ny=ny, nx=nx),
            plane_scratch(2, planes, ny=ny, nx=nx),
            plane_scratch(2, planes - 2, ny=ny, nx=nx),
            pltpu.SemaphoreType.DMA((2, planes - 2)),
        ],
        compiler_params=pltpu.CompilerParams(vmem_limit_bytes=44 * MIB),
        cost_estimate=cost(planes, 400 * ny * nx),
        name="inner_update",
    )(*operands)


def outer_kernel_update(once_groups, base_groups, *refs):
    refs = list(refs)
    v_first, v_last, v_before, v_after, v_kept, re, im, low, high = [refs.pop(0) for _ in range(9)]
    onces = [refs.pop(0) for _ in once_groups]
    bases = [refs.pop(0) for _ in base_groups]
    _, _, out_re, out_im, work, stage, sem = refs
    planes, ny, _ = re.shape
    at_psi = functools.partial(psi_plane, (re, im), low, high, planes)
    locals_of = {
        -1: (v_before, (0,)),
        0: (v_first, (0,)),
        1: (v_kept, (0,)),
        planes - 2: (v_kept, (1,)),
        planes - 1: (v_last, (0,)),
        planes: (v_after, (0,)),
    }
    order = list(locals_of)

    def at_w(part, z):
        return (work, (part, order.index(z)))

    copies = []
    for slot, z in enumerate((0, planes - 1)):
        for near in (z - 1, z, z + 1):
            ref, lead = locals_of[near]
            here = ref[lead]
            for part in range(2):
                source, where = at_psi(part, near)
                work[part, order.index(near)] = here * source[where]
        each_strip(
            ny,
            lambda start: update_strip(
                at_w,
                functools.partial(once_plane, once_groups, onces),
                functools.partial(once_plane, base_groups, bases),
                locals_of[z],
                stage,
                slot,
                z,
                start,
            ),
        )
        for part, out in enumerate((out_re, out_im)):
            copy = pltpu.make_async_copy(stage.at[part, slot], out.at[0, z], sem.at[part, slot])
            copy.start()
            copies.append(copy)
    for copy in copies:
        copy.wait()


def outer_update(new_re, new_im, v_planes, near, edges, onces, once_groups, bases, base_groups):
    planes, ny, nx = near[0].shape
    operands = [*v_planes, *near, *edges, *onces, *bases]
    return pl.pallas_call(
        functools.partial(outer_kernel_update, once_groups, base_groups),
        in_specs=[VMEM] * len(operands) + [ANY, ANY],
        out_specs=[ANY, ANY],
        out_shape=[shaped(*new_re.shape)] * 2,
        input_output_aliases={len(operands): 0, len(operands) + 1: 1},
        scratch_shapes=[
            plane_scratch(2, 6, ny=ny, nx=nx),
            plane_scratch(2, 2, ny=ny, nx=nx),
            pltpu.SemaphoreType.DMA((2, 2)),
        ],
        compiler_params=pltpu.CompilerParams(vmem_limit_bytes=32 * MIB),
        name="outer_update",
    )(*operands, new_re, new_im)


def ring(axis, shift):
    count = lax.axis_size(axis)
    return [(i, (i + shift) % count) for i in range(count)]


def forward(value, axis="z"):
    return lax.ppermute(value, axis, ring(axis, 1))


def backward(value, axis="z"):
    return lax.ppermute(value, axis, ring(axis, -1))


def slab_shift(value, shift):
    return lax.ppermute(value, "slab", ring("slab", shift))


def sum_over_ring(pieces):
    s0, s1, s2, s3, s4_first, s4_second, s5, s6, s7 = pieces
    half = s4_first.shape[0]
    got_up, got_down = forward(s4_first), backward(s4_second)
    up = jnp.concatenate([s3[:half] + got_up, s3[half:]], axis=0)
    down = jnp.concatenate([s5[:half], s5[half:] + got_down], axis=0)
    up, down = forward(up), backward(down)
    up, down = forward(up + s2), backward(down + s6)
    up, down = forward(up + s1), backward(down + s7)
    return up + down + s0


def gather_over_ring(block):
    half = block.shape[0] // 2
    up1, down1 = forward(block), backward(block)
    up2, down2 = forward(up1), backward(down1)
    up3, down3 = forward(up2), backward(down2)
    up4, down4 = forward(up3[:half]), backward(down3[half:])
    return [block, down1, down2, down3, up4, down4, up3, up2, up1]


def across(value):
    return lax.all_to_all(value, ("y", "slab"), split_axis=0, concat_axis=0, tiled=True)


def on_device(psi_re, psi_im, v_local, n_ground):
    total_orbs = psi_re.shape[0] * lax.axis_size("y") * lax.axis_size("z")
    planes, ny, nx = v_local.shape
    nz = planes * lax.axis_size("slab")
    y_table, x_table, z_table = cas_table(ny), cas_table(nx), cas_table(nz)

    pieces, near_re, near_im, to_prev, to_next = density(psi_re, psi_im, v_local, n_ground, y_table, total_orbs)
    near = (near_re, near_im)
    low, high = slab_shift(to_next, 1), slab_shift(to_prev, -1)
    edges = (low, high)

    middle = planes // 2
    once_groups = [list(range(1, middle)), list(range(middle, planes - 1)), [-1, 0, planes - 1, planes]]
    base_groups = [list(range(middle)), list(range(middle, planes))]
    onces = [
        once(near, (), once_groups[0], "once_a"),
        once(near, (), once_groups[1], "once_b"),
        once(near, edges, once_groups[2], "once_c"),
    ]
    bases = [base(near, onces, once_groups, group, name) for group, name in zip(base_groups, ("base_a", "base_b"))]
    columns = ring_columns(y_table)

    share = sum_over_ring(pieces)
    pencils = across(share).reshape(SIDES * nz, nx)
    hats = gather_over_ring(across(solve(pencils, x_table, z_table, ny, planes)))

    v_first, v_last = outer_potential(v_local, columns, hats)
    v_before, v_after = slab_shift(v_last, 1), slab_shift(v_first, -1)
    new_re, new_im, v_kept = inner_update(
        v_local, columns, v_first, v_last, near, hats, onces, once_groups, bases, base_groups
    )
    v_planes = (v_first, v_last, v_before, v_after, v_kept)
    return tuple(outer_update(new_re, new_im, v_planes, near, edges, onces, once_groups, bases, base_groups))


def solution(mesh):
    orbs, slabs = mesh.devices.shape
    mesh = Mesh(mesh.devices.reshape(SIDES, orbs // SIDES, slabs), ("y", "z", "slab"))
    orb = ("y", "z")
    placed = (
        P(orb, "slab", None, None),
        P(orb, "slab", None, None),
        P("slab", None, None),
        P("slab", orb, None),
    )
    return jax.shard_map(
        on_device,
        mesh=mesh,
        in_specs=placed,
        out_specs=(P(orb, "slab", None, None), P(orb, "slab", None, None)),
        check_vma=False,
    )
```

```python
import functools
import math

import jax
import jax.numpy as jnp
import numpy as np
from jax import lax
from jax.experimental import pallas as pl
from jax.experimental.pallas import tpu as pltpu
from jax.sharding import Mesh
from jax.sharding import PartitionSpec as P

SPACING = 0.5
TIME_STEP = 0.02
HALF_SQ = 0.5 * TIME_STEP * TIME_STEP
KINETIC = -0.5 / (SPACING * SPACING)
HIGHEST = lax.Precision.HIGHEST
SIDES = 2
MIB = 1 << 20
VMEM = pl.BlockSpec(memory_space=pltpu.VMEM)
ANY = pl.BlockSpec(memory_space=pl.ANY)


def cas_table(length):
    index = np.arange(length)
    angles = (index[:, None] * index[None, :] % length) * (2.0 * math.pi / length)
    return jnp.asarray((np.cos(angles) + np.sin(angles)).astype(np.float32))


def dot(left, right):
    return jnp.dot(left, right, precision=HIGHEST, preferred_element_type=jnp.float32)


def shaped(*shape):
    return jax.ShapeDtypeStruct(shape, jnp.float32)


def plane_scratch(*lead, ny, nx):
    return pltpu.VMEM(lead + (ny, nx), jnp.float32)


def cost(planes, weight):
    return pl.CostEstimate(flops=planes * weight, bytes_accessed=planes * MIB // 2, transcendentals=0)


def fill_rows(rows, table):
    ring = lax.axis_size("z")
    width = rows.shape[0] // ring
    z = lax.axis_index("z")
    for offset in range(ring):
        start = pl.multiple_of(lax.rem(z + offset, ring) * width, width)
        rows[offset * width : (offset + 1) * width, :] = table[pl.ds(start, width), :]


def density_kernel(scale, psi_re, psi_im, v_local, ground, y_table, *refs):
    pieces, (near_re, near_im, to_prev, to_next) = refs[:9], refs[9:13]
    table, own_ground, rows, rho, plane_sem, edge_sem, small_sem = refs[13:]
    planes, ny, nx = near_re.shape
    copies = []
    small = [
        pltpu.make_async_copy(y_table, table, small_sem.at[0]),
        pltpu.make_async_copy(ground, own_ground, small_sem.at[1]),
    ]
    for copy in small:
        copy.start()
    for z in range(planes):
        pair = [
            pltpu.make_async_copy(psi_re.at[0, z], near_re.at[z], plane_sem.at[0, z]),
            pltpu.make_async_copy(psi_im.at[0, z], near_im.at[z], plane_sem.at[1, z]),
        ]
        for copy in pair:
            copy.start()
        copies.append(pair)
    edges = []
    for which, (target, first, v_plane) in enumerate(((to_prev, 0, 0), (to_next, planes - 2, planes - 1))):
        edges += [
            pltpu.make_async_copy(psi_re.at[0, pl.ds(first, 2)], target.at[pl.ds(0, 2)], edge_sem.at[which, 0]),
            pltpu.make_async_copy(psi_im.at[0, pl.ds(first, 2)], target.at[pl.ds(2, 2)], edge_sem.at[which, 1]),
            pltpu.make_async_copy(v_local.at[pl.ds(v_plane, 1)], target.at[pl.ds(4, 1)], edge_sem.at[which, 2]),
        ]
    for copy in edges:
        copy.start()
    for copy in small:
        copy.wait()
    fill_rows(rows, table)
    ground_rows = own_ground.shape[1]
    place = lax.axis_index("y") * lax.axis_size("z") + lax.axis_index("z")
    own = pl.ds(pl.multiple_of(place * ground_rows, ground_rows), ground_rows)
    for z in range(planes):
        for copy in copies[z]:
            copy.wait()
        re, im = near_re[z], near_im[z]
        rho[...] = scale * (re * re + im * im)
        rho[own, :] = rho[own, :] - own_ground[z]
        image = dot(rows[...], rho[...])
        at = 0
        for piece in pieces:
            piece[:, z, :] = image[at : at + piece.shape[0]]
            at += piece.shape[0]
    for copy in edges:
        copy.wait()


def density(psi_re, psi_im, v_local, n_ground, y_table, total_orbs):
    planes, ny, nx = v_local.shape
    width = ny // lax.axis_size("z")
    heights = [width] * 4 + [width // 2] * 2 + [width] * 3
    outs = [shaped(h, planes, nx) for h in heights] + [shaped(planes, ny, nx)] * 2 + [shaped(5, ny, nx)] * 2
    far = [pltpu.with_memory_space_constraint(a, pltpu.HBM) for a in (psi_re, psi_im, v_local, n_ground, y_table)]
    result = pl.pallas_call(
        functools.partial(density_kernel, 2.0 / total_orbs),
        in_specs=[ANY] * 5,
        out_specs=[VMEM] * len(outs),
        out_shape=outs,
        scratch_shapes=[
            pltpu.VMEM((ny, ny), jnp.float32),
            pltpu.VMEM(n_ground.shape, jnp.float32),
            pltpu.VMEM((ny, ny), jnp.float32),
            pltpu.VMEM((ny, nx), jnp.float32),
            pltpu.SemaphoreType.DMA((2, planes)),
            pltpu.SemaphoreType.DMA((2, 3)),
            pltpu.SemaphoreType.DMA((2,)),
        ],
        compiler_params=pltpu.CompilerParams(vmem_limit_bytes=6 * MIB),
        name="density_y",
    )(*far)
    return result[:9], result[9], result[10], result[11], result[12]


def wave_sq(freq_index, length):
    signed = jnp.where(freq_index * 2 <= length, freq_index, freq_index - length)
    wave_number = signed.astype(jnp.float32) * (2.0 * math.pi / (length * SPACING))
    return wave_number * wave_number


def solve_kernel(y_len, field, x_table, z_table, out):
    nz, nx = z_table.shape[0], x_table.shape[0]
    half = out.shape[0] // SIDES
    width = y_len // lax.axis_size("z")
    ky = lax.axis_index("z") * width + lax.axis_index("y") * lax.axis_size("slab") + lax.axis_index("slab")
    z_index = lax.broadcasted_iota(jnp.int32, (nz, nx), 0)
    x_index = lax.broadcasted_iota(jnp.int32, (nz, nx), 1)
    y_index = jnp.full((nz, nx), ky, jnp.int32)
    total = wave_sq(z_index, nz) + wave_sq(y_index, y_len) + wave_sq(x_index, nx)
    anchor = (z_index == 0) & (y_index == 0) & (x_index == 0)
    safe = jnp.where(anchor, jnp.float32(1.0), total)
    greens = jnp.where(anchor, jnp.float32(0.0), (4.0 * math.pi) / safe) * (1.0 / (nz * y_len * nx))
    rho = field[0:nz] + field[nz : 2 * nz]
    spectrum = dot(z_table[...], dot(rho, x_table[...]))
    solved = dot(dot(z_table[...], spectrum * greens), x_table[...])
    solved = solved.reshape((half,) + out.shape[1:])
    out[0:half] = solved
    out[half:] = solved


def solve(field, x_table, z_table, y_len, planes):
    rows, nx = field.shape
    return pl.pallas_call(
        functools.partial(solve_kernel, y_len),
        in_specs=[VMEM] * 3,
        out_specs=VMEM,
        out_shape=shaped(rows // planes, planes, nx),
        compiler_params=pltpu.CompilerParams(vmem_limit_bytes=8 * MIB),
        name="solve_xz",
    )(field, x_table, z_table)


def whole(plane):
    ref, lead = plane
    return ref[lead]


def neighbour_matrix(length):
    matrix = np.zeros((length, length), np.float32)
    index = np.arange(length)
    matrix[index, (index + 1) % length] = KINETIC
    matrix[index, (index - 1) % length] = KINETIC
    return jnp.asarray(matrix, jnp.bfloat16)


def kinetic(below, plane, above, sides):
    mid = whole(plane)
    high = mid.astype(jnp.bfloat16)
    rest = (mid - high.astype(jnp.float32)).astype(jnp.bfloat16)
    matrix = sides[...]
    along_x = jnp.dot(high, matrix, preferred_element_type=jnp.float32)
    along_x = along_x + jnp.dot(rest, matrix, preferred_element_type=jnp.float32)
    along_y = pltpu.roll(mid, 1, 0) + pltpu.roll(mid, mid.shape[0] - 1, 0)
    along_z = whole(below) + whole(above)
    return mid, along_x + (KINETIC * (along_y + along_z) - (6.0 * KINETIC) * mid)


def psi_plane(fields, low, high, planes, part, z):
    if z < 0:
        return (low, (2 * part + z + 2,))
    if z >= planes:
        return (high, (2 * part + z - planes,))
    return (fields[part], (z,))


def once_kernel(planes, wanted, with_edges, sides, *refs):
    refs = list(refs)
    fields = [refs.pop(0), refs.pop(0)]
    low, high = (refs.pop(0), refs.pop(0)) if with_edges else (None, None)
    out = refs.pop(0)
    at = functools.partial(psi_plane, fields, low, high, planes)
    for slot, z in enumerate(wanted):
        for part in range(2):
            _, value = kinetic(at(part, z - 1), at(part, z), at(part, z + 1), sides)
            out[part, slot] = value


def once(sides, near, edges, wanted, name):
    planes, ny, nx = near[0].shape
    return pl.pallas_call(
        functools.partial(once_kernel, planes, wanted, bool(edges)),
        in_specs=[VMEM] * (3 + len(edges)),
        out_specs=VMEM,
        out_shape=shaped(2, len(wanted), ny, nx),
        compiler_params=pltpu.CompilerParams(vmem_limit_bytes=6 * MIB),
        cost_estimate=cost(len(wanted), 100 * ny * nx),
        name=name,
    )(sides, *near, *edges)


def once_plane(groups, refs, part, z):
    for ref, group in zip(refs, groups):
        if z in group:
            return (ref, (part, group.index(z)))


def base_kernel(groups, wanted, sides, re, im, *refs):
    onces, out = refs[:-1], refs[-1]
    at = functools.partial(once_plane, groups, onces)
    for slot, z in enumerate(wanted):
        first_re, second_re = kinetic(at(0, z - 1), at(0, z), at(0, z + 1), sides)
        first_im, second_im = kinetic(at(1, z - 1), at(1, z), at(1, z + 1), sides)
        out[0, slot] = re[z] + TIME_STEP * first_im - HALF_SQ * second_re
        out[1, slot] = im[z] - TIME_STEP * first_re - HALF_SQ * second_im


def base(sides, near, onces, groups, wanted, name):
    planes, ny, nx = near[0].shape
    return pl.pallas_call(
        functools.partial(base_kernel, groups, wanted),
        in_specs=[VMEM] * (3 + len(onces)),
        out_specs=VMEM,
        out_shape=shaped(2, len(wanted), ny, nx),
        compiler_params=pltpu.CompilerParams(vmem_limit_bytes=6 * MIB),
        cost_estimate=cost(len(wanted), 100 * ny * nx),
        name=name,
    )(sides, *near, *onces)


def columns_kernel(table, out, rows):
    fill_rows(rows, table)
    out[...] = rows[...].T


def ring_columns(y_table):
    return pl.pallas_call(
        columns_kernel,
        in_specs=[VMEM],
        out_specs=VMEM,
        out_shape=shaped(*y_table.shape),
        scratch_shapes=[pltpu.VMEM(y_table.shape, jnp.float32)],
        name="ring_columns",
    )(y_table)


def potential_plane(v_local, columns, hats, z):
    hat = jnp.concatenate([h[:, z, :] for h in hats], axis=0)
    return v_local[z] + dot(columns[...], hat)


def outer_kernel(v_local, columns, *refs):
    hats, (first, last) = refs[:-2], refs[-2:]
    first[0] = potential_plane(v_local, columns, hats, 0)
    last[0] = potential_plane(v_local, columns, hats, v_local.shape[0] - 1)


def outer_potential(v_local, columns, hats):
    planes, ny, nx = v_local.shape
    return pl.pallas_call(
        outer_kernel,
        in_specs=[VMEM] * (2 + len(hats)),
        out_specs=[VMEM] * 2,
        out_shape=[shaped(1, ny, nx)] * 2,
        compiler_params=pltpu.CompilerParams(vmem_limit_bytes=6 * MIB),
        name="outer_potential",
    )(v_local, columns, *hats)


def update_plane(at_w, at_once, at_base, local, sides, stage, slot, z):
    here = whole(local)
    mid_re, kin_re = kinetic(at_w(0, z - 1), at_w(0, z), at_w(0, z + 1), sides)
    mid_im, kin_im = kinetic(at_w(1, z - 1), at_w(1, z), at_w(1, z + 1), sides)
    second_re = kin_re + here * (whole(at_once(0, z)) + mid_re)
    second_im = kin_im + here * (whole(at_once(1, z)) + mid_im)
    stage[0, slot] = whole(at_base(0, z)) + TIME_STEP * mid_im - HALF_SQ * second_re
    stage[1, slot] = whole(at_base(1, z)) - TIME_STEP * mid_re - HALF_SQ * second_im


def inner_kernel(once_groups, base_groups, hat_count, *refs):
    refs = list(refs)
    sides, v_local, columns, v_first, v_last, re, im = [refs.pop(0) for _ in range(7)]
    hats = [refs.pop(0) for _ in range(hat_count)]
    onces = [refs.pop(0) for _ in once_groups]
    bases = [refs.pop(0) for _ in base_groups]
    out_re, out_im, v_kept, pot, work, stage, sem = refs
    planes, ny, _ = re.shape
    fields = (re, im)

    def at_w(part, z):
        return (work, (part, z))

    copies = []
    for z in range(planes):
        if z == 0:
            here = v_first[0]
        elif z == planes - 1:
            here = v_last[0]
        else:
            here = potential_plane(v_local, columns, hats, z)
            pot[z] = here
        for part in range(2):
            work[part, z] = here * fields[part][z]
        if z >= 2:
            done = z - 1
            update_plane(
                at_w,
                functools.partial(once_plane, once_groups, onces),
                functools.partial(once_plane, base_groups, bases),
                (pot, (done,)),
                sides,
                stage,
                done - 1,
                done,
            )
            for part, out in enumerate((out_re, out_im)):
                copy = pltpu.make_async_copy(stage.at[part, done - 1], out.at[0, done], sem.at[part, done - 1])
                copy.start()
                copies.append(copy)
    v_kept[0] = pot[1]
    v_kept[1] = pot[planes - 2]
    for copy in copies:
        copy.wait()


def inner_update(sides, v_local, columns, v_first, v_last, near, hats, onces, once_groups, bases, base_groups):
    planes, ny, nx = v_local.shape
    operands = [sides, v_local, columns, v_first, v_last, *near, *hats, *onces, *bases]
    full = shaped(1, planes, ny, nx)
    return pl.pallas_call(
        functools.partial(inner_kernel, once_groups, base_groups, len(hats)),
        in_specs=[VMEM] * len(operands),
        out_specs=[ANY, ANY, VMEM],
        out_shape=[full, full, shaped(2, ny, nx)],
        scratch_shapes=[
            plane_scratch(planes, ny=ny, nx=nx),
            plane_scratch(2, planes, ny=ny, nx=nx),
            plane_scratch(2, planes - 2, ny=ny, nx=nx),
            pltpu.SemaphoreType.DMA((2, planes - 2)),
        ],
        compiler_params=pltpu.CompilerParams(vmem_limit_bytes=14 * MIB),
        cost_estimate=cost(planes, 400 * ny * nx),
        name="inner_update",
    )(*operands)


def outer_kernel_update(once_groups, base_groups, *refs):
    refs = list(refs)
    sides, v_first, v_last, v_before, v_after, v_kept, re, im, low, high = [refs.pop(0) for _ in range(10)]
    onces = [refs.pop(0) for _ in once_groups]
    bases = [refs.pop(0) for _ in base_groups]
    _, _, out_re, out_im, work, stage, sem = refs
    planes = re.shape[0]
    at_psi = functools.partial(psi_plane, (re, im), low, high, planes)
    locals_of = {
        -1: (v_before, (0,)),
        0: (v_first, (0,)),
        1: (v_kept, (0,)),
        planes - 2: (v_kept, (1,)),
        planes - 1: (v_last, (0,)),
        planes: (v_after, (0,)),
    }
    order = list(locals_of)

    def at_w(part, z):
        return (work, (part, order.index(z)))

    copies = []
    for slot, z in enumerate((0, planes - 1)):
        for near in (z - 1, z, z + 1):
            ref, lead = locals_of[near]
            here = ref[lead]
            for part in range(2):
                source, where = at_psi(part, near)
                work[part, order.index(near)] = here * source[where]
        update_plane(
            at_w,
            functools.partial(once_plane, once_groups, onces),
            functools.partial(once_plane, base_groups, bases),
            locals_of[z],
            sides,
            stage,
            slot,
            z,
        )
        for part, out in enumerate((out_re, out_im)):
            copy = pltpu.make_async_copy(stage.at[part, slot], out.at[0, z], sem.at[part, slot])
            copy.start()
            copies.append(copy)
    for copy in copies:
        copy.wait()


def outer_update(sides, new_re, new_im, v_planes, near, edges, onces, once_groups, bases, base_groups):
    planes, ny, nx = near[0].shape
    operands = [sides, *v_planes, *near, *edges, *onces, *bases]
    return pl.pallas_call(
        functools.partial(outer_kernel_update, once_groups, base_groups),
        in_specs=[VMEM] * len(operands) + [ANY, ANY],
        out_specs=[ANY, ANY],
        out_shape=[shaped(*new_re.shape)] * 2,
        input_output_aliases={len(operands): 0, len(operands) + 1: 1},
        scratch_shapes=[
            plane_scratch(2, 6, ny=ny, nx=nx),
            plane_scratch(2, 2, ny=ny, nx=nx),
            pltpu.SemaphoreType.DMA((2, 2)),
        ],
        compiler_params=pltpu.CompilerParams(vmem_limit_bytes=8 * MIB),
        name="outer_update",
    )(*operands, new_re, new_im)


def ring(axis, shift):
    count = lax.axis_size(axis)
    return [(i, (i + shift) % count) for i in range(count)]


def forward(value, axis="z"):
    return lax.ppermute(value, axis, ring(axis, 1))


def backward(value, axis="z"):
    return lax.ppermute(value, axis, ring(axis, -1))


def slab_shift(value, shift):
    return lax.ppermute(value, "slab", ring("slab", shift))


def after(value, *others):
    return lax.optimization_barrier((value,) + others)[0]


def sum_over_ring(pieces, beside):
    s0, s1, s2, s3, s4_first, s4_second, s5, s6, s7 = pieces
    half = s4_first.shape[0]
    got_up, got_down = forward(s4_first), backward(s4_second)
    got_up = after(got_up, *beside[0])
    up = jnp.concatenate([s3[:half] + got_up, s3[half:]], axis=0)
    down = jnp.concatenate([s5[:half], s5[half:] + got_down], axis=0)
    up, down = forward(up), backward(down)
    up = after(up, *beside[1])
    up, down = forward(up + s2), backward(down + s6)
    up = after(up, *beside[2])
    up, down = forward(up + s1), backward(down + s7)
    up = after(up, *beside[3])
    return up + down + s0


def gather_over_ring(block):
    half = block.shape[0] // 2
    up1, down1 = forward(block), backward(block)
    up2, down2 = forward(up1), backward(down1)
    up3, down3 = forward(up2), backward(down2)
    up4, down4 = forward(up3[:half]), backward(down3[half:])
    return [block, down1, down2, down3, up4, down4, up3, up2, up1]


def across(value):
    return lax.all_to_all(value, ("y", "slab"), split_axis=0, concat_axis=0, tiled=True)


def on_device(psi_re, psi_im, v_local, n_ground):
    total_orbs = psi_re.shape[0] * lax.axis_size("y") * lax.axis_size("z")
    planes, ny, nx = v_local.shape
    nz = planes * lax.axis_size("slab")
    y_table, x_table, z_table = cas_table(ny), cas_table(nx), cas_table(nz)

    pieces, near_re, near_im, to_prev, to_next = density(psi_re, psi_im, v_local, n_ground, y_table, total_orbs)
    near = (near_re, near_im)
    low, high = slab_shift(to_next, 1), slab_shift(to_prev, -1)
    edges = (low, high)

    middle = planes // 2
    once_groups = [list(range(1, middle)), list(range(middle, planes - 1)), [-1, 0, planes - 1, planes]]
    base_groups = [list(range(middle)), list(range(middle, planes))]
    sides = neighbour_matrix(nx)
    onces = [
        once(sides, near, (), once_groups[0], "once_a"),
        once(sides, near, (), once_groups[1], "once_b"),
        once(sides, near, edges, once_groups[2], "once_c"),
    ]
    bases = [
        base(sides, near, onces, once_groups, group, name) for group, name in zip(base_groups, ("base_a", "base_b"))
    ]
    columns = ring_columns(y_table)

    beside = ((onces[0], columns), (onces[1],), (onces[2],), tuple(bases))
    share = sum_over_ring(pieces, beside)
    pencils = across(share).reshape(SIDES * nz, nx)
    hats = gather_over_ring(across(solve(pencils, x_table, z_table, ny, planes)))

    v_first, v_last = outer_potential(v_local, columns, hats)
    v_before, v_after = slab_shift(v_last, 1), slab_shift(v_first, -1)
    new_re, new_im, v_kept = inner_update(
        sides, v_local, columns, v_first, v_last, near, hats, onces, once_groups, bases, base_groups
    )
    v_planes = (v_first, v_last, v_before, v_after, v_kept)
    return tuple(outer_update(sides, new_re, new_im, v_planes, near, edges, onces, once_groups, bases, base_groups))


def solution(mesh):
    orbs, slabs = mesh.devices.shape
    mesh = Mesh(mesh.devices.reshape(SIDES, orbs // SIDES, slabs), ("y", "z", "slab"))
    orb = ("y", "z")
    placed = (
        P(orb, "slab", None, None),
        P(orb, "slab", None, None),
        P("slab", None, None),
        P("slab", orb, None),
    )
    return jax.shard_map(
        on_device,
        mesh=mesh,
        in_specs=placed,
        out_specs=(P(orb, "slab", None, None), P(orb, "slab", None, None)),
        check_vma=False,
    )
```

```python
import functools
import math

import jax
import jax.numpy as jnp
import numpy as np
from jax import lax
from jax.experimental import pallas as pl
from jax.experimental.pallas import tpu as pltpu
from jax.sharding import Mesh
from jax.sharding import PartitionSpec as P

SPACING = 0.5
TIME_STEP = 0.02
HALF_SQ = 0.5 * TIME_STEP * TIME_STEP
KINETIC = -0.5 / (SPACING * SPACING)
HIGHEST = lax.Precision.HIGHEST
SIDES = 2
MIB = 1 << 20
VMEM = pl.BlockSpec(memory_space=pltpu.VMEM)
ANY = pl.BlockSpec(memory_space=pl.ANY)


def cas_table(length):
    index = np.arange(length)
    angles = (index[:, None] * index[None, :] % length) * (2.0 * math.pi / length)
    return jnp.asarray((np.cos(angles) + np.sin(angles)).astype(np.float32))


def dot(left, right):
    return jnp.dot(left, right, precision=HIGHEST, preferred_element_type=jnp.float32)


def shaped(*shape):
    return jax.ShapeDtypeStruct(shape, jnp.float32)


def plane_scratch(*lead, ny, nx):
    return pltpu.VMEM(lead + (ny, nx), jnp.float32)


def cost(planes, weight):
    return pl.CostEstimate(flops=planes * weight, bytes_accessed=planes * MIB // 2, transcendentals=0)


def fill_rows(rows, table):
    ring = lax.axis_size("z")
    width = rows.shape[0] // ring
    z = lax.axis_index("z")
    for offset in range(ring):
        start = pl.multiple_of(lax.rem(z + offset, ring) * width, width)
        rows[offset * width : (offset + 1) * width, :] = table[pl.ds(start, width), :]


def density_kernel(scale, psi_re, psi_im, v_local, ground, y_table, *refs):
    pieces, (to_prev, to_next) = refs[:9], refs[9:11]
    near, table, own_ground, rows, rho, plane_sem, edge_sem, small_sem = refs[11:]
    planes = near.shape[1]
    half = planes // 2
    small = [
        pltpu.make_async_copy(y_table, table, small_sem.at[0]),
        pltpu.make_async_copy(ground, own_ground, small_sem.at[1]),
    ]
    copies = []
    for group in range(2):
        some = pl.ds(group * half, half)
        copies.append(
            [
                pltpu.make_async_copy(psi.at[0, some], near.at[part, some], plane_sem.at[part, group])
                for part, psi in enumerate((psi_re, psi_im))
            ]
        )
    edges = []
    for which, (target, first, v_plane) in enumerate(((to_prev, 0, 0), (to_next, planes - 2, planes - 1))):
        pair = pl.ds(first, 2)
        edges += [
            pltpu.make_async_copy(psi_re.at[0, pair], target.at[pl.ds(0, 2)], edge_sem.at[which, 0]),
            pltpu.make_async_copy(psi_im.at[0, pair], target.at[pl.ds(2, 2)], edge_sem.at[which, 1]),
            pltpu.make_async_copy(v_local.at[pl.ds(v_plane, 1)], target.at[pl.ds(4, 1)], edge_sem.at[which, 2]),
        ]
    for copy in copies[0] + small + copies[1] + edges:
        copy.start()
    ground_rows = own_ground.shape[1]
    place = lax.axis_index("y") * lax.axis_size("z") + lax.axis_index("z")
    own = pl.ds(pl.multiple_of(place * ground_rows, ground_rows), ground_rows)
    for group in range(2):
        for copy in copies[group] + (small if group == 0 else []):
            copy.wait()
        if group == 0:
            fill_rows(rows, table)
        for z in range(group * half, (group + 1) * half):
            re, im = near[0, z], near[1, z]
            rho[z] = scale * (re * re + im * im)
            rho[z, own, :] = rho[z, own, :] - own_ground[z]
        for z in range(group * half, (group + 1) * half):
            image = dot(rows[...], rho[z])
            at = 0
            for piece in pieces:
                piece[z] = image[at : at + piece.shape[1]]
                at += piece.shape[1]
    for copy in edges:
        copy.wait()


def density(psi_re, psi_im, v_local, n_ground, y_table, total_orbs):
    planes, ny, nx = v_local.shape
    width = ny // lax.axis_size("z")
    heights = [width] * 4 + [width // 2] * 2 + [width] * 3
    shapes = [(planes, h, nx) for h in heights] + [(5, ny, nx)] * 2
    far = [pltpu.with_memory_space_constraint(a, pltpu.HBM) for a in (psi_re, psi_im, v_local, n_ground, y_table)]
    result = pl.pallas_call(
        functools.partial(density_kernel, 2.0 / total_orbs),
        in_specs=[ANY] * 5,
        out_specs=[VMEM] * len(shapes),
        out_shape=[pltpu.VMEM(shape, jnp.float32) for shape in shapes],
        scratch_shapes=[
            plane_scratch(2, planes, ny=ny, nx=nx),
            pltpu.VMEM((ny, ny), jnp.float32),
            pltpu.VMEM(n_ground.shape, jnp.float32),
            pltpu.VMEM((ny, ny), jnp.float32),
            plane_scratch(planes, ny=ny, nx=nx),
            pltpu.SemaphoreType.DMA((2, 2)),
            pltpu.SemaphoreType.DMA((2, 3)),
            pltpu.SemaphoreType.DMA((2,)),
        ],
        compiler_params=pltpu.CompilerParams(vmem_limit_bytes=10 * MIB),
        name="density_y",
    )(*far)
    return result[:9], result[9], result[10]


def share_kernel(own, up, down, out):
    for z in range(own.shape[0]):
        out[:, z, :] = own[z] + up[z] + down[z]


def add_shares(own, up, down):
    planes, rows, nx = own.shape
    return pl.pallas_call(
        share_kernel,
        in_specs=[VMEM] * 3,
        out_specs=VMEM,
        out_shape=shaped(rows, planes, nx),
        compiler_params=pltpu.CompilerParams(vmem_limit_bytes=4 * MIB),
        name="add_shares",
    )(own, up, down)


def wave_sq(freq_index, length):
    signed = jnp.where(freq_index * 2 <= length, freq_index, freq_index - length)
    wave_number = signed.astype(jnp.float32) * (2.0 * math.pi / (length * SPACING))
    return wave_number * wave_number


def solve_kernel(y_len, field, x_table, z_table, out):
    nz, nx = z_table.shape[0], x_table.shape[0]
    half = out.shape[0] // SIDES
    width = y_len // lax.axis_size("z")
    ky = lax.axis_index("z") * width + lax.axis_index("y") * lax.axis_size("slab") + lax.axis_index("slab")
    z_index = lax.broadcasted_iota(jnp.int32, (nz, nx), 0)
    x_index = lax.broadcasted_iota(jnp.int32, (nz, nx), 1)
    y_index = jnp.full((nz, nx), ky, jnp.int32)
    total = wave_sq(z_index, nz) + wave_sq(y_index, y_len) + wave_sq(x_index, nx)
    anchor = (z_index == 0) & (y_index == 0) & (x_index == 0)
    safe = jnp.where(anchor, jnp.float32(1.0), total)
    greens = jnp.where(anchor, jnp.float32(0.0), (4.0 * math.pi) / safe) * (1.0 / (nz * y_len * nx))
    rho = field[0:nz] + field[nz : 2 * nz]
    spectrum = dot(z_table[...], dot(rho, x_table[...]))
    solved = dot(dot(z_table[...], spectrum * greens), x_table[...])
    solved = solved.reshape((half,) + out.shape[1:])
    out[0:half] = solved
    out[half:] = solved


def solve(field, x_table, z_table, y_len, planes):
    rows, nx = field.shape
    return pl.pallas_call(
        functools.partial(solve_kernel, y_len),
        in_specs=[VMEM] * 3,
        out_specs=VMEM,
        out_shape=shaped(rows // planes, planes, nx),
        compiler_params=pltpu.CompilerParams(vmem_limit_bytes=8 * MIB),
        name="solve_xz",
    )(field, x_table, z_table)


def whole(plane):
    ref, lead = plane
    return ref[lead]


def neighbour_matrix(length):
    matrix = np.zeros((length, length), np.float32)
    index = np.arange(length)
    matrix[index, (index + 1) % length] = KINETIC
    matrix[index, (index - 1) % length] = KINETIC
    return jnp.asarray(matrix, jnp.bfloat16)


def kinetic(below, plane, above, sides):
    mid = whole(plane)
    high = mid.astype(jnp.bfloat16)
    rest = (mid - high.astype(jnp.float32)).astype(jnp.bfloat16)
    matrix = sides[...]
    along_x = jnp.dot(high, matrix, preferred_element_type=jnp.float32)
    along_x = along_x + jnp.dot(rest, matrix, preferred_element_type=jnp.float32)
    along_y = pltpu.roll(mid, 1, 0) + pltpu.roll(mid, mid.shape[0] - 1, 0)
    along_z = whole(below) + whole(above)
    return mid, along_x + (KINETIC * (along_y + along_z) - (6.0 * KINETIC) * mid)


def psi_plane(fields, low, high, planes, part, z):
    if z < 0:
        return (low, (2 * part + z + 2,))
    if z >= planes:
        return (high, (2 * part + z - planes,))
    return (fields[part], (z,))


def once_kernel(planes, wanted, with_edges, sides, *refs):
    refs = list(refs)
    fields = [refs.pop(0), refs.pop(0)]
    low, high = (refs.pop(0), refs.pop(0)) if with_edges else (None, None)
    out = refs.pop(0)
    at = functools.partial(psi_plane, fields, low, high, planes)
    for slot, z in enumerate(wanted):
        for part in range(2):
            _, value = kinetic(at(part, z - 1), at(part, z), at(part, z + 1), sides)
            out[part, slot] = value


def once(sides, near, edges, wanted, name):
    planes, ny, nx = near[0].shape
    return pl.pallas_call(
        functools.partial(once_kernel, planes, wanted, bool(edges)),
        in_specs=[VMEM] * (3 + len(edges)),
        out_specs=VMEM,
        out_shape=shaped(2, len(wanted), ny, nx),
        compiler_params=pltpu.CompilerParams(vmem_limit_bytes=6 * MIB),
        cost_estimate=cost(len(wanted), 100 * ny * nx),
        name=name,
    )(sides, *near, *edges)


def once_plane(groups, refs, part, z):
    for ref, group in zip(refs, groups):
        if z in group:
            return (ref, (part, group.index(z)))


def base_kernel(groups, wanted, sides, re, im, *refs):
    onces, out = refs[:-1], refs[-1]
    at = functools.partial(once_plane, groups, onces)
    for slot, z in enumerate(wanted):
        first_re, second_re = kinetic(at(0, z - 1), at(0, z), at(0, z + 1), sides)
        first_im, second_im = kinetic(at(1, z - 1), at(1, z), at(1, z + 1), sides)
        out[0, slot] = re[z] + TIME_STEP * first_im - HALF_SQ * second_re
        out[1, slot] = im[z] - TIME_STEP * first_re - HALF_SQ * second_im


def base(sides, near, onces, groups, wanted, name):
    planes, ny, nx = near[0].shape
    return pl.pallas_call(
        functools.partial(base_kernel, groups, wanted),
        in_specs=[VMEM] * (3 + len(onces)),
        out_specs=VMEM,
        out_shape=shaped(2, len(wanted), ny, nx),
        compiler_params=pltpu.CompilerParams(vmem_limit_bytes=6 * MIB),
        cost_estimate=cost(len(wanted), 100 * ny * nx),
        name=name,
    )(sides, *near, *onces)


def ring_columns(table):
    ny = table.shape[1]
    return pltpu.roll(table[...], ny - lax.axis_index("z") * (ny // lax.axis_size("z")), 1)


def potential_plane(v_local, columns, hats, z):
    hat = jnp.concatenate([h[:, z, :] for h in hats], axis=0)
    return v_local[z] + dot(columns, hat)


def outer_kernel(v_local, table, *refs):
    hats, (first, last) = refs[:-2], refs[-2:]
    columns = ring_columns(table)
    first[0] = potential_plane(v_local, columns, hats, 0)
    last[0] = potential_plane(v_local, columns, hats, v_local.shape[0] - 1)


def outer_potential(v_local, table, hats):
    planes, ny, nx = v_local.shape
    return pl.pallas_call(
        outer_kernel,
        in_specs=[VMEM] * (2 + len(hats)),
        out_specs=[VMEM] * 2,
        out_shape=[shaped(1, ny, nx)] * 2,
        compiler_params=pltpu.CompilerParams(vmem_limit_bytes=6 * MIB),
        name="outer_potential",
    )(v_local, table, *hats)


def inner_kernel(once_groups, base_groups, hat_count, *refs):
    refs = list(refs)
    sides, v_local, table, v_first, v_last, re, im = [refs.pop(0) for _ in range(7)]
    hats = [refs.pop(0) for _ in range(hat_count)]
    onces = [refs.pop(0) for _ in once_groups]
    bases = [refs.pop(0) for _ in base_groups]
    out_re, out_im, open_ends, pot, work, stage, sem = refs
    planes = re.shape[0]
    fields = (re, im)
    columns = ring_columns(table)
    at_once = functools.partial(once_plane, once_groups, onces)
    at_base = functools.partial(once_plane, base_groups, bases)
    work[:, 0] = jnp.zeros_like(work[:, 0])
    work[:, planes + 1] = jnp.zeros_like(work[:, planes + 1])

    def update_plane(z):
        here = pot[z]
        mids, seconds = [], []
        for part in range(2):
            mid, kin = kinetic((work, (part, z)), (work, (part, z + 1)), (work, (part, z + 2)), sides)
            mids.append(mid)
            seconds.append(kin + here * (whole(at_once(part, z)) + mid))
        new_re = whole(at_base(0, z)) + TIME_STEP * mids[1] - HALF_SQ * seconds[0]
        new_im = whole(at_base(1, z)) - TIME_STEP * mids[0] - HALF_SQ * seconds[1]
        return new_re, new_im

    copies = []

    def finish(z):
        new = update_plane(z)
        for part, out in enumerate((out_re, out_im)):
            if z in (0, planes - 1):
                open_ends[part, 0 if z == 0 else 1] = new[part]
            else:
                stage[part, z - 1] = new[part]
                copy = pltpu.make_async_copy(stage.at[part, z - 1], out.at[0, z], sem.at[part, z - 1])
                copy.start()
                copies.append(copy)

    for z in range(planes):
        if z == 0:
            here = v_first[0]
        elif z == planes - 1:
            here = v_last[0]
        else:
            here = potential_plane(v_local, columns, hats, z)
        pot[z] = here
        for part in range(2):
            work[part, z + 1] = here * fields[part][z]
        if z >= 1:
            finish(z - 1)
    finish(planes - 1)
    for copy in copies:
        copy.wait()


def inner_update(sides, v_local, table, v_first, v_last, near, hats, onces, once_groups, bases, base_groups):
    planes, ny, nx = v_local.shape
    operands = [sides, v_local, table, v_first, v_last, *near, *hats, *onces, *bases]
    full = shaped(1, planes, ny, nx)
    return pl.pallas_call(
        functools.partial(inner_kernel, once_groups, base_groups, len(hats)),
        in_specs=[VMEM] * len(operands),
        out_specs=[ANY, ANY, VMEM],
        out_shape=[full, full, shaped(2, 2, ny, nx)],
        scratch_shapes=[
            plane_scratch(planes, ny=ny, nx=nx),
            plane_scratch(2, planes + 2, ny=ny, nx=nx),
            plane_scratch(2, planes - 2, ny=ny, nx=nx),
            pltpu.SemaphoreType.DMA((2, planes - 2)),
        ],
        compiler_params=pltpu.CompilerParams(vmem_limit_bytes=14 * MIB),
        cost_estimate=cost(planes, 400 * ny * nx),
        name="inner_update",
    )(*operands)


def close_kernel(open_ends, v_before, v_after, low, high, _re, _im, out_re, out_im, stage, sem):
    planes = out_re.shape[1]
    copies = []
    for slot, (z, v_ref, edge, first) in enumerate(((0, v_before, low, 1), (planes - 1, v_after, high, 0))):
        for part, out in enumerate((out_re, out_im)):
            beyond = v_ref[0] * edge[2 * part + first]
            stage[part, slot] = open_ends[part, slot] - (HALF_SQ * KINETIC) * beyond
            copy = pltpu.make_async_copy(stage.at[part, slot], out.at[0, z], sem.at[part, slot])
            copy.start()
            copies.append(copy)
    for copy in copies:
        copy.wait()


def close_ends(new_re, new_im, open_ends, v_before, v_after, edges):
    _, _, ny, nx = open_ends.shape
    return pl.pallas_call(
        close_kernel,
        in_specs=[VMEM] * 5 + [ANY, ANY],
        out_specs=[ANY, ANY],
        out_shape=[shaped(*new_re.shape)] * 2,
        input_output_aliases={5: 0, 6: 1},
        scratch_shapes=[plane_scratch(2, 2, ny=ny, nx=nx), pltpu.SemaphoreType.DMA((2, 2))],
        compiler_params=pltpu.CompilerParams(vmem_limit_bytes=4 * MIB),
        name="close_ends",
    )(open_ends, v_before, v_after, *edges, new_re, new_im)


def ring(axis, shift):
    count = lax.axis_size(axis)
    return [(i, (i + shift) % count) for i in range(count)]


def forward(value, axis="z"):
    return lax.ppermute(value, axis, ring(axis, 1))


def backward(value, axis="z"):
    return lax.ppermute(value, axis, ring(axis, -1))


def slab_shift(value, shift):
    return lax.ppermute(value, "slab", ring("slab", shift))


def after(value, *others):
    return lax.optimization_barrier((value,) + others)[0]


def sum_over_ring(pieces, beside):
    s0, s1, s2, s3, s4_first, s4_second, s5, s6, s7 = pieces
    half = s4_first.shape[1]
    got_up, got_down = forward(s4_first), backward(s4_second)
    up = jnp.concatenate([s3[:, :half] + got_up, s3[:, half:]], axis=1)
    down = jnp.concatenate([s5[:, :half], s5[:, half:] + got_down], axis=1)
    up, down = forward(up), backward(down)
    up = after(up, *beside[0])
    up, down = forward(up + s2), backward(down + s6)
    up = after(up, *beside[1])
    up, down = forward(up + s1), backward(down + s7)
    up = after(up, *beside[2])
    return add_shares(s0, up, down)


def gather_over_ring(block, beside):
    half = block.shape[0] // 2
    up1, down1 = forward(block), backward(block)
    up1 = after(up1, *beside[0])
    up2, down2 = forward(up1), backward(down1)
    up2 = after(up2, *beside[1])
    up3, down3 = forward(up2), backward(down2)
    up4, down4 = forward(up3[:half]), backward(down3[half:])
    return [block, down1, down2, down3, up4, down4, up3, up2, up1]


def across(value):
    return lax.all_to_all(value, ("y", "slab"), split_axis=0, concat_axis=0, tiled=True)


def on_device(psi_re, psi_im, v_local, n_ground):
    total_orbs = psi_re.shape[0] * lax.axis_size("y") * lax.axis_size("z")
    planes, ny, nx = v_local.shape
    nz = planes * lax.axis_size("slab")
    y_table, x_table, z_table = cas_table(ny), cas_table(nx), cas_table(nz)

    pieces, to_prev, to_next = density(psi_re, psi_im, v_local, n_ground, y_table, total_orbs)
    near = (psi_re[0], psi_im[0])
    low, high = slab_shift(to_next, 1), slab_shift(to_prev, -1)
    edges = (low, high)

    middle = planes // 2
    once_groups = [list(range(1, middle)), list(range(middle, planes - 1)), [-1, 0, planes - 1, planes]]
    base_groups = [list(range(middle)), list(range(middle, planes))]
    sides = neighbour_matrix(nx)
    onces = [
        once(sides, near, (), once_groups[0], "once_a"),
        once(sides, near, (), once_groups[1], "once_b"),
        once(sides, near, edges, once_groups[2], "once_c"),
    ]
    bases = [
        base(sides, near, onces, once_groups, group, name) for group, name in zip(base_groups, ("base_a", "base_b"))
    ]
    share = sum_over_ring(pieces, [[onces[0]], [onces[1]], [onces[2]]])
    pencils = across(share).reshape(SIDES * nz, nx)
    hats = gather_over_ring(across(solve(pencils, x_table, z_table, ny, planes)), [[bases[0]], [bases[1]]])

    v_first, v_last = outer_potential(v_local, y_table, hats)
    v_before, v_after = slab_shift(v_last, 1), slab_shift(v_first, -1)
    new_re, new_im, open_ends = inner_update(
        sides, v_local, y_table, v_first, v_last, near, hats, onces, once_groups, bases, base_groups
    )
    return tuple(close_ends(new_re, new_im, open_ends, v_before, v_after, edges))


def solution(mesh):
    orbs, slabs = mesh.devices.shape
    mesh = Mesh(mesh.devices.reshape(SIDES, orbs // SIDES, slabs), ("y", "z", "slab"))
    orb = ("y", "z")
    placed = (
        P(orb, "slab", None, None),
        P(orb, "slab", None, None),
        P("slab", None, None),
        P("slab", orb, None),
    )
    return jax.shard_map(
        on_device,
        mesh=mesh,
        in_specs=placed,
        out_specs=(P(orb, "slab", None, None), P(orb, "slab", None, None)),
        check_vma=False,
    )
```

```python
import functools
import math

import jax
import jax.numpy as jnp
import numpy as np
from jax import lax
from jax.experimental import pallas as pl
from jax.experimental.pallas import tpu as pltpu
from jax.sharding import Mesh
from jax.sharding import PartitionSpec as P

SPACING = 0.5
TIME_STEP = 0.02
HALF_SQ = 0.5 * TIME_STEP * TIME_STEP
KINETIC = -0.5 / (SPACING * SPACING)
HIGHEST = lax.Precision.HIGHEST
SIDES = 2
MIB = 1 << 20
VMEM = pl.BlockSpec(memory_space=pltpu.VMEM)
ANY = pl.BlockSpec(memory_space=pl.ANY)


def cas_table(length):
    index = np.arange(length)
    angles = (index[:, None] * index[None, :] % length) * (2.0 * math.pi / length)
    return jnp.asarray((np.cos(angles) + np.sin(angles)).astype(np.float32))


def dot(left, right):
    return jnp.dot(left, right, precision=HIGHEST, preferred_element_type=jnp.float32)


def shaped(*shape):
    return jax.ShapeDtypeStruct(shape, jnp.float32)


def plane_scratch(*lead, ny, nx):
    return pltpu.VMEM(lead + (ny, nx), jnp.float32)


def cost(microseconds):
    return pl.CostEstimate(flops=0, bytes_accessed=int(microseconds * 3.6e6), transcendentals=0)


def lower_core():
    return lax.rem(lax.axis_index("slab"), 2) == 0


def fill_rows(rows, table):
    ring = lax.axis_size("z")
    width = rows.shape[0] // ring
    z = lax.axis_index("z")
    for offset in range(ring):
        start = pl.multiple_of(lax.rem(z + offset, ring) * width, width)
        rows[offset * width : (offset + 1) * width, :] = table[pl.ds(start, width), :]


def density_kernel(scale, psi_re, psi_im, ground, y_table, *refs):
    rho, rows, first, second, to_mate, to_other = refs[:6]
    near, table, own_ground, plane_sem, small_sem = refs[6:]
    planes = near.shape[1]
    groups = plane_sem.shape[1]
    part_planes = planes // groups
    small = [
        pltpu.make_async_copy(y_table, table, small_sem.at[0]),
        pltpu.make_async_copy(ground, own_ground, small_sem.at[1]),
    ]
    copies = []
    for group in range(groups):
        some = pl.ds(group * part_planes, part_planes)
        copies.append(
            [
                pltpu.make_async_copy(psi.at[0, some], near.at[part, some], plane_sem.at[part, group])
                for part, psi in enumerate((psi_re, psi_im))
            ]
        )
    for copy in copies[0] + small + sum(copies[1:], []):
        copy.start()
    for copy in small:
        copy.wait()
    fill_rows(rows, table)
    ground_rows = own_ground.shape[1]
    place = lax.axis_index("y") * lax.axis_size("z") + lax.axis_index("z")
    own = pl.ds(pl.multiple_of(place * ground_rows, ground_rows), ground_rows)
    width = first.shape[1] + second.shape[1]
    far = rows[rows.shape[0] // 2 : rows.shape[0] // 2 + width, :]
    for group in range(groups):
        for copy in copies[group]:
            copy.wait()
        some = range(group * part_planes, (group + 1) * part_planes)
        for z in some:
            re, im = near[0, z], near[1, z]
            rho[z] = scale * (re * re + im * im)
            rho[z, own, :] = rho[z, own, :] - own_ground[z]
        for z in some:
            image = dot(far, rho[z])
            first[z] = image[: first.shape[1]]
            second[z] = image[first.shape[1] :]
    lower = lower_core()

    def fill_edges(low_target, high_target):
        for part in range(2):
            for which in range(2):
                low_target[2 * part + which] = near[part, which]
                high_target[2 * part + which] = near[part, planes - 2 + which]

    pl.when(lower)(functools.partial(fill_edges, to_other, to_mate))
    pl.when(jnp.logical_not(lower))(functools.partial(fill_edges, to_mate, to_other))


def density(psi_re, psi_im, n_ground, y_table, total_orbs):
    _, planes, ny, nx = psi_re.shape
    half = ny // lax.axis_size("z") // 2
    shapes = [(planes, ny, nx), (ny, ny), (planes, half, nx), (planes, half, nx)] + [(4, ny, nx)] * 2
    far = [pltpu.with_memory_space_constraint(a, pltpu.HBM) for a in (psi_re, psi_im, n_ground, y_table)]
    return pl.pallas_call(
        functools.partial(density_kernel, 2.0 / total_orbs),
        in_specs=[ANY] * 4,
        out_specs=[VMEM] * len(shapes),
        out_shape=[pltpu.VMEM(shape, jnp.float32) for shape in shapes],
        scratch_shapes=[
            plane_scratch(2, planes, ny=ny, nx=nx),
            pltpu.VMEM((ny, ny), jnp.float32),
            pltpu.VMEM(n_ground.shape, jnp.float32),
            pltpu.SemaphoreType.DMA((2, 2)),
            pltpu.SemaphoreType.DMA((2,)),
        ],
        compiler_params=pltpu.CompilerParams(vmem_limit_bytes=8 * MIB),
        name="density",
    )(*far)


def shares_kernel(rho, rows, *pieces):
    width = pieces[0].shape[1]
    for z in range(rho.shape[0]):
        image = dot(rows[...], rho[z])
        for offset, piece in zip((0, 1, 2, 3, 5, 6, 7), pieces):
            piece[z] = image[offset * width : (offset + 1) * width]


def shares(rho, rows):
    planes, ny, nx = rho.shape
    width = ny // lax.axis_size("z")
    return pl.pallas_call(
        shares_kernel,
        in_specs=[VMEM] * 2,
        out_specs=[VMEM] * 7,
        out_shape=[pltpu.VMEM((planes, width, nx), jnp.float32)] * 7,
        compiler_params=pltpu.CompilerParams(vmem_limit_bytes=4 * MIB),
        cost_estimate=cost(2.0),
        name="shares",
    )(rho, rows)


def share_kernel(own, up, down, out):
    for z in range(own.shape[0]):
        out[:, z, :] = own[z] + up[z] + down[z]


def add_shares(own, up, down):
    planes, rows, nx = own.shape
    return pl.pallas_call(
        share_kernel,
        in_specs=[VMEM] * 3,
        out_specs=VMEM,
        out_shape=shaped(rows, planes, nx),
        compiler_params=pltpu.CompilerParams(vmem_limit_bytes=4 * MIB),
        name="add_shares",
    )(own, up, down)


def wave_sq(freq_index, length):
    signed = jnp.where(freq_index * 2 <= length, freq_index, freq_index - length)
    wave_number = signed.astype(jnp.float32) * (2.0 * math.pi / (length * SPACING))
    return wave_number * wave_number


def solve_kernel(y_len, field, x_table, z_table, out):
    nz, nx = z_table.shape[0], x_table.shape[0]
    half = out.shape[0] // SIDES
    width = y_len // lax.axis_size("z")
    ky = lax.axis_index("z") * width + lax.axis_index("y") * lax.axis_size("slab") + lax.axis_index("slab")
    z_index = lax.broadcasted_iota(jnp.int32, (nz, nx), 0)
    x_index = lax.broadcasted_iota(jnp.int32, (nz, nx), 1)
    y_index = jnp.full((nz, nx), ky, jnp.int32)
    total = wave_sq(z_index, nz) + wave_sq(y_index, y_len) + wave_sq(x_index, nx)
    anchor = (z_index == 0) & (y_index == 0) & (x_index == 0)
    safe = jnp.where(anchor, jnp.float32(1.0), total)
    greens = jnp.where(anchor, jnp.float32(0.0), (4.0 * math.pi) / safe) * (1.0 / (nz * y_len * nx))
    rho = field[0:nz] + field[nz : 2 * nz]
    spectrum = dot(z_table[...], dot(rho, x_table[...]))
    solved = dot(dot(z_table[...], spectrum * greens), x_table[...])
    solved = solved.reshape((half,) + out.shape[1:])
    out[0:half] = solved
    out[half:] = solved


def solve(field, x_table, z_table, y_len, planes):
    rows, nx = field.shape
    return pl.pallas_call(
        functools.partial(solve_kernel, y_len),
        in_specs=[VMEM] * 3,
        out_specs=VMEM,
        out_shape=shaped(rows // planes, planes, nx),
        compiler_params=pltpu.CompilerParams(vmem_limit_bytes=8 * MIB),
        name="solve_xz",
    )(field, x_table, z_table)


def whole(plane):
    ref, lead = plane
    return ref[lead]


def neighbour_matrix(length):
    matrix = np.zeros((length, length), np.float32)
    index = np.arange(length)
    matrix[index, (index + 1) % length] = KINETIC
    matrix[index, (index - 1) % length] = KINETIC
    return jnp.asarray(matrix, jnp.bfloat16)


def kinetic(below, plane, above, sides):
    mid = whole(plane)
    high = mid.astype(jnp.bfloat16)
    rest = (mid - high.astype(jnp.float32)).astype(jnp.bfloat16)
    matrix = sides[...]
    along_x = jnp.dot(high, matrix, preferred_element_type=jnp.float32)
    along_x = along_x + jnp.dot(rest, matrix, preferred_element_type=jnp.float32)
    along_y = pltpu.roll(mid, 1, 0) + pltpu.roll(mid, mid.shape[0] - 1, 0)
    along_z = whole(below) + whole(above)
    return mid, along_x + (KINETIC * (along_y + along_z) - (6.0 * KINETIC) * mid)


def by_side(edges, run):
    mate, other = edges
    lower = lower_core()
    pl.when(lower)(functools.partial(run, other, mate))
    pl.when(jnp.logical_not(lower))(functools.partial(run, mate, other))


def psi_plane(fields, low, high, planes, part, z):
    if z < 0:
        return (low, (2 * part + z + 2,))
    if z >= planes:
        return (high, (2 * part + z - planes,))
    return (fields[part], (z,))


def once_kernel(planes, wanted, with_edges, sides, *refs):
    fields, edges, out = refs[:2], refs[2:-1], refs[-1]

    def run(low, high):
        at = functools.partial(psi_plane, fields, low, high, planes)
        for slot, z in enumerate(wanted):
            for part in range(2):
                _, value = kinetic(at(part, z - 1), at(part, z), at(part, z + 1), sides)
                out[part, slot] = value

    if with_edges:
        by_side(edges, run)
    else:
        run(None, None)


def once(sides, near, edges, wanted, name):
    planes, ny, nx = near[0].shape
    return pl.pallas_call(
        functools.partial(once_kernel, planes, wanted, bool(edges)),
        in_specs=[VMEM] * (3 + len(edges)),
        out_specs=VMEM,
        out_shape=shaped(2, len(wanted), ny, nx),
        compiler_params=pltpu.CompilerParams(vmem_limit_bytes=6 * MIB),
        cost_estimate=cost(0.3 * len(wanted)),
        name=name,
    )(sides, *near, *edges)


def once_plane(groups, refs, part, z):
    for ref, group in zip(refs, groups):
        if z in group:
            return (ref, (part, group.index(z)))


def base_kernel(groups, wanted, sides, re, im, *refs):
    onces, out = refs[:-1], refs[-1]
    at = functools.partial(once_plane, groups, onces)
    for slot, z in enumerate(wanted):
        first_re, second_re = kinetic(at(0, z - 1), at(0, z), at(0, z + 1), sides)
        first_im, second_im = kinetic(at(1, z - 1), at(1, z), at(1, z + 1), sides)
        out[0, slot] = re[z] + TIME_STEP * first_im - HALF_SQ * second_re
        out[1, slot] = im[z] - TIME_STEP * first_re - HALF_SQ * second_im


def base(sides, near, onces, groups, wanted, name):
    planes, ny, nx = near[0].shape
    return pl.pallas_call(
        functools.partial(base_kernel, groups, wanted),
        in_specs=[VMEM] * (3 + len(onces)),
        out_specs=VMEM,
        out_shape=shaped(2, len(wanted), ny, nx),
        compiler_params=pltpu.CompilerParams(vmem_limit_bytes=6 * MIB),
        cost_estimate=cost(0.4 * len(wanted)),
        name=name,
    )(sides, *near, *onces)


def ring_columns(table):
    ny = table.shape[1]
    return pltpu.roll(table[...], ny - lax.axis_index("z") * (ny // lax.axis_size("z")), 1)


def terms(value, count):
    found = []
    for _ in range(count):
        found.append(value.astype(jnp.bfloat16))
        value = value - found[-1].astype(jnp.float32)
    return found


LEFT_TERMS = (0, 0, 1, 1, 0, 2)
RIGHT_TERMS = (0, 1, 0, 1, 2, 0)


def early_kernel(v_local, table, *refs):
    hats, (pot, tail) = refs[:-2], refs[-2:]
    columns = ring_columns(table)
    width = hats[0].shape[0]
    first = columns.shape[1] // 2
    left = terms(columns[:, first : first + width], 3)
    tail[...] = jnp.concatenate([left[i] for i in LEFT_TERMS], axis=1)
    for z in range(v_local.shape[0]):
        rows = [hat[:, z, :] for hat in hats]
        rows.insert(len(hats) // 2 + 1, jnp.zeros_like(rows[0]))
        pot[z] = v_local[z] + dot(columns, jnp.concatenate(rows, axis=0))


def early_potential(v_local, table, hats):
    planes, ny, nx = v_local.shape
    width = ny // lax.axis_size("z")
    return pl.pallas_call(
        early_kernel,
        in_specs=[VMEM] * (2 + len(hats)),
        out_specs=[VMEM] * 2,
        out_shape=[shaped(planes, ny, nx), jax.ShapeDtypeStruct((ny, len(LEFT_TERMS) * width), jnp.bfloat16)],
        compiler_params=pltpu.CompilerParams(vmem_limit_bytes=6 * MIB),
        cost_estimate=cost(2.3),
        name="early_potential",
    )(v_local, table, *hats)


def potential_plane(early, tail, late, z):
    right = terms(jnp.concatenate([hat[:, z, :] for hat in late], axis=0), 3)
    stacked = jnp.concatenate([right[i] for i in RIGHT_TERMS], axis=0)
    return early[z] + jnp.dot(tail[...], stacked, preferred_element_type=jnp.float32)


def outer_kernel(early, tail, up, down, to_mate, to_other):
    first = potential_plane(early, tail, (up, down), 0)
    last = potential_plane(early, tail, (up, down), early.shape[0] - 1)
    lower = lower_core()
    to_mate[0] = jnp.where(lower, last, first)
    to_other[0] = jnp.where(lower, first, last)


def outer_potential(early, tail, late):
    planes, ny, nx = early.shape
    return pl.pallas_call(
        outer_kernel,
        in_specs=[VMEM] * (2 + len(late)),
        out_specs=[VMEM] * 2,
        out_shape=[shaped(1, ny, nx)] * 2,
        compiler_params=pltpu.CompilerParams(vmem_limit_bytes=4 * MIB),
        name="outer_potential",
    )(early, tail, *late)


def inner_kernel(once_groups, base_groups, *refs):
    refs = list(refs)
    sides, early, tail, late_up, late_down, re, im = [refs.pop(0) for _ in range(7)]
    onces = [refs.pop(0) for _ in once_groups]
    bases = [refs.pop(0) for _ in base_groups]
    out_re, out_im, open_ends, pot, work, stage, sem = refs
    planes = re.shape[0]
    fields = (re, im)
    at_once = functools.partial(once_plane, once_groups, onces)
    at_base = functools.partial(once_plane, base_groups, bases)
    work[:, 0] = jnp.zeros_like(work[:, 0])
    work[:, planes + 1] = jnp.zeros_like(work[:, planes + 1])

    def update_plane(z):
        here = pot[z]
        mids, seconds = [], []
        for part in range(2):
            mid, kin = kinetic((work, (part, z)), (work, (part, z + 1)), (work, (part, z + 2)), sides)
            mids.append(mid)
            seconds.append(kin + here * (whole(at_once(part, z)) + mid))
        new_re = whole(at_base(0, z)) + TIME_STEP * mids[1] - HALF_SQ * seconds[0]
        new_im = whole(at_base(1, z)) - TIME_STEP * mids[0] - HALF_SQ * seconds[1]
        return new_re, new_im

    copies = []

    def finish(z):
        new = update_plane(z)
        for part, out in enumerate((out_re, out_im)):
            if z in (0, planes - 1):
                open_ends[part, 0 if z == 0 else 1] = new[part]
            else:
                stage[part, z - 1] = new[part]
                copy = pltpu.make_async_copy(stage.at[part, z - 1], out.at[0, z], sem.at[part, z - 1])
                copy.start()
                copies.append(copy)

    for z in range(planes):
        here = potential_plane(early, tail, (late_up, late_down), z)
        pot[z] = here
        for part in range(2):
            work[part, z + 1] = here * fields[part][z]
        if z >= 1:
            finish(z - 1)
    finish(planes - 1)
    for copy in copies:
        copy.wait()


def inner_update(sides, early, tail, late, near, onces, once_groups, bases, base_groups):
    planes, ny, nx = early.shape
    operands = [sides, early, tail, *late, *near, *onces, *bases]
    full = shaped(1, planes, ny, nx)
    return pl.pallas_call(
        functools.partial(inner_kernel, once_groups, base_groups),
        in_specs=[VMEM] * len(operands),
        out_specs=[ANY, ANY, VMEM],
        out_shape=[full, full, shaped(2, 2, ny, nx)],
        scratch_shapes=[
            plane_scratch(planes, ny=ny, nx=nx),
            plane_scratch(2, planes + 2, ny=ny, nx=nx),
            plane_scratch(2, planes - 2, ny=ny, nx=nx),
            pltpu.SemaphoreType.DMA((2, planes - 2)),
        ],
        compiler_params=pltpu.CompilerParams(vmem_limit_bytes=14 * MIB),
        cost_estimate=cost(4.3),
        name="inner_update",
    )(*operands)


def close_kernel(open_ends, v_mate, v_other, mate, other, _re, _im, out_re, out_im, stage, sem):
    planes = out_re.shape[1]

    def run(below, above):
        for slot, ((v_ref, edge), first) in enumerate(((below, 1), (above, 0))):
            for part in range(2):
                beyond = v_ref[0] * edge[2 * part + first]
                stage[part, slot] = open_ends[part, slot] - (HALF_SQ * KINETIC) * beyond

    by_side(((v_mate, mate), (v_other, other)), run)
    copies = []
    for slot, z in enumerate((0, planes - 1)):
        for part, out in enumerate((out_re, out_im)):
            copy = pltpu.make_async_copy(stage.at[part, slot], out.at[0, z], sem.at[part, slot])
            copy.start()
            copies.append(copy)
    for copy in copies:
        copy.wait()


def close_ends(new_re, new_im, open_ends, v_planes, edges):
    _, _, ny, nx = open_ends.shape
    return pl.pallas_call(
        close_kernel,
        in_specs=[VMEM] * 5 + [ANY, ANY],
        out_specs=[ANY, ANY],
        out_shape=[shaped(*new_re.shape)] * 2,
        input_output_aliases={5: 0, 6: 1},
        scratch_shapes=[plane_scratch(2, 2, ny=ny, nx=nx), pltpu.SemaphoreType.DMA((2, 2))],
        compiler_params=pltpu.CompilerParams(vmem_limit_bytes=4 * MIB),
        name="close_ends",
    )(open_ends, *v_planes, *edges, new_re, new_im)


def ring(axis, shift):
    count = lax.axis_size(axis)
    return [(i, (i + shift) % count) for i in range(count)]


def forward(value, axis="z"):
    return lax.ppermute(value, axis, ring(axis, 1))


def backward(value, axis="z"):
    return lax.ppermute(value, axis, ring(axis, -1))


def swap_edges(to_mate, to_other):
    count = lax.axis_size("slab")
    others = [(i, (i - 1) % count if i % 2 == 0 else (i + 1) % count) for i in range(count)]
    from_other = lax.ppermute(to_other, "slab", others)
    from_mate = lax.ppermute(to_mate, "slab", [(i, i ^ 1) for i in range(count)])
    return from_mate, from_other


def after(value, *others):
    return lax.optimization_barrier((value,) + others)[0]


def sum_over_ring(first, second, pieces, beside):
    s0, s1, s2, s3, s5, s6, s7 = pieces
    half = first.shape[1]
    got_up, got_down = forward(first), backward(second)
    up = jnp.concatenate([s3[:, :half] + got_up, s3[:, half:]], axis=1)
    down = jnp.concatenate([s5[:, :half], s5[:, half:] + got_down], axis=1)
    up, down = forward(up), backward(down)
    up = after(up, *beside[0])
    up, down = forward(up + s2), backward(down + s6)
    up = after(up, *beside[1])
    up, down = forward(up + s1), backward(down + s7)
    up = after(up, *beside[2])
    return add_shares(s0, up, down)


def gather_over_ring(block, beside, early):
    half = block.shape[0] // 2
    up1, down1 = forward(block), backward(block)
    up1 = after(up1, *beside[0])
    up2, down2 = forward(up1), backward(down1)
    up2 = after(up2, *beside[1])
    up3, down3 = forward(up2), backward(down2)
    up4, down4 = forward(up3[:half]), backward(down3[half:])
    made = early([block, down1, down2, down3, up3, up2, up1])
    return made, (after(up4, *made), down4)


def across(value):
    return lax.all_to_all(value, ("y", "slab"), split_axis=0, concat_axis=0, tiled=True)


def on_device(psi_re, psi_im, v_local, n_ground):
    total_orbs = psi_re.shape[0] * lax.axis_size("y") * lax.axis_size("z")
    planes, ny, nx = v_local.shape
    nz = planes * lax.axis_size("slab")
    y_table, x_table, z_table = cas_table(ny), cas_table(nx), cas_table(nz)

    rho, rows, first, second, to_mate, to_other = density(psi_re, psi_im, n_ground, y_table, total_orbs)
    pieces = shares(rho, rows)
    near = (psi_re[0], psi_im[0])
    edges = swap_edges(to_mate, to_other)

    middle = planes // 2
    once_groups = [list(range(1, middle)), list(range(middle, planes - 1)), [-1, 0, planes - 1, planes]]
    base_groups = [list(range(middle)), list(range(middle, planes))]
    sides = neighbour_matrix(nx)
    onces = [
        once(sides, near, (), once_groups[0], "once_a"),
        once(sides, near, (), once_groups[1], "once_b"),
        once(sides, near, edges, once_groups[2], "once_c"),
    ]
    bases = [
        base(sides, near, onces, once_groups, group, name) for group, name in zip(base_groups, ("base_a", "base_b"))
    ]
    share = sum_over_ring(first, second, pieces, [[onces[0]], [onces[1]], [onces[2]]])
    pencils = across(share).reshape(SIDES * nz, nx)
    (early, tail), late = gather_over_ring(
        across(solve(pencils, x_table, z_table, ny, planes)),
        [[bases[0]], [bases[1]]],
        functools.partial(early_potential, v_local, y_table),
    )
    v_planes = swap_edges(*outer_potential(early, tail, late))
    new_re, new_im, open_ends = inner_update(
        sides, early, tail, late, near, onces, once_groups, bases, base_groups
    )
    return tuple(close_ends(new_re, new_im, open_ends, v_planes, edges))


def solution(mesh):
    orbs, slabs = mesh.devices.shape
    mesh = Mesh(mesh.devices.reshape(SIDES, orbs // SIDES, slabs), ("y", "z", "slab"))
    orb = ("y", "z")
    placed = (
        P(orb, "slab", None, None),
        P(orb, "slab", None, None),
        P("slab", None, None),
        P("slab", orb, None),
    )
    return jax.shard_map(
        on_device,
        mesh=mesh,
        in_specs=placed,
        out_specs=(P(orb, "slab", None, None), P(orb, "slab", None, None)),
        check_vma=False,
    )
```

```python
import functools
import math

import jax
import jax.numpy as jnp
import numpy as np
from jax import lax
from jax.experimental import pallas as pl
from jax.experimental.pallas import tpu as pltpu
from jax.sharding import Mesh
from jax.sharding import PartitionSpec as P

SPACING = 0.5
TIME_STEP = 0.02
HALF_SQ = 0.5 * TIME_STEP * TIME_STEP
KINETIC = -0.5 / (SPACING * SPACING)
HIGHEST = lax.Precision.HIGHEST
SIDES = 2
MIB = 1 << 20
VMEM = pl.BlockSpec(memory_space=pltpu.VMEM)
ANY = pl.BlockSpec(memory_space=pl.ANY)


def cas_table(length):
    index = np.arange(length)
    angles = (index[:, None] * index[None, :] % length) * (2.0 * math.pi / length)
    return jnp.asarray((np.cos(angles) + np.sin(angles)).astype(np.float32))


def dot(left, right):
    return jnp.dot(left, right, precision=HIGHEST, preferred_element_type=jnp.float32)


def terms(value, count):
    found = []
    for _ in range(count):
        found.append(value.astype(jnp.bfloat16))
        value = value - found[-1].astype(jnp.float32)
    return found


def dot_three(left, right):
    (a, b), (c, d) = terms(left, 2), terms(right, 2)

    def one(x, y):
        return jnp.dot(x, y, preferred_element_type=jnp.float32)

    return one(a, c) + (one(a, d) + one(b, c))


def shaped(*shape):
    return jax.ShapeDtypeStruct(shape, jnp.float32)


def plane_scratch(*lead, ny, nx):
    return pltpu.VMEM(lead + (ny, nx), jnp.float32)


def cost(microseconds):
    return pl.CostEstimate(flops=0, bytes_accessed=int(microseconds * 3.6e6), transcendentals=0)


def lower_core():
    return lax.rem(lax.axis_index("slab"), 2) == 0


def fill_rows(rows, table):
    ring = lax.axis_size("z")
    width = rows.shape[0] // ring
    z = lax.axis_index("z")
    step = 1 + lax.rem(z, 2) * (ring - 2)
    for offset in range(ring):
        start = pl.multiple_of(lax.rem(z + offset * step, ring) * width, width)
        rows[offset * width : (offset + 1) * width, :] = table[pl.ds(start, width), :]


def density_kernel(scale, psi_re, psi_im, ground, y_table, *refs):
    rho, rows, first, second, to_mate, to_other = refs[:6]
    near, table, own_ground, plane_sem, small_sem = refs[6:]
    planes = near.shape[1]
    groups = plane_sem.shape[1]
    part_planes = planes // groups
    small = [
        pltpu.make_async_copy(y_table, table, small_sem.at[0]),
        pltpu.make_async_copy(ground, own_ground, small_sem.at[1]),
    ]
    copies = []
    for group in range(groups):
        some = pl.ds(group * part_planes, part_planes)
        copies.append(
            [
                pltpu.make_async_copy(psi.at[0, some], near.at[part, some], plane_sem.at[part, group])
                for part, psi in enumerate((psi_re, psi_im))
            ]
        )
    for copy in copies[0] + small + sum(copies[1:], []):
        copy.start()
    for copy in small:
        copy.wait()
    fill_rows(rows, table)
    ground_rows = own_ground.shape[1]
    place = lax.axis_index("y") * lax.axis_size("z") + lax.axis_index("z")
    own = pl.ds(pl.multiple_of(place * ground_rows, ground_rows), ground_rows)
    width = first.shape[1] + second.shape[1]
    far = rows[rows.shape[0] // 2 : rows.shape[0] // 2 + width, :]
    for group in range(groups):
        for copy in copies[group]:
            copy.wait()
        some = range(group * part_planes, (group + 1) * part_planes)
        for z in some:
            re, im = near[0, z], near[1, z]
            rho[z] = scale * (re * re + im * im)
            rho[z, own, :] = rho[z, own, :] - own_ground[z]
        for z in some:
            image = dot(far, rho[z])
            first[z] = image[: first.shape[1]]
            second[z] = image[first.shape[1] :]
    lower = lower_core()

    def fill_edges(low_target, high_target):
        for part in range(2):
            for which in range(2):
                low_target[2 * part + which] = near[part, which]
                high_target[2 * part + which] = near[part, planes - 2 + which]

    pl.when(lower)(functools.partial(fill_edges, to_other, to_mate))
    pl.when(jnp.logical_not(lower))(functools.partial(fill_edges, to_mate, to_other))


def density(psi_re, psi_im, n_ground, y_table, total_orbs):
    _, planes, ny, nx = psi_re.shape
    half = ny // lax.axis_size("z") // 2
    shapes = [(planes, ny, nx), (ny, ny), (planes, half, nx), (planes, half, nx)] + [(4, ny, nx)] * 2
    far = [pltpu.with_memory_space_constraint(a, pltpu.HBM) for a in (psi_re, psi_im, n_ground, y_table)]
    return pl.pallas_call(
        functools.partial(density_kernel, 2.0 / total_orbs),
        in_specs=[ANY] * 4,
        out_specs=[VMEM] * len(shapes),
        out_shape=[pltpu.VMEM(shape, jnp.float32) for shape in shapes],
        scratch_shapes=[
            plane_scratch(2, planes, ny=ny, nx=nx),
            pltpu.VMEM((ny, ny), jnp.float32),
            pltpu.VMEM(n_ground.shape, jnp.float32),
            pltpu.SemaphoreType.DMA((2, 2)),
            pltpu.SemaphoreType.DMA((2,)),
        ],
        compiler_params=pltpu.CompilerParams(vmem_limit_bytes=8 * MIB),
        name="density",
    )(*far)


def shares_kernel(rho, rows, *pieces):
    width = pieces[0].shape[1]
    for z in range(rho.shape[0]):
        image = dot(rows[...], rho[z])
        for offset, piece in zip((0, 1, 2, 3, 5, 6, 7), pieces):
            piece[z] = image[offset * width : (offset + 1) * width]


def shares(rho, rows):
    planes, ny, nx = rho.shape
    width = ny // lax.axis_size("z")
    return pl.pallas_call(
        shares_kernel,
        in_specs=[VMEM] * 2,
        out_specs=[VMEM] * 7,
        out_shape=[pltpu.VMEM((planes, width, nx), jnp.float32)] * 7,
        compiler_params=pltpu.CompilerParams(vmem_limit_bytes=4 * MIB),
        cost_estimate=cost(2.0),
        name="shares",
    )(rho, rows)


def share_kernel(own, up, down, out):
    for z in range(own.shape[0]):
        out[:, z, :] = own[z] + up[z] + down[z]


def add_shares(own, up, down):
    planes, rows, nx = own.shape
    return pl.pallas_call(
        share_kernel,
        in_specs=[VMEM] * 3,
        out_specs=VMEM,
        out_shape=shaped(rows, planes, nx),
        compiler_params=pltpu.CompilerParams(vmem_limit_bytes=4 * MIB),
        name="add_shares",
    )(own, up, down)


def wave_sq(freq_index, length):
    signed = jnp.where(freq_index * 2 <= length, freq_index, freq_index - length)
    wave_number = signed.astype(jnp.float32) * (2.0 * math.pi / (length * SPACING))
    return wave_number * wave_number


def solve_kernel(y_len, field, x_table, z_table, out):
    nz, nx = z_table.shape[0], x_table.shape[0]
    half = out.shape[0] // SIDES
    width = y_len // lax.axis_size("z")
    ky = lax.axis_index("z") * width + lax.axis_index("y") * lax.axis_size("slab") + lax.axis_index("slab")
    z_index = lax.broadcasted_iota(jnp.int32, (nz, nx), 0)
    x_index = lax.broadcasted_iota(jnp.int32, (nz, nx), 1)
    y_index = jnp.full((nz, nx), ky, jnp.int32)
    total = wave_sq(z_index, nz) + wave_sq(y_index, y_len) + wave_sq(x_index, nx)
    anchor = (z_index == 0) & (y_index == 0) & (x_index == 0)
    safe = jnp.where(anchor, jnp.float32(1.0), total)
    greens = jnp.where(anchor, jnp.float32(0.0), (4.0 * math.pi) / safe) * (1.0 / (nz * y_len * nx))
    rho = field[0:nz] + field[nz : 2 * nz]
    spectrum = dot(z_table[...], dot(rho, x_table[...]))
    solved = dot_three(dot_three(z_table[...], spectrum * greens), x_table[...])
    solved = solved.reshape((half,) + out.shape[1:])
    out[0:half] = solved
    out[half:] = solved


def solve(field, x_table, z_table, y_len, planes):
    rows, nx = field.shape
    return pl.pallas_call(
        functools.partial(solve_kernel, y_len),
        in_specs=[VMEM] * 3,
        out_specs=VMEM,
        out_shape=shaped(rows // planes, planes, nx),
        compiler_params=pltpu.CompilerParams(vmem_limit_bytes=8 * MIB),
        name="solve_xz",
    )(field, x_table, z_table)


def whole(plane):
    ref, lead = plane
    return ref[lead]


def neighbour_matrix(length):
    matrix = np.zeros((length, length), np.float32)
    index = np.arange(length)
    matrix[index, (index + 1) % length] = KINETIC
    matrix[index, (index - 1) % length] = KINETIC
    return jnp.asarray(matrix, jnp.bfloat16)


def kinetic(below, plane, above, sides):
    mid = whole(plane)
    high = mid.astype(jnp.bfloat16)
    rest = (mid - high.astype(jnp.float32)).astype(jnp.bfloat16)
    matrix = sides[...]
    along_x = jnp.dot(high, matrix, preferred_element_type=jnp.float32)
    along_x = along_x + jnp.dot(rest, matrix, preferred_element_type=jnp.float32)
    along_y = pltpu.roll(mid, 1, 0) + pltpu.roll(mid, mid.shape[0] - 1, 0)
    along_z = whole(below) + whole(above)
    return mid, along_x + (KINETIC * (along_y + along_z) - (6.0 * KINETIC) * mid)


def by_side(edges, run):
    mate, other = edges
    lower = lower_core()
    pl.when(lower)(functools.partial(run, other, mate))
    pl.when(jnp.logical_not(lower))(functools.partial(run, mate, other))


def psi_plane(fields, low, high, planes, part, z):
    if z < 0:
        return (low, (2 * part + z + 2,))
    if z >= planes:
        return (high, (2 * part + z - planes,))
    return (fields[part], (z,))


def once_kernel(planes, wanted, with_edges, sides, *refs):
    fields, edges, out = refs[:2], refs[2:-1], refs[-1]

    def run(low, high):
        at = functools.partial(psi_plane, fields, low, high, planes)
        for slot, z in enumerate(wanted):
            for part in range(2):
                _, value = kinetic(at(part, z - 1), at(part, z), at(part, z + 1), sides)
                out[part, slot] = value

    if with_edges:
        by_side(edges, run)
    else:
        run(None, None)


def once(sides, near, edges, wanted, name):
    planes, ny, nx = near[0].shape
    return pl.pallas_call(
        functools.partial(once_kernel, planes, wanted, bool(edges)),
        in_specs=[VMEM] * (3 + len(edges)),
        out_specs=VMEM,
        out_shape=shaped(2, len(wanted), ny, nx),
        compiler_params=pltpu.CompilerParams(vmem_limit_bytes=6 * MIB),
        cost_estimate=cost(0.3 * len(wanted)),
        name=name,
    )(sides, *near, *edges)


def once_plane(groups, refs, part, z):
    for ref, group in zip(refs, groups):
        if z in group:
            return (ref, (part, group.index(z)))


def base_kernel(groups, wanted, sides, re, im, *refs):
    onces, out = refs[:-1], refs[-1]
    at = functools.partial(once_plane, groups, onces)
    for slot, z in enumerate(wanted):
        first_re, second_re = kinetic(at(0, z - 1), at(0, z), at(0, z + 1), sides)
        first_im, second_im = kinetic(at(1, z - 1), at(1, z), at(1, z + 1), sides)
        out[0, slot] = re[z] + TIME_STEP * first_im - HALF_SQ * second_re
        out[1, slot] = im[z] - TIME_STEP * first_re - HALF_SQ * second_im


def base(sides, near, onces, groups, wanted, name):
    planes, ny, nx = near[0].shape
    return pl.pallas_call(
        functools.partial(base_kernel, groups, wanted),
        in_specs=[VMEM] * (3 + len(onces)),
        out_specs=VMEM,
        out_shape=shaped(2, len(wanted), ny, nx),
        compiler_params=pltpu.CompilerParams(vmem_limit_bytes=6 * MIB),
        cost_estimate=cost(0.4 * len(wanted)),
        name=name,
    )(sides, *near, *onces)


def ring_columns(table):
    ny = table.shape[1]
    return pltpu.roll(table[...], ny - lax.axis_index("z") * (ny // lax.axis_size("z")), 1)


LEFT_TERMS = (0, 0, 1, 1, 0, 2)
RIGHT_TERMS = (0, 1, 0, 1, 2, 0)


def early_kernel(v_local, table, *refs):
    hats, (pot, tail) = refs[:-2], refs[-2:]
    columns = ring_columns(table)
    width = hats[0].shape[0]
    first = columns.shape[1] // 2
    left = terms(columns[:, first : first + width], 3)
    tail[...] = jnp.concatenate([left[i] for i in LEFT_TERMS], axis=1)
    hats = list(hats)
    hats.insert(len(hats) // 2 + 1, None)
    even = lax.rem(lax.axis_index("z"), 2) == 0

    def fill(order):
        for z in range(v_local.shape[0]):
            rows = [jnp.zeros((width, columns.shape[1]), jnp.float32) if h is None else h[:, z, :] for h in order]
            pot[z] = v_local[z] + dot(columns, jnp.concatenate(rows, axis=0))

    pl.when(even)(functools.partial(fill, hats))
    pl.when(jnp.logical_not(even))(functools.partial(fill, hats[:1] + hats[:0:-1]))


def early_potential(v_local, table, hats):
    planes, ny, nx = v_local.shape
    width = ny // lax.axis_size("z")
    return pl.pallas_call(
        early_kernel,
        in_specs=[VMEM] * (2 + len(hats)),
        out_specs=[VMEM] * 2,
        out_shape=[shaped(planes, ny, nx), jax.ShapeDtypeStruct((ny, len(LEFT_TERMS) * width), jnp.bfloat16)],
        compiler_params=pltpu.CompilerParams(vmem_limit_bytes=6 * MIB),
        cost_estimate=cost(2.3),
        name="early_potential",
    )(v_local, table, *hats)


def potential_plane(early, tail, late, z):
    right = terms(jnp.concatenate([hat[:, z, :] for hat in late], axis=0), 3)
    stacked = jnp.concatenate([right[i] for i in RIGHT_TERMS], axis=0)
    return early[z] + jnp.dot(tail[...], stacked, preferred_element_type=jnp.float32)


def outer_kernel(early, tail, up, down, to_mate, to_other):
    first = potential_plane(early, tail, (up, down), 0)
    last = potential_plane(early, tail, (up, down), early.shape[0] - 1)
    lower = lower_core()
    to_mate[0] = jnp.where(lower, last, first)
    to_other[0] = jnp.where(lower, first, last)


def outer_potential(early, tail, late):
    planes, ny, nx = early.shape
    return pl.pallas_call(
        outer_kernel,
        in_specs=[VMEM] * (2 + len(late)),
        out_specs=[VMEM] * 2,
        out_shape=[shaped(1, ny, nx)] * 2,
        compiler_params=pltpu.CompilerParams(vmem_limit_bytes=4 * MIB),
        name="outer_potential",
    )(early, tail, *late)


def inner_kernel(once_groups, base_groups, *refs):
    refs = list(refs)
    sides, early, tail, late_up, late_down, re, im = [refs.pop(0) for _ in range(7)]
    onces = [refs.pop(0) for _ in once_groups]
    bases = [refs.pop(0) for _ in base_groups]
    out_re, out_im, open_ends, pot, work, stage, sem = refs
    planes = re.shape[0]
    fields = (re, im)
    at_once = functools.partial(once_plane, once_groups, onces)
    at_base = functools.partial(once_plane, base_groups, bases)
    work[:, 0] = jnp.zeros_like(work[:, 0])
    work[:, planes + 1] = jnp.zeros_like(work[:, planes + 1])

    def update_plane(z):
        here = pot[z]
        mids, seconds = [], []
        for part in range(2):
            mid, kin = kinetic((work, (part, z)), (work, (part, z + 1)), (work, (part, z + 2)), sides)
            mids.append(mid)
            seconds.append(kin + here * (whole(at_once(part, z)) + mid))
        new_re = whole(at_base(0, z)) + TIME_STEP * mids[1] - HALF_SQ * seconds[0]
        new_im = whole(at_base(1, z)) - TIME_STEP * mids[0] - HALF_SQ * seconds[1]
        return new_re, new_im

    copies = []

    def finish(z):
        new = update_plane(z)
        for part, out in enumerate((out_re, out_im)):
            if z in (0, planes - 1):
                open_ends[part, 0 if z == 0 else 1] = new[part]
            else:
                stage[part, z - 1] = new[part]
                copy = pltpu.make_async_copy(stage.at[part, z - 1], out.at[0, z], sem.at[part, z - 1])
                copy.start()
                copies.append(copy)

    for z in range(planes):
        here = potential_plane(early, tail, (late_up, late_down), z)
        pot[z] = here
        for part in range(2):
            work[part, z + 1] = here * fields[part][z]
        if z >= 1:
            finish(z - 1)
    finish(planes - 1)
    for copy in copies:
        copy.wait()


def inner_update(sides, early, tail, late, near, onces, once_groups, bases, base_groups):
    planes, ny, nx = early.shape
    operands = [sides, early, tail, *late, *near, *onces, *bases]
    full = shaped(1, planes, ny, nx)
    return pl.pallas_call(
        functools.partial(inner_kernel, once_groups, base_groups),
        in_specs=[VMEM] * len(operands),
        out_specs=[ANY, ANY, VMEM],
        out_shape=[full, full, shaped(2, 2, ny, nx)],
        scratch_shapes=[
            plane_scratch(planes, ny=ny, nx=nx),
            plane_scratch(2, planes + 2, ny=ny, nx=nx),
            plane_scratch(2, planes - 2, ny=ny, nx=nx),
            pltpu.SemaphoreType.DMA((2, planes - 2)),
        ],
        compiler_params=pltpu.CompilerParams(vmem_limit_bytes=14 * MIB),
        cost_estimate=cost(4.3),
        name="inner_update",
    )(*operands)


def close_kernel(open_ends, v_mate, v_other, mate, other, _re, _im, out_re, out_im, stage, sem):
    planes = out_re.shape[1]

    def run(below, above):
        for slot, ((v_ref, edge), first) in enumerate(((below, 1), (above, 0))):
            for part in range(2):
                beyond = v_ref[0] * edge[2 * part + first]
                stage[part, slot] = open_ends[part, slot] - (HALF_SQ * KINETIC) * beyond

    by_side(((v_mate, mate), (v_other, other)), run)
    copies = []
    for slot, z in enumerate((0, planes - 1)):
        for part, out in enumerate((out_re, out_im)):
            copy = pltpu.make_async_copy(stage.at[part, slot], out.at[0, z], sem.at[part, slot])
            copy.start()
            copies.append(copy)
    for copy in copies:
        copy.wait()


def close_ends(new_re, new_im, open_ends, v_planes, edges):
    _, _, ny, nx = open_ends.shape
    return pl.pallas_call(
        close_kernel,
        in_specs=[VMEM] * 5 + [ANY, ANY],
        out_specs=[ANY, ANY],
        out_shape=[shaped(*new_re.shape)] * 2,
        input_output_aliases={5: 0, 6: 1},
        scratch_shapes=[plane_scratch(2, 2, ny=ny, nx=nx), pltpu.SemaphoreType.DMA((2, 2))],
        compiler_params=pltpu.CompilerParams(vmem_limit_bytes=4 * MIB),
        name="close_ends",
    )(open_ends, *v_planes, *edges, new_re, new_im)


def swap_near(value):
    return lax.ppermute(value, "z", [(i, i ^ 1) for i in range(lax.axis_size("z"))])


def swap_far(value):
    count = lax.axis_size("z")
    return lax.ppermute(value, "z", [(i, (i - 1) % count if i % 2 == 0 else (i + 1) % count) for i in range(count)])


def swap_edges(to_mate, to_other, same_on_orb=False):
    count = lax.axis_size("slab")
    pairs = []
    for y in range(SIDES):
        for slab in range(count):
            other = (slab - 1) % count if slab % 2 == 0 else (slab + 1) % count
            crossing = slab * 2 // count != other * 2 // count
            side = (y + 1) % SIDES if crossing and same_on_orb else y
            pairs.append((y * count + slab, side * count + other))
    from_other = lax.ppermute(to_other, ("y", "slab"), pairs)
    from_mate = lax.ppermute(to_mate, "slab", [(i, i ^ 1) for i in range(count)])
    return from_mate, from_other


def after(value, *others):
    return lax.optimization_barrier((value,) + others)[0]


def sum_over_ring(first, second, pieces, beside):
    s0, s1, s2, s3, s5, s6, s7 = pieces
    half = first.shape[1]
    near, far = swap_near(first), swap_far(second)
    near = jnp.concatenate([s5[:, :half] + near, s5[:, half:]], axis=1)
    far = jnp.concatenate([s3[:, :half], s3[:, half:] + far], axis=1)
    near, far = swap_far(near), swap_near(far)
    near, far = after(near, *beside[0]), after(far, *beside[0])
    near, far = swap_near(near + s2), swap_far(far + s6)
    near, far = after(near, *beside[1]), after(far, *beside[1])
    near, far = swap_far(near + s7), swap_near(far + s1)
    near, far = after(near, *beside[2]), after(far, *beside[2])
    return add_shares(s0, near, far)


def gather_over_ring(block, beside, early):
    half = block.shape[0] // 2
    near1, far1 = swap_near(block), swap_far(block)
    near1, far1 = after(near1, *beside[0]), after(far1, *beside[0])
    near2, far2 = swap_near(far1), swap_far(near1)
    near2, far2 = after(near2, *beside[1]), after(far2, *beside[1])
    near3, far3 = swap_near(far2), swap_far(near2)
    near4, far4 = swap_near(far3[:half]), swap_far(near3[half:])
    made = early([block, near1, near2, near3, far3, far2, far1])
    return made, (after(near4, *made), far4)


def across(value):
    return lax.all_to_all(value, ("y", "slab"), split_axis=0, concat_axis=0, tiled=True)


def on_device(psi_re, psi_im, v_local, n_ground):
    total_orbs = psi_re.shape[0] * lax.axis_size("y") * lax.axis_size("z")
    planes, ny, nx = v_local.shape
    nz = planes * lax.axis_size("slab")
    y_table, x_table, z_table = cas_table(ny), cas_table(nx), cas_table(nz)

    rho, rows, first, second, to_mate, to_other = density(psi_re, psi_im, n_ground, y_table, total_orbs)
    pieces = shares(rho, rows)
    near = (psi_re[0], psi_im[0])
    edges = swap_edges(to_mate, to_other)

    middle = planes // 2
    once_groups = [list(range(1, middle)), list(range(middle, planes - 1)), [-1, 0, planes - 1, planes]]
    base_groups = [list(range(middle)), list(range(middle, planes))]
    sides = neighbour_matrix(nx)
    onces = [
        once(sides, near, (), once_groups[0], "once_a"),
        once(sides, near, (), once_groups[1], "once_b"),
        once(sides, near, edges, once_groups[2], "once_c"),
    ]
    bases = [
        base(sides, near, onces, once_groups, group, name) for group, name in zip(base_groups, ("base_a", "base_b"))
    ]
    share = sum_over_ring(first, second, pieces, [[onces[0]], [onces[1]], [onces[2]]])
    pencils = across(share).reshape(SIDES * nz, nx)
    (early, tail), late = gather_over_ring(
        across(solve(pencils, x_table, z_table, ny, planes)),
        [[bases[0]], [bases[1]]],
        functools.partial(early_potential, v_local, y_table),
    )
    v_planes = swap_edges(*outer_potential(early, tail, late), same_on_orb=True)
    new_re, new_im, open_ends = inner_update(
        sides, early, tail, late, near, onces, once_groups, bases, base_groups
    )
    return tuple(close_ends(new_re, new_im, open_ends, v_planes, edges))


def solution(mesh):
    orbs, slabs = mesh.devices.shape
    mesh = Mesh(mesh.devices.reshape(SIDES, orbs // SIDES, slabs), ("y", "z", "slab"))
    orb = ("y", "z")
    placed = (
        P(orb, "slab", None, None),
        P(orb, "slab", None, None),
        P("slab", None, None),
        P("slab", orb, None),
    )
    return jax.shard_map(
        on_device,
        mesh=mesh,
        in_specs=placed,
        out_specs=(P(orb, "slab", None, None), P(orb, "slab", None, None)),
        check_vma=False,
    )
```

```python
import functools
import math

import jax
import jax.numpy as jnp
import numpy as np
from jax import lax
from jax.experimental import pallas as pl
from jax.experimental.pallas import tpu as pltpu
from jax.sharding import Mesh
from jax.sharding import PartitionSpec as P

SPACING = 0.5
TIME_STEP = 0.02
HALF_SQ = 0.5 * TIME_STEP * TIME_STEP
KINETIC = -0.5 / (SPACING * SPACING)
HIGHEST = lax.Precision.HIGHEST
SIDES = 2
MIB = 1 << 20
VMEM = pl.BlockSpec(memory_space=pltpu.VMEM)
ANY = pl.BlockSpec(memory_space=pl.ANY)


def cas_table(length):
    index = np.arange(length)
    angles = (index[:, None] * index[None, :] % length) * (2.0 * math.pi / length)
    return jnp.asarray((np.cos(angles) + np.sin(angles)).astype(np.float32))


def dot(left, right):
    return jnp.dot(left, right, precision=HIGHEST, preferred_element_type=jnp.float32)


def terms(value, count):
    found = []
    for _ in range(count):
        found.append(value.astype(jnp.bfloat16))
        value = value - found[-1].astype(jnp.float32)
    return found


def dot_three(left, right):
    (a, b), (c, d) = terms(left, 2), terms(right, 2)

    def one(x, y):
        return jnp.dot(x, y, preferred_element_type=jnp.float32)

    return one(a, c) + (one(a, d) + one(b, c))


def shaped(*shape):
    return jax.ShapeDtypeStruct(shape, jnp.float32)


def plane_scratch(*lead, ny, nx):
    return pltpu.VMEM(lead + (ny, nx), jnp.float32)


def cost(microseconds):
    return pl.CostEstimate(flops=0, bytes_accessed=int(microseconds * 3.6e6), transcendentals=0)


def lower_core():
    return lax.rem(lax.axis_index("slab"), 2) == 0


def fill_rows(rows, table):
    ring = lax.axis_size("z")
    width = rows.shape[0] // ring
    z = lax.axis_index("z")
    step = 1 + lax.rem(z, 2) * (ring - 2)
    for offset in range(ring):
        start = pl.multiple_of(lax.rem(z + offset * step, ring) * width, width)
        rows[offset * width : (offset + 1) * width, :] = table[pl.ds(start, width), :]


def density_kernel(scale, psi_re, psi_im, ground, y_table, *refs):
    rho, rows, first, second, to_mate, to_other = refs[:6]
    near, table, own_ground, plane_sem, small_sem = refs[6:]
    planes = near.shape[1]
    groups = plane_sem.shape[1]
    part_planes = planes // groups
    small = [
        pltpu.make_async_copy(y_table, table, small_sem.at[0]),
        pltpu.make_async_copy(ground, own_ground, small_sem.at[1]),
    ]
    copies = []
    for group in range(groups):
        some = pl.ds(group * part_planes, part_planes)
        copies.append(
            [
                pltpu.make_async_copy(psi.at[0, some], near.at[part, some], plane_sem.at[part, group])
                for part, psi in enumerate((psi_re, psi_im))
            ]
        )
    for copy in copies[0] + small + sum(copies[1:], []):
        copy.start()
    for copy in small:
        copy.wait()
    fill_rows(rows, table)
    ground_rows = own_ground.shape[1]
    place = lax.axis_index("y") * lax.axis_size("z") + lax.axis_index("z")
    own = pl.ds(pl.multiple_of(place * ground_rows, ground_rows), ground_rows)
    width = first.shape[1] + second.shape[1]
    far = rows[rows.shape[0] // 2 : rows.shape[0] // 2 + width, :]
    for group in range(groups):
        for copy in copies[group]:
            copy.wait()
        some = range(group * part_planes, (group + 1) * part_planes)
        for z in some:
            re, im = near[0, z], near[1, z]
            rho[z] = scale * (re * re + im * im)
            rho[z, own, :] = rho[z, own, :] - own_ground[z]
        for z in some:
            image = dot(far, rho[z])
            first[z] = image[: first.shape[1]]
            second[z] = image[first.shape[1] :]
    lower = lower_core()

    def fill_edges(low_target, high_target):
        for part in range(2):
            for which in range(2):
                low_target[2 * part + which] = near[part, which]
                high_target[2 * part + which] = near[part, planes - 2 + which]

    pl.when(lower)(functools.partial(fill_edges, to_other, to_mate))
    pl.when(jnp.logical_not(lower))(functools.partial(fill_edges, to_mate, to_other))


def density(psi_re, psi_im, n_ground, y_table, total_orbs):
    _, planes, ny, nx = psi_re.shape
    half = ny // lax.axis_size("z") // 2
    shapes = [(planes, ny, nx), (ny, ny), (planes, half, nx), (planes, half, nx)] + [(4, ny, nx)] * 2
    far = [pltpu.with_memory_space_constraint(a, pltpu.HBM) for a in (psi_re, psi_im, n_ground, y_table)]
    return pl.pallas_call(
        functools.partial(density_kernel, 2.0 / total_orbs),
        in_specs=[ANY] * 4,
        out_specs=[VMEM] * len(shapes),
        out_shape=[pltpu.VMEM(shape, jnp.float32) for shape in shapes],
        scratch_shapes=[
            plane_scratch(2, planes, ny=ny, nx=nx),
            pltpu.VMEM((ny, ny), jnp.float32),
            pltpu.VMEM(n_ground.shape, jnp.float32),
            pltpu.SemaphoreType.DMA((2, 2)),
            pltpu.SemaphoreType.DMA((2,)),
        ],
        compiler_params=pltpu.CompilerParams(vmem_limit_bytes=8 * MIB),
        name="density",
    )(*far)


def shares_kernel(offsets, rho, rows, *pieces):
    width = pieces[0].shape[1]
    wanted = jnp.concatenate([rows[offset * width : (offset + 1) * width, :] for offset in offsets], axis=0)
    for z in range(rho.shape[0]):
        image = dot(wanted, rho[z])
        for index, piece in enumerate(pieces):
            piece[z] = image[index * width : (index + 1) * width]


def shares(offsets, rho, rows, name):
    planes, ny, nx = rho.shape
    width = ny // lax.axis_size("z")
    return pl.pallas_call(
        functools.partial(shares_kernel, offsets),
        in_specs=[VMEM] * 2,
        out_specs=[VMEM] * len(offsets),
        out_shape=[pltpu.VMEM((planes, width, nx), jnp.float32)] * len(offsets),
        compiler_params=pltpu.CompilerParams(vmem_limit_bytes=4 * MIB),
        cost_estimate=cost(0.3 * len(offsets)),
        name=name,
    )(rho, rows)


def share_kernel(own, up, down, out):
    for z in range(own.shape[0]):
        out[:, z, :] = own[z] + up[z] + down[z]


def add_shares(own, up, down):
    planes, rows, nx = own.shape
    return pl.pallas_call(
        share_kernel,
        in_specs=[VMEM] * 3,
        out_specs=VMEM,
        out_shape=shaped(rows, planes, nx),
        compiler_params=pltpu.CompilerParams(vmem_limit_bytes=4 * MIB),
        name="add_shares",
    )(own, up, down)


def wave_sq(freq_index, length):
    signed = jnp.where(freq_index * 2 <= length, freq_index, freq_index - length)
    wave_number = signed.astype(jnp.float32) * (2.0 * math.pi / (length * SPACING))
    return wave_number * wave_number


def solve_kernel(y_len, field, x_table, z_table, out):
    nz, nx = z_table.shape[0], x_table.shape[0]
    half = out.shape[0] // SIDES
    width = y_len // lax.axis_size("z")
    ky = lax.axis_index("z") * width + lax.axis_index("y") * lax.axis_size("slab") + lax.axis_index("slab")
    z_index = lax.broadcasted_iota(jnp.int32, (nz, nx), 0)
    x_index = lax.broadcasted_iota(jnp.int32, (nz, nx), 1)
    y_index = jnp.full((nz, nx), ky, jnp.int32)
    total = wave_sq(z_index, nz) + wave_sq(y_index, y_len) + wave_sq(x_index, nx)
    anchor = (z_index == 0) & (y_index == 0) & (x_index == 0)
    safe = jnp.where(anchor, jnp.float32(1.0), total)
    greens = jnp.where(anchor, jnp.float32(0.0), (4.0 * math.pi) / safe) * (1.0 / (nz * y_len * nx))
    rho = field[0:nz] + field[nz : 2 * nz]
    spectrum = dot(z_table[...], dot(rho, x_table[...]))
    solved = dot_three(dot_three(z_table[...], spectrum * greens), x_table[...])
    solved = solved.reshape((half,) + out.shape[1:])
    out[0:half] = solved
    out[half:] = solved


def solve(field, x_table, z_table, y_len, planes):
    rows, nx = field.shape
    return pl.pallas_call(
        functools.partial(solve_kernel, y_len),
        in_specs=[VMEM] * 3,
        out_specs=VMEM,
        out_shape=shaped(rows // planes, planes, nx),
        compiler_params=pltpu.CompilerParams(vmem_limit_bytes=8 * MIB),
        name="solve_xz",
    )(field, x_table, z_table)


def whole(plane):
    ref, lead = plane
    return ref[lead]


def neighbour_matrix(length):
    matrix = np.zeros((length, length), np.float32)
    index = np.arange(length)
    matrix[index, (index + 1) % length] = KINETIC
    matrix[index, (index - 1) % length] = KINETIC
    return jnp.asarray(matrix, jnp.bfloat16)


def kinetic(below, plane, above, sides):
    mid = whole(plane)
    high = mid.astype(jnp.bfloat16)
    rest = (mid - high.astype(jnp.float32)).astype(jnp.bfloat16)
    matrix = sides[...]
    along_x = jnp.dot(high, matrix, preferred_element_type=jnp.float32)
    along_x = along_x + jnp.dot(rest, matrix, preferred_element_type=jnp.float32)
    along_y = pltpu.roll(mid, 1, 0) + pltpu.roll(mid, mid.shape[0] - 1, 0)
    along_z = whole(below) + whole(above)
    return mid, along_x + (KINETIC * (along_y + along_z) - (6.0 * KINETIC) * mid)


def by_side(edges, run):
    mate, other = edges
    lower = lower_core()
    pl.when(lower)(functools.partial(run, other, mate))
    pl.when(jnp.logical_not(lower))(functools.partial(run, mate, other))


def psi_plane(fields, low, high, planes, part, z):
    if z < 0:
        return (low, (2 * part + z + 2,))
    if z >= planes:
        return (high, (2 * part + z - planes,))
    return (fields[part], (z,))


def once_kernel(planes, wanted, with_edges, sides, *refs):
    fields, edges, out = refs[:2], refs[2:-1], refs[-1]

    def run(low, high):
        at = functools.partial(psi_plane, fields, low, high, planes)
        for slot, z in enumerate(wanted):
            for part in range(2):
                _, value = kinetic(at(part, z - 1), at(part, z), at(part, z + 1), sides)
                out[part, slot] = value

    if with_edges:
        by_side(edges, run)
    else:
        run(None, None)


def once(sides, near, edges, wanted, name):
    planes, ny, nx = near[0].shape
    return pl.pallas_call(
        functools.partial(once_kernel, planes, wanted, bool(edges)),
        in_specs=[VMEM] * (3 + len(edges)),
        out_specs=VMEM,
        out_shape=shaped(2, len(wanted), ny, nx),
        compiler_params=pltpu.CompilerParams(vmem_limit_bytes=6 * MIB),
        cost_estimate=cost(0.3 * len(wanted)),
        name=name,
    )(sides, *near, *edges)


def once_plane(groups, refs, part, z):
    for ref, group in zip(refs, groups):
        if z in group:
            return (ref, (part, group.index(z)))


def base_kernel(groups, wanted, sides, re, im, *refs):
    onces, out = refs[:-1], refs[-1]
    at = functools.partial(once_plane, groups, onces)
    for slot, z in enumerate(wanted):
        first_re, second_re = kinetic(at(0, z - 1), at(0, z), at(0, z + 1), sides)
        first_im, second_im = kinetic(at(1, z - 1), at(1, z), at(1, z + 1), sides)
        out[0, slot] = re[z] + TIME_STEP * first_im - HALF_SQ * second_re
        out[1, slot] = im[z] - TIME_STEP * first_re - HALF_SQ * second_im


def base(sides, near, onces, groups, wanted, name):
    planes, ny, nx = near[0].shape
    return pl.pallas_call(
        functools.partial(base_kernel, groups, wanted),
        in_specs=[VMEM] * (3 + len(onces)),
        out_specs=VMEM,
        out_shape=shaped(2, len(wanted), ny, nx),
        compiler_params=pltpu.CompilerParams(vmem_limit_bytes=6 * MIB),
        cost_estimate=cost(0.4 * len(wanted)),
        name=name,
    )(sides, *near, *onces)


def ring_columns(table):
    ny = table.shape[1]
    return pltpu.roll(table[...], ny - lax.axis_index("z") * (ny // lax.axis_size("z")), 1)


LEFT_TERMS = (0, 0, 1, 1, 0, 2)
RIGHT_TERMS = (0, 1, 0, 1, 2, 0)


def early_kernel(v_local, table, *refs):
    hats, (pot, tail) = refs[:-2], refs[-2:]
    columns = ring_columns(table)
    width = hats[0].shape[0]
    first = columns.shape[1] // 2
    left = terms(columns[:, first : first + width], 3)
    tail[...] = jnp.concatenate([left[i] for i in LEFT_TERMS], axis=1)
    hats = list(hats)
    hats.insert(len(hats) // 2 + 1, None)
    even = lax.rem(lax.axis_index("z"), 2) == 0

    def fill(order):
        for z in range(v_local.shape[0]):
            rows = [jnp.zeros((width, columns.shape[1]), jnp.float32) if h is None else h[:, z, :] for h in order]
            pot[z] = v_local[z] + dot(columns, jnp.concatenate(rows, axis=0))

    pl.when(even)(functools.partial(fill, hats))
    pl.when(jnp.logical_not(even))(functools.partial(fill, hats[:1] + hats[:0:-1]))


def early_potential(v_local, table, hats):
    planes, ny, nx = v_local.shape
    width = ny // lax.axis_size("z")
    return pl.pallas_call(
        early_kernel,
        in_specs=[VMEM] * (2 + len(hats)),
        out_specs=[VMEM] * 2,
        out_shape=[shaped(planes, ny, nx), jax.ShapeDtypeStruct((ny, len(LEFT_TERMS) * width), jnp.bfloat16)],
        compiler_params=pltpu.CompilerParams(vmem_limit_bytes=6 * MIB),
        cost_estimate=cost(2.3),
        name="early_potential",
    )(v_local, table, *hats)


def potential_plane(early, tail, late, z):
    right = terms(jnp.concatenate([hat[:, z, :] for hat in late], axis=0), 3)
    stacked = jnp.concatenate([right[i] for i in RIGHT_TERMS], axis=0)
    return early[z] + jnp.dot(tail[...], stacked, preferred_element_type=jnp.float32)


def outer_kernel(early, tail, up, down, to_other, to_mate):
    first = potential_plane(early, tail, (up, down), 0)
    last = potential_plane(early, tail, (up, down), early.shape[0] - 1)
    lower = lower_core()
    to_mate[0] = jnp.where(lower, last, first)
    to_other[0] = jnp.where(lower, first, last)


def outer_potential(early, tail, late):
    planes, ny, nx = early.shape
    return pl.pallas_call(
        outer_kernel,
        in_specs=[VMEM] * (2 + len(late)),
        out_specs=[VMEM] * 2,
        out_shape=[shaped(1, ny, nx)] * 2,
        compiler_params=pltpu.CompilerParams(vmem_limit_bytes=4 * MIB),
        name="outer_potential",
    )(early, tail, *late)


def inner_kernel(once_groups, base_groups, *refs):
    refs = list(refs)
    sides, early, tail, late_up, late_down, re, im = [refs.pop(0) for _ in range(7)]
    onces = [refs.pop(0) for _ in once_groups]
    bases = [refs.pop(0) for _ in base_groups]
    out_re, out_im, open_ends, pot, work, stage, sem = refs
    planes = re.shape[0]
    fields = (re, im)
    at_once = functools.partial(once_plane, once_groups, onces)
    at_base = functools.partial(once_plane, base_groups, bases)
    work[:, 0] = jnp.zeros_like(work[:, 0])
    work[:, planes + 1] = jnp.zeros_like(work[:, planes + 1])

    def update_plane(z):
        here = pot[z]
        mids, seconds = [], []
        for part in range(2):
            mid, kin = kinetic((work, (part, z)), (work, (part, z + 1)), (work, (part, z + 2)), sides)
            mids.append(mid)
            seconds.append(kin + here * (whole(at_once(part, z)) + mid))
        new_re = whole(at_base(0, z)) + TIME_STEP * mids[1] - HALF_SQ * seconds[0]
        new_im = whole(at_base(1, z)) - TIME_STEP * mids[0] - HALF_SQ * seconds[1]
        return new_re, new_im

    copies = []

    def finish(z):
        new = update_plane(z)
        for part, out in enumerate((out_re, out_im)):
            if z in (0, planes - 1):
                open_ends[part, 0 if z == 0 else 1] = new[part]
            else:
                stage[part, z - 1] = new[part]
                copy = pltpu.make_async_copy(stage.at[part, z - 1], out.at[0, z], sem.at[part, z - 1])
                copy.start()
                copies.append(copy)

    for z in range(planes):
        here = potential_plane(early, tail, (late_up, late_down), z)
        pot[z] = here
        for part in range(2):
            work[part, z + 1] = here * fields[part][z]
        if z >= 1:
            finish(z - 1)
    finish(planes - 1)
    for copy in copies:
        copy.wait()


def inner_update(sides, early, tail, late, near, onces, once_groups, bases, base_groups):
    planes, ny, nx = early.shape
    operands = [sides, early, tail, *late, *near, *onces, *bases]
    full = shaped(1, planes, ny, nx)
    return pl.pallas_call(
        functools.partial(inner_kernel, once_groups, base_groups),
        in_specs=[VMEM] * len(operands),
        out_specs=[ANY, ANY, VMEM],
        out_shape=[full, full, shaped(2, 2, ny, nx)],
        scratch_shapes=[
            plane_scratch(planes, ny=ny, nx=nx),
            plane_scratch(2, planes + 2, ny=ny, nx=nx),
            plane_scratch(2, planes - 2, ny=ny, nx=nx),
            pltpu.SemaphoreType.DMA((2, planes - 2)),
        ],
        compiler_params=pltpu.CompilerParams(vmem_limit_bytes=14 * MIB),
        cost_estimate=cost(4.3),
        name="inner_update",
    )(*operands)


def close_kernel(open_ends, v_other, v_mate, mate, other, _re, _im, out_re, out_im, stage, sem):
    planes = out_re.shape[1]

    def run(below, above):
        for slot, ((v_ref, edge), first) in enumerate(((below, 1), (above, 0))):
            for part in range(2):
                beyond = v_ref[0] * edge[2 * part + first]
                stage[part, slot] = open_ends[part, slot] - (HALF_SQ * KINETIC) * beyond

    by_side(((v_mate, mate), (v_other, other)), run)
    copies = []
    for slot, z in enumerate((0, planes - 1)):
        for part, out in enumerate((out_re, out_im)):
            copy = pltpu.make_async_copy(stage.at[part, slot], out.at[0, z], sem.at[part, slot])
            copy.start()
            copies.append(copy)
    for copy in copies:
        copy.wait()


def close_ends(new_re, new_im, open_ends, v_planes, edges):
    v_planes = v_planes[::-1]
    _, _, ny, nx = open_ends.shape
    return pl.pallas_call(
        close_kernel,
        in_specs=[VMEM] * 5 + [ANY, ANY],
        out_specs=[ANY, ANY],
        out_shape=[shaped(*new_re.shape)] * 2,
        input_output_aliases={5: 0, 6: 1},
        scratch_shapes=[plane_scratch(2, 2, ny=ny, nx=nx), pltpu.SemaphoreType.DMA((2, 2))],
        compiler_params=pltpu.CompilerParams(vmem_limit_bytes=4 * MIB),
        name="close_ends",
    )(open_ends, *v_planes, *edges, new_re, new_im)


def swap_near(value):
    return lax.ppermute(value, "z", [(i, i ^ 1) for i in range(lax.axis_size("z"))])


def swap_far(value):
    count = lax.axis_size("z")
    return lax.ppermute(value, "z", [(i, (i - 1) % count if i % 2 == 0 else (i + 1) % count) for i in range(count)])


def swap_edges(to_mate, to_other, same_on_orb=False):
    count = lax.axis_size("slab")
    pairs = []
    for y in range(SIDES):
        for slab in range(count):
            other = (slab - 1) % count if slab % 2 == 0 else (slab + 1) % count
            crossing = slab * 2 // count != other * 2 // count
            side = (y + 1) % SIDES if crossing and same_on_orb else y
            pairs.append((y * count + slab, side * count + other))
    from_mate = lax.ppermute(to_mate, "slab", [(i, i ^ 1) for i in range(count)])
    from_other = lax.ppermute(to_other, ("y", "slab"), pairs)
    return from_mate, from_other


def after(value, *others):
    return lax.optimization_barrier((value,) + others)[0]


def sum_over_ring(first, second, pieces, beside):
    s0, s1, s2, s3, s5, s6, s7 = pieces
    half = first.shape[1]
    near, far = swap_near(first), swap_far(second)
    near = jnp.concatenate([s5[:, :half] + near, s5[:, half:]], axis=1)
    far = jnp.concatenate([s3[:, :half], s3[:, half:] + far], axis=1)
    near, far = swap_far(near), swap_near(far)
    near, far = after(near, *beside[0]), after(far, *beside[0])
    near, far = swap_near(near + s2), swap_far(far + s6)
    near, far = after(near, *beside[1]), after(far, *beside[1])
    near, far = swap_far(near + s7), swap_near(far + s1)
    near, far = after(near, *beside[2]), after(far, *beside[2])
    return add_shares(s0, near, far)


def gather_over_ring(block, beside, early):
    half = block.shape[0] // 2
    near1, far1 = swap_near(block), swap_far(block)
    near1, far1 = after(near1, *beside[0]), after(far1, *beside[0])
    near2, far2 = swap_near(far1), swap_far(near1)
    near2, far2 = after(near2, *beside[1]), after(far2, *beside[1])
    near3, far3 = swap_near(far2), swap_far(near2)
    near4, far4 = swap_near(far3[:half]), swap_far(near3[half:])
    made = early([block, near1, near2, near3, far3, far2, far1])
    return made, (after(near4, *made), far4)


def across(value):
    return lax.all_to_all(value, ("y", "slab"), split_axis=0, concat_axis=0, tiled=True)


def on_device(psi_re, psi_im, v_local, n_ground):
    total_orbs = psi_re.shape[0] * lax.axis_size("y") * lax.axis_size("z")
    planes, ny, nx = v_local.shape
    nz = planes * lax.axis_size("slab")
    y_table, x_table, z_table = cas_table(ny), cas_table(nx), cas_table(nz)

    rho, rows, first, second, to_mate, to_other = density(psi_re, psi_im, n_ground, y_table, total_orbs)
    s3, s5 = shares((3, 5), rho, rows, "shares_a")
    s0, s1, s2, s6, s7 = shares((0, 1, 2, 6, 7), rho, rows, "shares_b")
    pieces = (s0, s1, s2, s3, s5, s6, s7)
    near = (psi_re[0], psi_im[0])
    edges = swap_edges(to_mate, to_other)

    middle = planes // 2
    once_groups = [list(range(1, middle)), list(range(middle, planes - 1)), [-1, 0, planes - 1, planes]]
    base_groups = [list(range(middle)), list(range(middle, planes))]
    sides = neighbour_matrix(nx)
    onces = [
        once(sides, near, (), once_groups[0], "once_a"),
        once(sides, near, (), once_groups[1], "once_b"),
        once(sides, near, edges, once_groups[2], "once_c"),
    ]
    bases = [
        base(sides, near, onces, once_groups, group, name) for group, name in zip(base_groups, ("base_a", "base_b"))
    ]
    share = sum_over_ring(first, second, pieces, [[onces[0]], [onces[1]], [onces[2]]])
    pencils = across(share).reshape(SIDES * nz, nx)
    (early, tail), late = gather_over_ring(
        across(solve(pencils, x_table, z_table, ny, planes)),
        [[bases[0]], [bases[1]]],
        functools.partial(early_potential, v_local, y_table),
    )
    v_other, v_mate = outer_potential(early, tail, late)
    v_planes = swap_edges(v_mate, v_other, same_on_orb=True)
    new_re, new_im, open_ends = inner_update(
        sides, early, tail, late, near, onces, once_groups, bases, base_groups
    )
    return tuple(close_ends(new_re, new_im, open_ends, v_planes, edges))


def solution(mesh):
    orbs, slabs = mesh.devices.shape
    mesh = Mesh(mesh.devices.reshape(SIDES, orbs // SIDES, slabs), ("y", "z", "slab"))
    orb = ("y", "z")
    placed = (
        P(orb, "slab", None, None),
        P(orb, "slab", None, None),
        P("slab", None, None),
        P("slab", orb, None),
    )
    return jax.shard_map(
        on_device,
        mesh=mesh,
        in_specs=placed,
        out_specs=(P(orb, "slab", None, None), P(orb, "slab", None, None)),
        check_vma=False,
    )
```

```python
import functools
import math

import jax
import jax.numpy as jnp
import numpy as np
from jax import lax
from jax.experimental import pallas as pl
from jax.experimental.pallas import tpu as pltpu
from jax.sharding import Mesh
from jax.sharding import PartitionSpec as P

SPACING = 0.5
TIME_STEP = 0.02
HALF_SQ = 0.5 * TIME_STEP * TIME_STEP
KINETIC = -0.5 / (SPACING * SPACING)
HIGHEST = lax.Precision.HIGHEST
SIDES = 2
MIB = 1 << 20
VMEM = pl.BlockSpec(memory_space=pltpu.VMEM)
ANY = pl.BlockSpec(memory_space=pl.ANY)


def cas_table(length):
    index = np.arange(length)
    angles = (index[:, None] * index[None, :] % length) * (2.0 * math.pi / length)
    return jnp.asarray((np.cos(angles) + np.sin(angles)).astype(np.float32))


def dot(left, right):
    return jnp.dot(left, right, precision=HIGHEST, preferred_element_type=jnp.float32)


def terms(value, count):
    found = []
    for _ in range(count):
        found.append(value.astype(jnp.bfloat16))
        value = value - found[-1].astype(jnp.float32)
    return found


def dot_three(left, right):
    (a, b), (c, d) = terms(left, 2), terms(right, 2)

    def one(x, y):
        return jnp.dot(x, y, preferred_element_type=jnp.float32)

    return one(a, c) + (one(a, d) + one(b, c))


def shaped(*shape):
    return jax.ShapeDtypeStruct(shape, jnp.float32)


def plane_scratch(*lead, ny, nx):
    return pltpu.VMEM(lead + (ny, nx), jnp.float32)


def cost(microseconds):
    return pl.CostEstimate(flops=0, bytes_accessed=int(microseconds * 3.6e6), transcendentals=0)


def lower_core():
    return lax.rem(lax.axis_index("slab"), 2) == 0


def fill_rows(rows, table):
    ring = lax.axis_size("z")
    width = rows.shape[0] // ring
    z = lax.axis_index("z")
    step = 1 + lax.rem(z, 2) * (ring - 2)
    for offset in range(ring):
        start = pl.multiple_of(lax.rem(z + offset * step, ring) * width, width)
        rows[offset * width : (offset + 1) * width, :] = table[pl.ds(start, width), :]


def density_kernel(scale, psi_re, psi_im, ground, y_table, *refs):
    rho, rows, first, second, to_mate, to_other = refs[:6]
    near, table, own_ground, plane_sem, small_sem = refs[6:]
    planes = near.shape[1]
    groups = plane_sem.shape[1]
    part_planes = planes // groups
    small = [
        pltpu.make_async_copy(y_table, table, small_sem.at[0]),
        pltpu.make_async_copy(ground, own_ground, small_sem.at[1]),
    ]
    copies = []
    for group in range(groups):
        some = pl.ds(group * part_planes, part_planes)
        copies.append(
            [
                pltpu.make_async_copy(psi.at[0, some], near.at[part, some], plane_sem.at[part, group])
                for part, psi in enumerate((psi_re, psi_im))
            ]
        )
    for copy in copies[0] + small + sum(copies[1:], []):
        copy.start()
    for copy in small:
        copy.wait()
    fill_rows(rows, table)
    ground_rows = own_ground.shape[1]
    place = lax.axis_index("y") * lax.axis_size("z") + lax.axis_index("z")
    own = pl.ds(pl.multiple_of(place * ground_rows, ground_rows), ground_rows)
    width = first.shape[1] + second.shape[1]
    far = rows[rows.shape[0] // 2 : rows.shape[0] // 2 + width, :]
    for group in range(groups):
        for copy in copies[group]:
            copy.wait()
        some = range(group * part_planes, (group + 1) * part_planes)
        for z in some:
            re, im = near[0, z], near[1, z]
            rho[z] = scale * (re * re + im * im)
            rho[z, own, :] = rho[z, own, :] - own_ground[z]
        for z in some:
            image = dot(far, rho[z])
            first[z] = image[: first.shape[1]]
            second[z] = image[first.shape[1] :]
    lower = lower_core()

    def fill_edges(low_target, high_target):
        for part in range(2):
            for which in range(2):
                low_target[2 * part + which] = near[part, which]
                high_target[2 * part + which] = near[part, planes - 2 + which]

    pl.when(lower)(functools.partial(fill_edges, to_other, to_mate))
    pl.when(jnp.logical_not(lower))(functools.partial(fill_edges, to_mate, to_other))


def density(psi_re, psi_im, n_ground, y_table, total_orbs):
    _, planes, ny, nx = psi_re.shape
    half = ny // lax.axis_size("z") // 2
    shapes = [(planes, ny, nx), (ny, ny), (planes, half, nx), (planes, half, nx)] + [(4, ny, nx)] * 2
    far = [pltpu.with_memory_space_constraint(a, pltpu.HBM) for a in (psi_re, psi_im, n_ground, y_table)]
    return pl.pallas_call(
        functools.partial(density_kernel, 2.0 / total_orbs),
        in_specs=[ANY] * 4,
        out_specs=[VMEM] * len(shapes),
        out_shape=[pltpu.VMEM(shape, jnp.float32) for shape in shapes],
        scratch_shapes=[
            plane_scratch(2, planes, ny=ny, nx=nx),
            pltpu.VMEM((ny, ny), jnp.float32),
            pltpu.VMEM(n_ground.shape, jnp.float32),
            pltpu.SemaphoreType.DMA((2, 2)),
            pltpu.SemaphoreType.DMA((2,)),
        ],
        compiler_params=pltpu.CompilerParams(vmem_limit_bytes=8 * MIB),
        name="density",
    )(*far)


def shares_kernel(offsets, rho, rows, *pieces):
    width = pieces[0].shape[1]
    wanted = jnp.concatenate([rows[offset * width : (offset + 1) * width, :] for offset in offsets], axis=0)
    for z in range(rho.shape[0]):
        image = dot(wanted, rho[z])
        for index, piece in enumerate(pieces):
            piece[z] = image[index * width : (index + 1) * width]


def shares(offsets, rho, rows, name):
    planes, ny, nx = rho.shape
    width = ny // lax.axis_size("z")
    return pl.pallas_call(
        functools.partial(shares_kernel, offsets),
        in_specs=[VMEM] * 2,
        out_specs=[VMEM] * len(offsets),
        out_shape=[pltpu.VMEM((planes, width, nx), jnp.float32)] * len(offsets),
        compiler_params=pltpu.CompilerParams(vmem_limit_bytes=4 * MIB),
        cost_estimate=cost(0.3 * len(offsets)),
        name=name,
    )(rho, rows)


def share_kernel(own, up, down, out):
    for z in range(own.shape[0]):
        out[:, z, :] = own[z] + up[z] + down[z]


def add_shares(own, up, down):
    planes, rows, nx = own.shape
    return pl.pallas_call(
        share_kernel,
        in_specs=[VMEM] * 3,
        out_specs=VMEM,
        out_shape=shaped(rows, planes, nx),
        compiler_params=pltpu.CompilerParams(vmem_limit_bytes=4 * MIB),
        name="add_shares",
    )(own, up, down)


def wave_sq(freq_index, length):
    signed = jnp.where(freq_index * 2 <= length, freq_index, freq_index - length)
    wave_number = signed.astype(jnp.float32) * (2.0 * math.pi / (length * SPACING))
    return wave_number * wave_number


def solve_kernel(y_len, field, x_table, z_table, out):
    nz, nx = z_table.shape[0], x_table.shape[0]
    half = out.shape[0] // SIDES
    width = y_len // lax.axis_size("z")
    ky = lax.axis_index("z") * width + lax.axis_index("y") * lax.axis_size("slab") + lax.axis_index("slab")
    z_index = lax.broadcasted_iota(jnp.int32, (nz, nx), 0)
    x_index = lax.broadcasted_iota(jnp.int32, (nz, nx), 1)
    y_index = jnp.full((nz, nx), ky, jnp.int32)
    total = wave_sq(z_index, nz) + wave_sq(y_index, y_len) + wave_sq(x_index, nx)
    anchor = (z_index == 0) & (y_index == 0) & (x_index == 0)
    safe = jnp.where(anchor, jnp.float32(1.0), total)
    greens = jnp.where(anchor, jnp.float32(0.0), (4.0 * math.pi) / safe) * (1.0 / (nz * y_len * nx))
    rho = field[0:nz] + field[nz : 2 * nz]
    spectrum = dot(z_table[...], dot(rho, x_table[...]))
    solved = dot_three(dot_three(z_table[...], spectrum * greens), x_table[...])
    solved = solved.reshape((half,) + out.shape[1:])
    out[0:half] = solved
    out[half:] = solved


def solve(field, x_table, z_table, y_len, planes):
    rows, nx = field.shape
    return pl.pallas_call(
        functools.partial(solve_kernel, y_len),
        in_specs=[VMEM] * 3,
        out_specs=VMEM,
        out_shape=shaped(rows // planes, planes, nx),
        compiler_params=pltpu.CompilerParams(vmem_limit_bytes=8 * MIB),
        name="solve_xz",
    )(field, x_table, z_table)


def whole(plane):
    ref, lead = plane
    return ref[lead]


def neighbour_matrix(length):
    matrix = np.zeros((length, length), np.float32)
    index = np.arange(length)
    matrix[index, (index + 1) % length] = KINETIC
    matrix[index, (index - 1) % length] = KINETIC
    return jnp.asarray(matrix, jnp.bfloat16)


def kinetic(below, plane, above, sides):
    mid = whole(plane)
    high = mid.astype(jnp.bfloat16)
    rest = (mid - high.astype(jnp.float32)).astype(jnp.bfloat16)
    matrix = sides[...]
    along_x = jnp.dot(high, matrix, preferred_element_type=jnp.float32)
    along_x = along_x + jnp.dot(rest, matrix, preferred_element_type=jnp.float32)
    along_y = pltpu.roll(mid, 1, 0) + pltpu.roll(mid, mid.shape[0] - 1, 0)
    along_z = whole(below) + whole(above)
    return mid, along_x + (KINETIC * (along_y + along_z) - (6.0 * KINETIC) * mid)


def by_side(edges, run):
    mate, other = edges
    lower = lower_core()
    pl.when(lower)(functools.partial(run, other, mate))
    pl.when(jnp.logical_not(lower))(functools.partial(run, mate, other))


def psi_plane(fields, low, high, planes, part, z):
    if z < 0:
        return (low, (2 * part + z + 2,))
    if z >= planes:
        return (high, (2 * part + z - planes,))
    return (fields[part], (z,))


def once_kernel(planes, wanted, with_edges, sides, *refs):
    fields, edges, out = refs[:2], refs[2:-1], refs[-1]

    def run(low, high):
        at = functools.partial(psi_plane, fields, low, high, planes)
        for slot, z in enumerate(wanted):
            for part in range(2):
                _, value = kinetic(at(part, z - 1), at(part, z), at(part, z + 1), sides)
                out[part, slot] = value

    if with_edges:
        by_side(edges, run)
    else:
        run(None, None)


def once(sides, near, edges, wanted, name):
    planes, ny, nx = near[0].shape
    return pl.pallas_call(
        functools.partial(once_kernel, planes, wanted, bool(edges)),
        in_specs=[VMEM] * (3 + len(edges)),
        out_specs=VMEM,
        out_shape=shaped(2, len(wanted), ny, nx),
        compiler_params=pltpu.CompilerParams(vmem_limit_bytes=6 * MIB),
        cost_estimate=cost(0.3 * len(wanted)),
        name=name,
    )(sides, *near, *edges)


def once_plane(groups, refs, part, z):
    for ref, group in zip(refs, groups):
        if z in group:
            return (ref, (part, group.index(z)))


def base_kernel(groups, wanted, sides, re, im, *refs):
    onces, out = refs[:-1], refs[-1]
    at = functools.partial(once_plane, groups, onces)
    for slot, z in enumerate(wanted):
        first_re, second_re = kinetic(at(0, z - 1), at(0, z), at(0, z + 1), sides)
        first_im, second_im = kinetic(at(1, z - 1), at(1, z), at(1, z + 1), sides)
        out[0, slot] = re[z] + TIME_STEP * first_im - HALF_SQ * second_re
        out[1, slot] = im[z] - TIME_STEP * first_re - HALF_SQ * second_im


def base(sides, near, onces, groups, wanted, name):
    planes, ny, nx = near[0].shape
    return pl.pallas_call(
        functools.partial(base_kernel, groups, wanted),
        in_specs=[VMEM] * (3 + len(onces)),
        out_specs=VMEM,
        out_shape=shaped(2, len(wanted), ny, nx),
        compiler_params=pltpu.CompilerParams(vmem_limit_bytes=6 * MIB),
        cost_estimate=cost(0.4 * len(wanted)),
        name=name,
    )(sides, *near, *onces)


def ring_columns(table):
    ny = table.shape[1]
    return pltpu.roll(table[...], ny - lax.axis_index("z") * (ny // lax.axis_size("z")), 1)


LEFT_TERMS = (0, 0, 1, 1, 0, 2)
RIGHT_TERMS = (0, 1, 0, 1, 2, 0)


def early_kernel(v_local, table, *refs):
    hats, (pot, tail) = refs[:-2], refs[-2:]
    columns = ring_columns(table)
    width = hats[0].shape[0]
    first = columns.shape[1] // 2
    left = terms(columns[:, first : first + width], 3)
    tail[...] = jnp.concatenate([left[i] for i in LEFT_TERMS], axis=1)
    hats = list(hats)
    hats.insert(len(hats) // 2 + 1, None)
    even = lax.rem(lax.axis_index("z"), 2) == 0

    def fill(order):
        for z in range(v_local.shape[0]):
            rows = [jnp.zeros((width, columns.shape[1]), jnp.float32) if h is None else h[:, z, :] for h in order]
            pot[z] = v_local[z] + dot(columns, jnp.concatenate(rows, axis=0))

    pl.when(even)(functools.partial(fill, hats))
    pl.when(jnp.logical_not(even))(functools.partial(fill, hats[:1] + hats[:0:-1]))


def early_potential(v_local, table, hats):
    planes, ny, nx = v_local.shape
    width = ny // lax.axis_size("z")
    return pl.pallas_call(
        early_kernel,
        in_specs=[VMEM] * (2 + len(hats)),
        out_specs=[VMEM] * 2,
        out_shape=[shaped(planes, ny, nx), jax.ShapeDtypeStruct((ny, len(LEFT_TERMS) * width), jnp.bfloat16)],
        compiler_params=pltpu.CompilerParams(vmem_limit_bytes=6 * MIB),
        cost_estimate=cost(2.3),
        name="early_potential",
    )(v_local, table, *hats)


def potential_plane(early, tail, late, z):
    right = terms(jnp.concatenate([hat[:, z, :] for hat in late], axis=0), 3)
    stacked = jnp.concatenate([right[i] for i in RIGHT_TERMS], axis=0)
    return early[z] + jnp.dot(tail[...], stacked, preferred_element_type=jnp.float32)


def outer_kernel(early, tail, up, down, to_other, to_mate):
    first = potential_plane(early, tail, (up, down), 0)
    last = potential_plane(early, tail, (up, down), early.shape[0] - 1)
    lower = lower_core()
    to_mate[0] = jnp.where(lower, last, first)
    to_other[0] = jnp.where(lower, first, last)


def outer_potential(early, tail, late):
    planes, ny, nx = early.shape
    return pl.pallas_call(
        outer_kernel,
        in_specs=[VMEM] * (2 + len(late)),
        out_specs=[VMEM] * 2,
        out_shape=[shaped(1, ny, nx)] * 2,
        compiler_params=pltpu.CompilerParams(vmem_limit_bytes=4 * MIB),
        name="outer_potential",
    )(early, tail, *late)


def inner_kernel(once_groups, base_groups, *refs):
    refs = list(refs)
    sides, early, tail, late_up, late_down, re, im = [refs.pop(0) for _ in range(7)]
    onces = [refs.pop(0) for _ in once_groups]
    bases = [refs.pop(0) for _ in base_groups]
    out_re, out_im, open_ends, pot, work, stage, sem = refs
    planes = re.shape[0]
    fields = (re, im)
    at_once = functools.partial(once_plane, once_groups, onces)
    at_base = functools.partial(once_plane, base_groups, bases)
    work[:, 0] = jnp.zeros_like(work[:, 0])
    work[:, planes + 1] = jnp.zeros_like(work[:, planes + 1])

    def update_plane(z):
        here = pot[z]
        mids, seconds = [], []
        for part in range(2):
            mid, kin = kinetic((work, (part, z)), (work, (part, z + 1)), (work, (part, z + 2)), sides)
            mids.append(mid)
            seconds.append(kin + here * (whole(at_once(part, z)) + mid))
        new_re = whole(at_base(0, z)) + TIME_STEP * mids[1] - HALF_SQ * seconds[0]
        new_im = whole(at_base(1, z)) - TIME_STEP * mids[0] - HALF_SQ * seconds[1]
        return new_re, new_im

    copies = []

    def finish(z):
        new = update_plane(z)
        for part, out in enumerate((out_re, out_im)):
            if z in (0, planes - 1):
                open_ends[part, 0 if z == 0 else 1] = new[part]
            else:
                stage[part, z - 1] = new[part]
                copy = pltpu.make_async_copy(stage.at[part, z - 1], out.at[0, z], sem.at[part, z - 1])
                copy.start()
                copies.append(copy)

    for z in range(planes):
        here = potential_plane(early, tail, (late_up, late_down), z)
        pot[z] = here
        for part in range(2):
            work[part, z + 1] = here * fields[part][z]
        if z >= 1:
            finish(z - 1)
    finish(planes - 1)
    for copy in copies:
        copy.wait()


def inner_update(sides, early, tail, late, near, onces, once_groups, bases, base_groups):
    planes, ny, nx = early.shape
    operands = [sides, early, tail, *late, *near, *onces, *bases]
    full = shaped(1, planes, ny, nx)
    return pl.pallas_call(
        functools.partial(inner_kernel, once_groups, base_groups),
        in_specs=[VMEM] * len(operands),
        out_specs=[ANY, ANY, VMEM],
        out_shape=[full, full, shaped(2, 2, ny, nx)],
        scratch_shapes=[
            plane_scratch(planes, ny=ny, nx=nx),
            plane_scratch(2, planes + 2, ny=ny, nx=nx),
            plane_scratch(2, planes - 2, ny=ny, nx=nx),
            pltpu.SemaphoreType.DMA((2, planes - 2)),
        ],
        compiler_params=pltpu.CompilerParams(vmem_limit_bytes=14 * MIB),
        cost_estimate=cost(4.3),
        name="inner_update",
    )(*operands)


def close_kernel(open_ends, v_other, v_mate, mate, other, _re, _im, out_re, out_im, stage, sem):
    planes = out_re.shape[1]

    def run(below, above):
        for slot, ((v_ref, edge), first) in enumerate(((below, 1), (above, 0))):
            for part in range(2):
                beyond = v_ref[0] * edge[2 * part + first]
                stage[part, slot] = open_ends[part, slot] - (HALF_SQ * KINETIC) * beyond

    by_side(((v_mate, mate), (v_other, other)), run)
    copies = []
    for slot, z in enumerate((0, planes - 1)):
        for part, out in enumerate((out_re, out_im)):
            copy = pltpu.make_async_copy(stage.at[part, slot], out.at[0, z], sem.at[part, slot])
            copy.start()
            copies.append(copy)
    for copy in copies:
        copy.wait()


def close_ends(new_re, new_im, open_ends, v_planes, edges):
    v_planes = v_planes[::-1]
    _, _, ny, nx = open_ends.shape
    return pl.pallas_call(
        close_kernel,
        in_specs=[VMEM] * 5 + [ANY, ANY],
        out_specs=[ANY, ANY],
        out_shape=[shaped(*new_re.shape)] * 2,
        input_output_aliases={5: 0, 6: 1},
        scratch_shapes=[plane_scratch(2, 2, ny=ny, nx=nx), pltpu.SemaphoreType.DMA((2, 2))],
        compiler_params=pltpu.CompilerParams(vmem_limit_bytes=4 * MIB),
        name="close_ends",
    )(open_ends, *v_planes, *edges, new_re, new_im)


def swap_near(value):
    return lax.ppermute(value, "z", [(i, i ^ 1) for i in range(lax.axis_size("z"))])


def swap_far(value):
    count = lax.axis_size("z")
    return lax.ppermute(value, "z", [(i, (i - 1) % count if i % 2 == 0 else (i + 1) % count) for i in range(count)])


def swap_edges(to_mate, to_other, same_on_orb=False):
    count = lax.axis_size("slab")
    pairs = []
    for y in range(SIDES):
        for slab in range(count):
            other = (slab - 1) % count if slab % 2 == 0 else (slab + 1) % count
            crossing = slab * 2 // count != other * 2 // count
            side = (y + 1) % SIDES if crossing and same_on_orb else y
            pairs.append((y * count + slab, side * count + other))
    from_mate = lax.ppermute(to_mate, "slab", [(i, i ^ 1) for i in range(count)])
    from_other = lax.ppermute(to_other, ("y", "slab"), pairs)
    return from_mate, from_other


def after(value, *others):
    return lax.optimization_barrier((value,) + others)[0]


def sum_over_ring(first, second, pieces, beside):
    s0, s1, s2, s3, s5, s6, s7 = pieces
    half = first.shape[1]
    near, far = swap_near(first), swap_far(second)
    near = jnp.concatenate([s5[:, :half] + near, s5[:, half:]], axis=1)
    far = jnp.concatenate([s3[:, :half], s3[:, half:] + far], axis=1)
    near, far = swap_far(near), swap_near(far)
    near, far = after(near, *beside[0]), after(far, *beside[0])
    near, far = swap_near(near + s2), swap_far(far + s6)
    near, far = after(near, *beside[1]), after(far, *beside[1])
    near, far = swap_far(near + s7), swap_near(far + s1)
    return add_shares(s0, near, far)


def gather_over_ring(block, beside, early):
    half = block.shape[0] // 2
    near1, far1 = swap_near(block), swap_far(block)
    near1, far1 = after(near1, *beside[0]), after(far1, *beside[0])
    near2, far2 = swap_near(far1), swap_far(near1)
    near2, far2 = after(near2, *beside[1]), after(far2, *beside[1])
    near3, far3 = swap_near(far2), swap_far(near2)
    near3, far3 = after(near3, *beside[2]), after(far3, *beside[2])
    near4, far4 = swap_near(far3[:half]), swap_far(near3[half:])
    made = early([block, near1, near2, near3, far3, far2, far1])
    return made, (after(near4, *made), far4)


def across(value):
    return lax.all_to_all(value, ("y", "slab"), split_axis=0, concat_axis=0, tiled=True)


def on_device(psi_re, psi_im, v_local, n_ground):
    total_orbs = psi_re.shape[0] * lax.axis_size("y") * lax.axis_size("z")
    planes, ny, nx = v_local.shape
    nz = planes * lax.axis_size("slab")
    y_table, x_table, z_table = cas_table(ny), cas_table(nx), cas_table(nz)

    rho, rows, first, second, to_mate, to_other = density(psi_re, psi_im, n_ground, y_table, total_orbs)
    s3, s5 = shares((3, 5), rho, rows, "shares_a")
    s0, s1, s2, s6, s7 = shares((0, 1, 2, 6, 7), rho, rows, "shares_b")
    pieces = (s0, s1, s2, s3, s5, s6, s7)
    near = (psi_re[0], psi_im[0])
    edges = swap_edges(to_mate, to_other)

    middle = planes // 2
    once_groups = [list(range(1, middle)), list(range(middle, planes - 1)), [-1, 0, planes - 1, planes]]
    base_groups = [list(range(middle)), list(range(middle, planes))]
    sides = neighbour_matrix(nx)
    onces = [
        once(sides, near, (), once_groups[0], "once_a"),
        once(sides, near, (), once_groups[1], "once_b"),
        once(sides, near, edges, once_groups[2], "once_c"),
    ]
    bases = [
        base(sides, near, onces, once_groups, group, name) for group, name in zip(base_groups, ("base_a", "base_b"))
    ]
    share = sum_over_ring(first, second, pieces, [[onces[0]], [onces[1]]])
    pencils = across(share).reshape(SIDES * nz, nx)
    (early, tail), late = gather_over_ring(
        across(solve(pencils, x_table, z_table, ny, planes)),
        [[onces[2]], [bases[0]], [bases[1]]],
        functools.partial(early_potential, v_local, y_table),
    )
    v_other, v_mate = outer_potential(early, tail, late)
    v_planes = swap_edges(v_mate, v_other, same_on_orb=True)
    new_re, new_im, open_ends = inner_update(
        sides, early, tail, late, near, onces, once_groups, bases, base_groups
    )
    return tuple(close_ends(new_re, new_im, open_ends, v_planes, edges))


def solution(mesh):
    orbs, slabs = mesh.devices.shape
    mesh = Mesh(mesh.devices.reshape(SIDES, orbs // SIDES, slabs), ("y", "z", "slab"))
    orb = ("y", "z")
    placed = (
        P(orb, "slab", None, None),
        P(orb, "slab", None, None),
        P("slab", None, None),
        P("slab", orb, None),
    )
    return jax.shard_map(
        on_device,
        mesh=mesh,
        in_specs=placed,
        out_specs=(P(orb, "slab", None, None), P(orb, "slab", None, None)),
        check_vma=False,
    )
```

```python
import functools
import math

import jax
import jax.numpy as jnp
import numpy as np
from jax import lax
from jax.experimental import pallas as pl
from jax.experimental.pallas import tpu as pltpu
from jax.sharding import Mesh
from jax.sharding import PartitionSpec as P

SPACING = 0.5
TIME_STEP = 0.02
HALF_SQ = 0.5 * TIME_STEP * TIME_STEP
KINETIC = -0.5 / (SPACING * SPACING)
HIGHEST = lax.Precision.HIGHEST
SIDES = 2
MIB = 1 << 20
VMEM = pl.BlockSpec(memory_space=pltpu.VMEM)
ANY = pl.BlockSpec(memory_space=pl.ANY)


def cas_table(length):
    index = np.arange(length)
    angles = (index[:, None] * index[None, :] % length) * (2.0 * math.pi / length)
    return jnp.asarray((np.cos(angles) + np.sin(angles)).astype(np.float32))


def dot(left, right):
    return jnp.dot(left, right, precision=HIGHEST, preferred_element_type=jnp.float32)


def terms(value, count):
    found = []
    for _ in range(count):
        found.append(value.astype(jnp.bfloat16))
        value = value - found[-1].astype(jnp.float32)
    return found


def dot_three(left, right):
    (a, b), (c, d) = terms(left, 2), terms(right, 2)

    def one(x, y):
        return jnp.dot(x, y, preferred_element_type=jnp.float32)

    return one(a, c) + (one(a, d) + one(b, c))


def shaped(*shape):
    return jax.ShapeDtypeStruct(shape, jnp.float32)


def plane_scratch(*lead, ny, nx):
    return pltpu.VMEM(lead + (ny, nx), jnp.float32)


def cost(microseconds):
    return pl.CostEstimate(flops=0, bytes_accessed=int(microseconds * 3.6e6), transcendentals=0)


def lower_core():
    return lax.rem(lax.axis_index("slab"), 2) == 0


def fill_rows(rows, table):
    ring = lax.axis_size("z")
    width = rows.shape[0] // ring
    z = lax.axis_index("z")
    step = 1 + lax.rem(z, 2) * (ring - 2)
    for offset in range(ring):
        start = pl.multiple_of(lax.rem(z + offset * step, ring) * width, width)
        rows[offset * width : (offset + 1) * width, :] = table[pl.ds(start, width), :]


def density_kernel(scale, psi_re, psi_im, ground, y_table, *refs):
    rho, rows, first, second, to_mate, to_other = refs[:6]
    near, table, own_ground, plane_sem, small_sem = refs[6:]
    planes = near.shape[1]
    groups = plane_sem.shape[1]
    part_planes = planes // groups
    small = [
        pltpu.make_async_copy(y_table, table, small_sem.at[0]),
        pltpu.make_async_copy(ground, own_ground, small_sem.at[1]),
    ]
    copies = []
    for group in range(groups):
        some = pl.ds(group * part_planes, part_planes)
        copies.append(
            [
                pltpu.make_async_copy(psi.at[0, some], near.at[part, some], plane_sem.at[part, group])
                for part, psi in enumerate((psi_re, psi_im))
            ]
        )
    for copy in copies[0] + small + sum(copies[1:], []):
        copy.start()
    for copy in small:
        copy.wait()
    fill_rows(rows, table)
    ground_rows = own_ground.shape[1]
    place = lax.axis_index("y") * lax.axis_size("z") + lax.axis_index("z")
    own = pl.ds(pl.multiple_of(place * ground_rows, ground_rows), ground_rows)
    width = first.shape[1] + second.shape[1]
    far = rows[rows.shape[0] // 2 : rows.shape[0] // 2 + width, :]
    for group in range(groups):
        for copy in copies[group]:
            copy.wait()
        some = range(group * part_planes, (group + 1) * part_planes)
        for z in some:
            re, im = near[0, z], near[1, z]
            rho[z] = scale * (re * re + im * im)
            rho[z, own, :] = rho[z, own, :] - own_ground[z]
        for z in some:
            image = dot(far, rho[z])
            first[z] = image[: first.shape[1]]
            second[z] = image[first.shape[1] :]
    lower = lower_core()

    def fill_edges(low_target, high_target):
        for part in range(2):
            for which in range(2):
                low_target[2 * part + which] = near[part, which]
                high_target[2 * part + which] = near[part, planes - 2 + which]

    pl.when(lower)(functools.partial(fill_edges, to_other, to_mate))
    pl.when(jnp.logical_not(lower))(functools.partial(fill_edges, to_mate, to_other))


def density(psi_re, psi_im, n_ground, y_table, total_orbs):
    _, planes, ny, nx = psi_re.shape
    half = ny // lax.axis_size("z") // 2
    shapes = [(planes, ny, nx), (ny, ny), (planes, half, nx), (planes, half, nx)] + [(4, ny, nx)] * 2
    far = [pltpu.with_memory_space_constraint(a, pltpu.HBM) for a in (psi_re, psi_im, n_ground, y_table)]
    return pl.pallas_call(
        functools.partial(density_kernel, 2.0 / total_orbs),
        in_specs=[ANY] * 4,
        out_specs=[VMEM] * len(shapes),
        out_shape=[pltpu.VMEM(shape, jnp.float32) for shape in shapes],
        scratch_shapes=[
            plane_scratch(2, planes, ny=ny, nx=nx),
            pltpu.VMEM((ny, ny), jnp.float32),
            pltpu.VMEM(n_ground.shape, jnp.float32),
            pltpu.SemaphoreType.DMA((2, 2)),
            pltpu.SemaphoreType.DMA((2,)),
        ],
        compiler_params=pltpu.CompilerParams(vmem_limit_bytes=8 * MIB),
        name="density",
    )(*far)


def shares_kernel(offsets, rho, rows, *pieces):
    width = pieces[0].shape[1]
    wanted = jnp.concatenate([rows[offset * width : (offset + 1) * width, :] for offset in offsets], axis=0)
    for z in range(rho.shape[0]):
        image = dot(wanted, rho[z])
        for index, piece in enumerate(pieces):
            piece[z] = image[index * width : (index + 1) * width]


def shares(offsets, rho, rows, name):
    planes, ny, nx = rho.shape
    width = ny // lax.axis_size("z")
    return pl.pallas_call(
        functools.partial(shares_kernel, offsets),
        in_specs=[VMEM] * 2,
        out_specs=[VMEM] * len(offsets),
        out_shape=[pltpu.VMEM((planes, width, nx), jnp.float32)] * len(offsets),
        compiler_params=pltpu.CompilerParams(vmem_limit_bytes=4 * MIB),
        cost_estimate=cost(0.3 * len(offsets)),
        name=name,
    )(rho, rows)


def share_kernel(own, up, down, out):
    for z in range(own.shape[0]):
        out[:, z, :] = own[z] + up[z] + down[z]


def add_shares(own, up, down):
    planes, rows, nx = own.shape
    return pl.pallas_call(
        share_kernel,
        in_specs=[VMEM] * 3,
        out_specs=VMEM,
        out_shape=shaped(rows, planes, nx),
        compiler_params=pltpu.CompilerParams(vmem_limit_bytes=4 * MIB),
        name="add_shares",
    )(own, up, down)


def wave_sq(freq_index, length):
    signed = jnp.where(freq_index * 2 <= length, freq_index, freq_index - length)
    wave_number = signed.astype(jnp.float32) * (2.0 * math.pi / (length * SPACING))
    return wave_number * wave_number


def solve_kernel(y_len, field, x_table, z_table, out):
    nz, nx = z_table.shape[0], x_table.shape[0]
    half = out.shape[0] // SIDES
    width = y_len // lax.axis_size("z")
    ky = lax.axis_index("z") * width + lax.axis_index("slab") * SIDES + lax.axis_index("y")
    z_index = lax.broadcasted_iota(jnp.int32, (nz, nx), 0)
    x_index = lax.broadcasted_iota(jnp.int32, (nz, nx), 1)
    y_index = jnp.full((nz, nx), ky, jnp.int32)
    total = wave_sq(z_index, nz) + wave_sq(y_index, y_len) + wave_sq(x_index, nx)
    anchor = (z_index == 0) & (y_index == 0) & (x_index == 0)
    safe = jnp.where(anchor, jnp.float32(1.0), total)
    greens = jnp.where(anchor, jnp.float32(0.0), (4.0 * math.pi) / safe) * (1.0 / (nz * y_len * nx))
    planes = out.shape[1]
    pairs = field[...].reshape(half, SIDES * planes, nx)
    rho = (pairs[:, :planes] + pairs[:, planes:]).reshape(nz, nx)
    spectrum = dot(z_table[...], dot(rho, x_table[...]))
    solved = dot_three(dot_three(z_table[...], spectrum * greens), x_table[...])
    solved = solved.reshape((half,) + out.shape[1:])
    for slab in range(half):
        for side in range(SIDES):
            out[SIDES * slab + side] = solved[slab]


def solve(field, x_table, z_table, y_len, planes):
    rows, nx = field.shape
    return pl.pallas_call(
        functools.partial(solve_kernel, y_len),
        in_specs=[VMEM] * 3,
        out_specs=VMEM,
        out_shape=shaped(rows // planes, planes, nx),
        compiler_params=pltpu.CompilerParams(vmem_limit_bytes=8 * MIB),
        name="solve_xz",
    )(field, x_table, z_table)


def whole(plane):
    ref, lead = plane
    return ref[lead]


def neighbour_matrix(length):
    matrix = np.zeros((length, length), np.float32)
    index = np.arange(length)
    matrix[index, (index + 1) % length] = KINETIC
    matrix[index, (index - 1) % length] = KINETIC
    return jnp.asarray(matrix, jnp.bfloat16)


def kinetic(below, plane, above, sides):
    mid = whole(plane)
    high = mid.astype(jnp.bfloat16)
    rest = (mid - high.astype(jnp.float32)).astype(jnp.bfloat16)
    matrix = sides[...]
    along_x = jnp.dot(high, matrix, preferred_element_type=jnp.float32)
    along_x = along_x + jnp.dot(rest, matrix, preferred_element_type=jnp.float32)
    along_y = pltpu.roll(mid, 1, 0) + pltpu.roll(mid, mid.shape[0] - 1, 0)
    along_z = whole(below) + whole(above)
    return mid, along_x + (KINETIC * (along_y + along_z) - (6.0 * KINETIC) * mid)


def by_side(edges, run):
    mate, other = edges
    lower = lower_core()
    pl.when(lower)(functools.partial(run, other, mate))
    pl.when(jnp.logical_not(lower))(functools.partial(run, mate, other))


def psi_plane(fields, low, high, planes, part, z):
    if z < 0:
        return (low, (2 * part + z + 2,))
    if z >= planes:
        return (high, (2 * part + z - planes,))
    return (fields[part], (z,))


def once_kernel(planes, wanted, with_edges, sides, *refs):
    fields, edges, out = refs[:2], refs[2:-1], refs[-1]

    def run(low, high):
        at = functools.partial(psi_plane, fields, low, high, planes)
        for slot, z in enumerate(wanted):
            for part in range(2):
                _, value = kinetic(at(part, z - 1), at(part, z), at(part, z + 1), sides)
                out[part, slot] = value

    if with_edges:
        by_side(edges, run)
    else:
        run(None, None)


def once(sides, near, edges, wanted, name):
    planes, ny, nx = near[0].shape
    return pl.pallas_call(
        functools.partial(once_kernel, planes, wanted, bool(edges)),
        in_specs=[VMEM] * (3 + len(edges)),
        out_specs=VMEM,
        out_shape=shaped(2, len(wanted), ny, nx),
        compiler_params=pltpu.CompilerParams(vmem_limit_bytes=6 * MIB),
        cost_estimate=cost(0.3 * len(wanted)),
        name=name,
    )(sides, *near, *edges)


def once_plane(groups, refs, part, z):
    for ref, group in zip(refs, groups):
        if z in group:
            return (ref, (part, group.index(z)))


def base_kernel(groups, wanted, sides, re, im, *refs):
    onces, out = refs[:-1], refs[-1]
    at = functools.partial(once_plane, groups, onces)
    for slot, z in enumerate(wanted):
        first_re, second_re = kinetic(at(0, z - 1), at(0, z), at(0, z + 1), sides)
        first_im, second_im = kinetic(at(1, z - 1), at(1, z), at(1, z + 1), sides)
        out[0, slot] = re[z] + TIME_STEP * first_im - HALF_SQ * second_re
        out[1, slot] = im[z] - TIME_STEP * first_re - HALF_SQ * second_im


def base(sides, near, onces, groups, wanted, name):
    planes, ny, nx = near[0].shape
    return pl.pallas_call(
        functools.partial(base_kernel, groups, wanted),
        in_specs=[VMEM] * (3 + len(onces)),
        out_specs=VMEM,
        out_shape=shaped(2, len(wanted), ny, nx),
        compiler_params=pltpu.CompilerParams(vmem_limit_bytes=6 * MIB),
        cost_estimate=cost(0.4 * len(wanted)),
        name=name,
    )(sides, *near, *onces)


def ring_columns(table):
    ny = table.shape[1]
    return pltpu.roll(table[...], ny - lax.axis_index("z") * (ny // lax.axis_size("z")), 1)


LEFT_TERMS = (0, 0, 1, 1, 0, 2)
RIGHT_TERMS = (0, 1, 0, 1, 2, 0)


def early_kernel(v_local, table, *refs):
    hats, (pot, tail) = refs[:-2], refs[-2:]
    columns = ring_columns(table)
    width = hats[0].shape[0]
    first = columns.shape[1] // 2
    left = terms(columns[:, first : first + width], 3)
    tail[...] = jnp.concatenate([left[i] for i in LEFT_TERMS], axis=1)
    hats = list(hats)
    hats.insert(len(hats) // 2 + 1, None)
    even = lax.rem(lax.axis_index("z"), 2) == 0

    def fill(order):
        for z in range(v_local.shape[0]):
            rows = [jnp.zeros((width, columns.shape[1]), jnp.float32) if h is None else h[:, z, :] for h in order]
            pot[z] = v_local[z] + dot(columns, jnp.concatenate(rows, axis=0))

    pl.when(even)(functools.partial(fill, hats))
    pl.when(jnp.logical_not(even))(functools.partial(fill, hats[:1] + hats[:0:-1]))


def early_potential(v_local, table, hats):
    planes, ny, nx = v_local.shape
    width = ny // lax.axis_size("z")
    return pl.pallas_call(
        early_kernel,
        in_specs=[VMEM] * (2 + len(hats)),
        out_specs=[VMEM] * 2,
        out_shape=[shaped(planes, ny, nx), jax.ShapeDtypeStruct((ny, len(LEFT_TERMS) * width), jnp.bfloat16)],
        compiler_params=pltpu.CompilerParams(vmem_limit_bytes=6 * MIB),
        cost_estimate=cost(2.3),
        name="early_potential",
    )(v_local, table, *hats)


def potential_plane(early, tail, late, z):
    right = terms(jnp.concatenate([hat[:, z, :] for hat in late], axis=0), 3)
    stacked = jnp.concatenate([right[i] for i in RIGHT_TERMS], axis=0)
    return early[z] + jnp.dot(tail[...], stacked, preferred_element_type=jnp.float32)


def outer_kernel(early, tail, up, down, to_other, to_mate):
    first = potential_plane(early, tail, (up, down), 0)
    last = potential_plane(early, tail, (up, down), early.shape[0] - 1)
    lower = lower_core()
    to_mate[0] = jnp.where(lower, last, first)
    to_other[0] = jnp.where(lower, first, last)


def outer_potential(early, tail, late):
    planes, ny, nx = early.shape
    return pl.pallas_call(
        outer_kernel,
        in_specs=[VMEM] * (2 + len(late)),
        out_specs=[VMEM] * 2,
        out_shape=[shaped(1, ny, nx)] * 2,
        compiler_params=pltpu.CompilerParams(vmem_limit_bytes=4 * MIB),
        name="outer_potential",
    )(early, tail, *late)


def inner_kernel(once_groups, base_groups, *refs):
    refs = list(refs)
    sides, early, tail, late_up, late_down, re, im = [refs.pop(0) for _ in range(7)]
    onces = [refs.pop(0) for _ in once_groups]
    bases = [refs.pop(0) for _ in base_groups]
    out_re, out_im, open_ends, pot, work, stage, sem = refs
    planes = re.shape[0]
    fields = (re, im)
    at_once = functools.partial(once_plane, once_groups, onces)
    at_base = functools.partial(once_plane, base_groups, bases)
    work[:, 0] = jnp.zeros_like(work[:, 0])
    work[:, planes + 1] = jnp.zeros_like(work[:, planes + 1])

    def update_plane(z):
        here = pot[z]
        mids, seconds = [], []
        for part in range(2):
            mid, kin = kinetic((work, (part, z)), (work, (part, z + 1)), (work, (part, z + 2)), sides)
            mids.append(mid)
            seconds.append(kin + here * (whole(at_once(part, z)) + mid))
        new_re = whole(at_base(0, z)) + TIME_STEP * mids[1] - HALF_SQ * seconds[0]
        new_im = whole(at_base(1, z)) - TIME_STEP * mids[0] - HALF_SQ * seconds[1]
        return new_re, new_im

    copies = []

    def finish(z):
        new = update_plane(z)
        for part, out in enumerate((out_re, out_im)):
            if z in (0, planes - 1):
                open_ends[part, 0 if z == 0 else 1] = new[part]
            else:
                stage[part, z - 1] = new[part]
                copy = pltpu.make_async_copy(stage.at[part, z - 1], out.at[0, z], sem.at[part, z - 1])
                copy.start()
                copies.append(copy)

    for z in range(planes):
        here = potential_plane(early, tail, (late_up, late_down), z)
        pot[z] = here
        for part in range(2):
            work[part, z + 1] = here * fields[part][z]
        if z >= 1:
            finish(z - 1)
    finish(planes - 1)
    for copy in copies:
        copy.wait()


def inner_update(sides, early, tail, late, near, onces, once_groups, bases, base_groups):
    planes, ny, nx = early.shape
    operands = [sides, early, tail, *late, *near, *onces, *bases]
    full = shaped(1, planes, ny, nx)
    return pl.pallas_call(
        functools.partial(inner_kernel, once_groups, base_groups),
        in_specs=[VMEM] * len(operands),
        out_specs=[ANY, ANY, VMEM],
        out_shape=[full, full, shaped(2, 2, ny, nx)],
        scratch_shapes=[
            plane_scratch(planes, ny=ny, nx=nx),
            plane_scratch(2, planes + 2, ny=ny, nx=nx),
            plane_scratch(2, planes - 2, ny=ny, nx=nx),
            pltpu.SemaphoreType.DMA((2, planes - 2)),
        ],
        compiler_params=pltpu.CompilerParams(vmem_limit_bytes=14 * MIB),
        cost_estimate=cost(4.3),
        name="inner_update",
    )(*operands)


def close_kernel(open_ends, v_other, v_mate, mate, other, _re, _im, out_re, out_im, stage, sem):
    planes = out_re.shape[1]

    def run(below, above):
        for slot, ((v_ref, edge), first) in enumerate(((below, 1), (above, 0))):
            for part in range(2):
                beyond = v_ref[0] * edge[2 * part + first]
                stage[part, slot] = open_ends[part, slot] - (HALF_SQ * KINETIC) * beyond

    by_side(((v_mate, mate), (v_other, other)), run)
    copies = []
    for slot, z in enumerate((0, planes - 1)):
        for part, out in enumerate((out_re, out_im)):
            copy = pltpu.make_async_copy(stage.at[part, slot], out.at[0, z], sem.at[part, slot])
            copy.start()
            copies.append(copy)
    for copy in copies:
        copy.wait()


def close_ends(new_re, new_im, open_ends, v_planes, edges):
    v_planes = v_planes[::-1]
    _, _, ny, nx = open_ends.shape
    return pl.pallas_call(
        close_kernel,
        in_specs=[VMEM] * 5 + [ANY, ANY],
        out_specs=[ANY, ANY],
        out_shape=[shaped(*new_re.shape)] * 2,
        input_output_aliases={5: 0, 6: 1},
        scratch_shapes=[plane_scratch(2, 2, ny=ny, nx=nx), pltpu.SemaphoreType.DMA((2, 2))],
        compiler_params=pltpu.CompilerParams(vmem_limit_bytes=4 * MIB),
        name="close_ends",
    )(open_ends, *v_planes, *edges, new_re, new_im)


def swap_near(value):
    return lax.ppermute(value, "z", [(i, i ^ 1) for i in range(lax.axis_size("z"))])


def swap_far(value):
    count = lax.axis_size("z")
    return lax.ppermute(value, "z", [(i, (i - 1) % count if i % 2 == 0 else (i + 1) % count) for i in range(count)])


def swap_edges(to_mate, to_other, same_on_orb=False):
    count = lax.axis_size("slab")
    pairs = []
    for y in range(SIDES):
        for slab in range(count):
            other = (slab - 1) % count if slab % 2 == 0 else (slab + 1) % count
            crossing = slab * 2 // count != other * 2 // count
            side = (y + 1) % SIDES if crossing and same_on_orb else y
            pairs.append((y * count + slab, side * count + other))
    from_mate = lax.ppermute(to_mate, "slab", [(i, i ^ 1) for i in range(count)])
    from_other = lax.ppermute(to_other, ("y", "slab"), pairs)
    return from_mate, from_other


def after(value, *others):
    return lax.optimization_barrier((value,) + others)[0]


def sum_over_ring(first, second, pieces, beside):
    s0, s1, s2, s3, s5, s6, s7 = pieces
    half = first.shape[1]
    near, far = swap_near(first), swap_far(second)
    near = jnp.concatenate([s5[:, :half] + near, s5[:, half:]], axis=1)
    far = jnp.concatenate([s3[:, :half], s3[:, half:] + far], axis=1)
    near, far = swap_far(near), swap_near(far)
    near, far = after(near, *beside[0]), after(far, *beside[0])
    near, far = swap_near(near + s2), swap_far(far + s6)
    near, far = after(near, *beside[1]), after(far, *beside[1])
    near, far = swap_far(near + s7), swap_near(far + s1)
    return add_shares(s0, near, far)


def gather_over_ring(block, beside, early):
    half = block.shape[0] // 2
    near1, far1 = swap_near(block), swap_far(block)
    near1, far1 = after(near1, *beside[0]), after(far1, *beside[0])
    near2, far2 = swap_near(far1), swap_far(near1)
    near2, far2 = after(near2, *beside[1]), after(far2, *beside[1])
    near3, far3 = swap_near(far2), swap_far(near2)
    near3, far3 = after(near3, *beside[2]), after(far3, *beside[2])
    near4, far4 = swap_near(far3[:half]), swap_far(near3[half:])
    made = early([block, near1, near2, near3, far3, far2, far1])
    return made, (after(near4, *made), far4)


def across(value):
    return lax.all_to_all(value, ("slab", "y"), split_axis=0, concat_axis=0, tiled=True)


def on_device(psi_re, psi_im, v_local, n_ground):
    total_orbs = psi_re.shape[0] * lax.axis_size("y") * lax.axis_size("z")
    planes, ny, nx = v_local.shape
    nz = planes * lax.axis_size("slab")
    y_table, x_table, z_table = cas_table(ny), cas_table(nx), cas_table(nz)

    rho, rows, first, second, to_mate, to_other = density(psi_re, psi_im, n_ground, y_table, total_orbs)
    s3, s5 = shares((3, 5), rho, rows, "shares_a")
    s0, s1, s2, s6, s7 = shares((0, 1, 2, 6, 7), rho, rows, "shares_b")
    pieces = (s0, s1, s2, s3, s5, s6, s7)
    near = (psi_re[0], psi_im[0])
    edges = swap_edges(to_mate, to_other)

    middle = planes // 2
    once_groups = [list(range(1, middle)), list(range(middle, planes - 1)), [-1, 0, planes - 1, planes]]
    base_groups = [list(range(middle)), list(range(middle, planes))]
    sides = neighbour_matrix(nx)
    onces = [
        once(sides, near, (), once_groups[0], "once_a"),
        once(sides, near, (), once_groups[1], "once_b"),
        once(sides, near, edges, once_groups[2], "once_c"),
    ]
    bases = [
        base(sides, near, onces, once_groups, group, name) for group, name in zip(base_groups, ("base_a", "base_b"))
    ]
    share = sum_over_ring(first, second, pieces, [[onces[0]], [onces[1]]])
    pencils = across(share).reshape(SIDES * nz, nx)
    (early, tail), late = gather_over_ring(
        across(solve(pencils, x_table, z_table, ny, planes)),
        [[onces[2]], [bases[0]], [bases[1]]],
        functools.partial(early_potential, v_local, y_table),
    )
    v_other, v_mate = outer_potential(early, tail, late)
    v_planes = swap_edges(v_mate, v_other, same_on_orb=True)
    new_re, new_im, open_ends = inner_update(
        sides, early, tail, late, near, onces, once_groups, bases, base_groups
    )
    return tuple(close_ends(new_re, new_im, open_ends, v_planes, edges))


def solution(mesh):
    orbs, slabs = mesh.devices.shape
    mesh = Mesh(mesh.devices.reshape(SIDES, orbs // SIDES, slabs), ("y", "z", "slab"))
    orb = ("y", "z")
    placed = (
        P(orb, "slab", None, None),
        P(orb, "slab", None, None),
        P("slab", None, None),
        P("slab", orb, None),
    )
    return jax.shard_map(
        on_device,
        mesh=mesh,
        in_specs=placed,
        out_specs=(P(orb, "slab", None, None), P(orb, "slab", None, None)),
        check_vma=False,
    )
```

```python
import functools
import math

import jax
import jax.numpy as jnp
import numpy as np
from jax import lax
from jax.experimental import pallas as pl
from jax.experimental.pallas import tpu as pltpu
from jax.sharding import Mesh
from jax.sharding import PartitionSpec as P

SPACING = 0.5
TIME_STEP = 0.02
HALF_SQ = 0.5 * TIME_STEP * TIME_STEP
KINETIC = -0.5 / (SPACING * SPACING)
HIGHEST = lax.Precision.HIGHEST
SIDES = 2
MIB = 1 << 20
VMEM = pl.BlockSpec(memory_space=pltpu.VMEM)
ANY = pl.BlockSpec(memory_space=pl.ANY)


def cas_table(length):
    index = np.arange(length)
    angles = (index[:, None] * index[None, :] % length) * (2.0 * math.pi / length)
    return jnp.asarray((np.cos(angles) + np.sin(angles)).astype(np.float32))


def dot(left, right):
    return jnp.dot(left, right, precision=HIGHEST, preferred_element_type=jnp.float32)


def terms(value, count):
    found = []
    for _ in range(count):
        found.append(value.astype(jnp.bfloat16))
        value = value - found[-1].astype(jnp.float32)
    return found


def dot_three(left, right):
    (a, b), (c, d) = terms(left, 2), terms(right, 2)

    def one(x, y):
        return jnp.dot(x, y, preferred_element_type=jnp.float32)

    return one(a, c) + (one(a, d) + one(b, c))


def shaped(*shape):
    return jax.ShapeDtypeStruct(shape, jnp.float32)


def plane_scratch(*lead, ny, nx):
    return pltpu.VMEM(lead + (ny, nx), jnp.float32)


def cost(microseconds):
    return pl.CostEstimate(flops=0, bytes_accessed=int(microseconds * 3.6e6), transcendentals=0)


def lower_core():
    return lax.rem(lax.axis_index("slab"), 2) == 0


def fill_rows(rows, table):
    ring = lax.axis_size("z")
    width = rows.shape[0] // ring
    z = lax.axis_index("z")
    step = 1 + lax.rem(z, 2) * (ring - 2)
    for offset in range(ring):
        start = pl.multiple_of(lax.rem(z + offset * step, ring) * width, width)
        rows[offset * width : (offset + 1) * width, :] = table[pl.ds(start, width), :]


def density_kernel(scale, psi_re, psi_im, ground, y_table, *refs):
    rho, rows, first, second, to_mate, to_other = refs[:6]
    near, table, own_ground, plane_sem, small_sem = refs[6:]
    planes = near.shape[1]
    groups = plane_sem.shape[1]
    part_planes = planes // groups
    small = [
        pltpu.make_async_copy(y_table, table, small_sem.at[0]),
        pltpu.make_async_copy(ground, own_ground, small_sem.at[1]),
    ]
    copies = []
    for group in range(groups):
        some = pl.ds(group * part_planes, part_planes)
        copies.append(
            [
                pltpu.make_async_copy(psi.at[0, some], near.at[part, some], plane_sem.at[part, group])
                for part, psi in enumerate((psi_re, psi_im))
            ]
        )
    for copy in copies[0] + small + sum(copies[1:], []):
        copy.start()
    for copy in small:
        copy.wait()
    fill_rows(rows, table)
    ground_rows = own_ground.shape[1]
    place = lax.axis_index("y") * lax.axis_size("z") + lax.axis_index("z")
    own = pl.ds(pl.multiple_of(place * ground_rows, ground_rows), ground_rows)
    width = first.shape[1] + second.shape[1]
    far = rows[rows.shape[0] // 2 : rows.shape[0] // 2 + width, :]
    for group in range(groups):
        for copy in copies[group]:
            copy.wait()
        some = range(group * part_planes, (group + 1) * part_planes)
        for z in some:
            re, im = near[0, z], near[1, z]
            rho[z] = scale * (re * re + im * im)
            rho[z, own, :] = rho[z, own, :] - own_ground[z]
        for z in some:
            image = dot(far, rho[z])
            first[z] = image[: first.shape[1]]
            second[z] = image[first.shape[1] :]
    lower = lower_core()

    def fill_edges(low_target, high_target):
        for part in range(2):
            for which in range(2):
                low_target[2 * part + which] = near[part, which]
                high_target[2 * part + which] = near[part, planes - 2 + which]

    pl.when(lower)(functools.partial(fill_edges, to_other, to_mate))
    pl.when(jnp.logical_not(lower))(functools.partial(fill_edges, to_mate, to_other))


def density(psi_re, psi_im, n_ground, y_table, total_orbs):
    _, planes, ny, nx = psi_re.shape
    half = ny // lax.axis_size("z") // 2
    shapes = [(planes, ny, nx), (ny, ny), (planes, half, nx), (planes, half, nx)] + [(4, ny, nx)] * 2
    far = [pltpu.with_memory_space_constraint(a, pltpu.HBM) for a in (psi_re, psi_im, n_ground, y_table)]
    return pl.pallas_call(
        functools.partial(density_kernel, 2.0 / total_orbs),
        in_specs=[ANY] * 4,
        out_specs=[VMEM] * len(shapes),
        out_shape=[pltpu.VMEM(shape, jnp.float32) for shape in shapes],
        scratch_shapes=[
            plane_scratch(2, planes, ny=ny, nx=nx),
            pltpu.VMEM((ny, ny), jnp.float32),
            pltpu.VMEM(n_ground.shape, jnp.float32),
            pltpu.SemaphoreType.DMA((2, 2)),
            pltpu.SemaphoreType.DMA((2,)),
        ],
        compiler_params=pltpu.CompilerParams(vmem_limit_bytes=8 * MIB),
        name="density",
    )(*far)


def shares_kernel(offsets, rho, rows, *pieces):
    width = pieces[0].shape[1]
    wanted = jnp.concatenate([rows[offset * width : (offset + 1) * width, :] for offset in offsets], axis=0)
    for z in range(rho.shape[0]):
        image = dot(wanted, rho[z])
        for index, piece in enumerate(pieces):
            piece[z] = image[index * width : (index + 1) * width]


def shares(offsets, rho, rows, name):
    planes, ny, nx = rho.shape
    width = ny // lax.axis_size("z")
    return pl.pallas_call(
        functools.partial(shares_kernel, offsets),
        in_specs=[VMEM] * 2,
        out_specs=[VMEM] * len(offsets),
        out_shape=[pltpu.VMEM((planes, width, nx), jnp.float32)] * len(offsets),
        compiler_params=pltpu.CompilerParams(vmem_limit_bytes=4 * MIB),
        cost_estimate=cost(0.3 * len(offsets)),
        name=name,
    )(rho, rows)


def share_kernel(own, up, down, out):
    for z in range(own.shape[0]):
        out[:, z, :] = own[z] + up[z] + down[z]


def add_shares(own, up, down):
    planes, rows, nx = own.shape
    return pl.pallas_call(
        share_kernel,
        in_specs=[VMEM] * 3,
        out_specs=VMEM,
        out_shape=shaped(rows, planes, nx),
        compiler_params=pltpu.CompilerParams(vmem_limit_bytes=4 * MIB),
        name="add_shares",
    )(own, up, down)


def wave_sq(freq_index, length):
    signed = jnp.where(freq_index * 2 <= length, freq_index, freq_index - length)
    wave_number = signed.astype(jnp.float32) * (2.0 * math.pi / (length * SPACING))
    return wave_number * wave_number


def solve_kernel(y_len, field, x_table, z_table, out):
    nz, nx = z_table.shape[0], x_table.shape[0]
    half = out.shape[0] // SIDES
    width = y_len // lax.axis_size("z")
    ky = lax.axis_index("z") * width + lax.axis_index("slab") * SIDES + lax.axis_index("y")
    z_index = lax.broadcasted_iota(jnp.int32, (nz, nx), 0)
    x_index = lax.broadcasted_iota(jnp.int32, (nz, nx), 1)
    y_index = jnp.full((nz, nx), ky, jnp.int32)
    total = wave_sq(z_index, nz) + wave_sq(y_index, y_len) + wave_sq(x_index, nx)
    anchor = (z_index == 0) & (y_index == 0) & (x_index == 0)
    safe = jnp.where(anchor, jnp.float32(1.0), total)
    greens = jnp.where(anchor, jnp.float32(0.0), (4.0 * math.pi) / safe) * (1.0 / (nz * y_len * nx))
    planes = out.shape[1]
    pairs = field[...].reshape(half, SIDES * planes, nx)
    rho = (pairs[:, :planes] + pairs[:, planes:]).reshape(nz, nx)
    spectrum = dot(z_table[...], dot(rho, x_table[...]))
    solved = dot_three(dot_three(z_table[...], spectrum * greens), x_table[...])
    solved = solved.reshape((half,) + out.shape[1:])
    for slab in range(half):
        for side in range(SIDES):
            out[SIDES * slab + side] = solved[slab]


def solve(field, x_table, z_table, y_len, planes):
    rows, nx = field.shape
    return pl.pallas_call(
        functools.partial(solve_kernel, y_len),
        in_specs=[VMEM] * 3,
        out_specs=VMEM,
        out_shape=shaped(rows // planes, planes, nx),
        compiler_params=pltpu.CompilerParams(vmem_limit_bytes=8 * MIB),
        name="solve_xz",
    )(field, x_table, z_table)


def whole(plane):
    ref, lead = plane
    return ref[lead]


def neighbour_matrix(length):
    matrix = np.zeros((length, length), np.float32)
    index = np.arange(length)
    matrix[index, (index + 1) % length] = KINETIC
    matrix[index, (index - 1) % length] = KINETIC
    return jnp.asarray(matrix, jnp.bfloat16)


def kinetic(below, plane, above, sides):
    mid = whole(plane)
    high = mid.astype(jnp.bfloat16)
    rest = (mid - high.astype(jnp.float32)).astype(jnp.bfloat16)
    matrix = sides[...]
    along_x = jnp.dot(high, matrix, preferred_element_type=jnp.float32)
    along_x = along_x + jnp.dot(rest, matrix, preferred_element_type=jnp.float32)
    along_y = pltpu.roll(mid, 1, 0) + pltpu.roll(mid, mid.shape[0] - 1, 0)
    along_z = whole(below) + whole(above)
    return mid, along_x + (KINETIC * (along_y + along_z) - (6.0 * KINETIC) * mid)


def by_side(edges, run):
    mate, other = edges
    lower = lower_core()
    pl.when(lower)(functools.partial(run, other, mate))
    pl.when(jnp.logical_not(lower))(functools.partial(run, mate, other))


def psi_plane(fields, low, high, planes, part, z):
    if z < 0:
        return (low, (2 * part + z + 2,))
    if z >= planes:
        return (high, (2 * part + z - planes,))
    return (fields[part], (z,))


def once_kernel(planes, wanted, with_edges, sides, *refs):
    fields, edges, out = refs[:2], refs[2:-1], refs[-1]

    def run(low, high):
        at = functools.partial(psi_plane, fields, low, high, planes)
        for slot, z in enumerate(wanted):
            for part in range(2):
                _, value = kinetic(at(part, z - 1), at(part, z), at(part, z + 1), sides)
                out[part, slot] = value

    if with_edges:
        by_side(edges, run)
    else:
        run(None, None)


def once(sides, near, edges, wanted, name):
    planes, ny, nx = near[0].shape
    return pl.pallas_call(
        functools.partial(once_kernel, planes, wanted, bool(edges)),
        in_specs=[VMEM] * (3 + len(edges)),
        out_specs=VMEM,
        out_shape=shaped(2, len(wanted), ny, nx),
        compiler_params=pltpu.CompilerParams(vmem_limit_bytes=6 * MIB),
        cost_estimate=cost(0.3 * len(wanted)),
        name=name,
    )(sides, *near, *edges)


def once_plane(groups, refs, part, z):
    for ref, group in zip(refs, groups):
        if z in group:
            return (ref, (part, group.index(z)))


def base_kernel(groups, wanted, sides, re, im, *refs):
    onces, out = refs[:-1], refs[-1]
    at = functools.partial(once_plane, groups, onces)
    for slot, z in enumerate(wanted):
        first_re, second_re = kinetic(at(0, z - 1), at(0, z), at(0, z + 1), sides)
        first_im, second_im = kinetic(at(1, z - 1), at(1, z), at(1, z + 1), sides)
        out[0, slot] = re[z] + TIME_STEP * first_im - HALF_SQ * second_re
        out[1, slot] = im[z] - TIME_STEP * first_re - HALF_SQ * second_im


def base(sides, near, onces, groups, wanted, name):
    planes, ny, nx = near[0].shape
    return pl.pallas_call(
        functools.partial(base_kernel, groups, wanted),
        in_specs=[VMEM] * (3 + len(onces)),
        out_specs=VMEM,
        out_shape=shaped(2, len(wanted), ny, nx),
        compiler_params=pltpu.CompilerParams(vmem_limit_bytes=6 * MIB),
        cost_estimate=cost(0.4 * len(wanted)),
        name=name,
    )(sides, *near, *onces)


def ring_columns(table):
    ny = table.shape[1]
    return pltpu.roll(table[...], ny - lax.axis_index("z") * (ny // lax.axis_size("z")), 1)


LEFT_TERMS = (0, 0, 1, 1, 0, 2)
RIGHT_TERMS = (0, 1, 0, 1, 2, 0)


def early_kernel(v_local, table, *refs):
    hats, (pot, tail) = refs[:-2], refs[-2:]
    columns = ring_columns(table)
    width = hats[0].shape[0]
    first = columns.shape[1] // 2
    left = terms(columns[:, first : first + width], 3)
    tail[...] = jnp.concatenate([left[i] for i in LEFT_TERMS], axis=1)
    hats = list(hats)
    hats.insert(len(hats) // 2 + 1, None)
    even = lax.rem(lax.axis_index("z"), 2) == 0

    high, low = terms(columns, 2)

    def one(left, right):
        return jnp.dot(left, right, preferred_element_type=jnp.float32)

    def fill(order):
        for z in range(v_local.shape[0]):
            rows = [jnp.zeros((width, columns.shape[1]), jnp.float32) if h is None else h[:, z, :] for h in order]
            upper, lower = terms(jnp.concatenate(rows, axis=0), 2)
            pot[z] = v_local[z] + (one(high, upper) + (one(high, lower) + one(low, upper)))

    pl.when(even)(functools.partial(fill, hats))
    pl.when(jnp.logical_not(even))(functools.partial(fill, hats[:1] + hats[:0:-1]))


def early_potential(v_local, table, hats):
    planes, ny, nx = v_local.shape
    width = ny // lax.axis_size("z")
    return pl.pallas_call(
        early_kernel,
        in_specs=[VMEM] * (2 + len(hats)),
        out_specs=[VMEM] * 2,
        out_shape=[shaped(planes, ny, nx), jax.ShapeDtypeStruct((ny, len(LEFT_TERMS) * width), jnp.bfloat16)],
        compiler_params=pltpu.CompilerParams(vmem_limit_bytes=6 * MIB),
        cost_estimate=cost(2.3),
        name="early_potential",
    )(v_local, table, *hats)


def potential_plane(early, tail, late, z):
    right = terms(jnp.concatenate([hat[:, z, :] for hat in late], axis=0), 3)
    stacked = jnp.concatenate([right[i] for i in RIGHT_TERMS], axis=0)
    return early[z] + jnp.dot(tail[...], stacked, preferred_element_type=jnp.float32)


def outer_kernel(early, tail, up, down, to_other, to_mate):
    first = potential_plane(early, tail, (up, down), 0)
    last = potential_plane(early, tail, (up, down), early.shape[0] - 1)
    lower = lower_core()
    to_mate[0] = jnp.where(lower, last, first)
    to_other[0] = jnp.where(lower, first, last)


def outer_potential(early, tail, late):
    planes, ny, nx = early.shape
    return pl.pallas_call(
        outer_kernel,
        in_specs=[VMEM] * (2 + len(late)),
        out_specs=[VMEM] * 2,
        out_shape=[shaped(1, ny, nx)] * 2,
        compiler_params=pltpu.CompilerParams(vmem_limit_bytes=4 * MIB),
        name="outer_potential",
    )(early, tail, *late)


def inner_kernel(once_groups, base_groups, *refs):
    refs = list(refs)
    sides, early, tail, late_up, late_down, re, im = [refs.pop(0) for _ in range(7)]
    onces = [refs.pop(0) for _ in once_groups]
    bases = [refs.pop(0) for _ in base_groups]
    out_re, out_im, open_ends, pot, work, stage, sem = refs
    planes = re.shape[0]
    fields = (re, im)
    at_once = functools.partial(once_plane, once_groups, onces)
    at_base = functools.partial(once_plane, base_groups, bases)
    work[:, 0] = jnp.zeros_like(work[:, 0])
    work[:, planes + 1] = jnp.zeros_like(work[:, planes + 1])

    def update_plane(z):
        here = pot[z]
        mids, seconds = [], []
        for part in range(2):
            mid, kin = kinetic((work, (part, z)), (work, (part, z + 1)), (work, (part, z + 2)), sides)
            mids.append(mid)
            seconds.append(kin + here * (whole(at_once(part, z)) + mid))
        new_re = whole(at_base(0, z)) + TIME_STEP * mids[1] - HALF_SQ * seconds[0]
        new_im = whole(at_base(1, z)) - TIME_STEP * mids[0] - HALF_SQ * seconds[1]
        return new_re, new_im

    copies = []

    def finish(z):
        new = update_plane(z)
        for part, out in enumerate((out_re, out_im)):
            if z in (0, planes - 1):
                open_ends[part, 0 if z == 0 else 1] = new[part]
            else:
                stage[part, z - 1] = new[part]
                copy = pltpu.make_async_copy(stage.at[part, z - 1], out.at[0, z], sem.at[part, z - 1])
                copy.start()
                copies.append(copy)

    for z in range(planes):
        here = potential_plane(early, tail, (late_up, late_down), z)
        pot[z] = here
        for part in range(2):
            work[part, z + 1] = here * fields[part][z]
        if z >= 1:
            finish(z - 1)
    finish(planes - 1)
    for copy in copies:
        copy.wait()


def inner_update(sides, early, tail, late, near, onces, once_groups, bases, base_groups):
    planes, ny, nx = early.shape
    operands = [sides, early, tail, *late, *near, *onces, *bases]
    full = shaped(1, planes, ny, nx)
    return pl.pallas_call(
        functools.partial(inner_kernel, once_groups, base_groups),
        in_specs=[VMEM] * len(operands),
        out_specs=[ANY, ANY, VMEM],
        out_shape=[full, full, shaped(2, 2, ny, nx)],
        scratch_shapes=[
            plane_scratch(planes, ny=ny, nx=nx),
            plane_scratch(2, planes + 2, ny=ny, nx=nx),
            plane_scratch(2, planes - 2, ny=ny, nx=nx),
            pltpu.SemaphoreType.DMA((2, planes - 2)),
        ],
        compiler_params=pltpu.CompilerParams(vmem_limit_bytes=14 * MIB),
        cost_estimate=cost(4.3),
        name="inner_update",
    )(*operands)


def close_kernel(open_ends, v_other, v_mate, mate, other, _re, _im, out_re, out_im, stage, sem):
    planes = out_re.shape[1]

    def run(below, above):
        for slot, ((v_ref, edge), first) in enumerate(((below, 1), (above, 0))):
            for part in range(2):
                beyond = v_ref[0] * edge[2 * part + first]
                stage[part, slot] = open_ends[part, slot] - (HALF_SQ * KINETIC) * beyond

    by_side(((v_mate, mate), (v_other, other)), run)
    copies = []
    for slot, z in enumerate((0, planes - 1)):
        for part, out in enumerate((out_re, out_im)):
            copy = pltpu.make_async_copy(stage.at[part, slot], out.at[0, z], sem.at[part, slot])
            copy.start()
            copies.append(copy)
    for copy in copies:
        copy.wait()


def close_ends(new_re, new_im, open_ends, v_planes, edges):
    v_planes = v_planes[::-1]
    _, _, ny, nx = open_ends.shape
    return pl.pallas_call(
        close_kernel,
        in_specs=[VMEM] * 5 + [ANY, ANY],
        out_specs=[ANY, ANY],
        out_shape=[shaped(*new_re.shape)] * 2,
        input_output_aliases={5: 0, 6: 1},
        scratch_shapes=[plane_scratch(2, 2, ny=ny, nx=nx), pltpu.SemaphoreType.DMA((2, 2))],
        compiler_params=pltpu.CompilerParams(vmem_limit_bytes=4 * MIB),
        name="close_ends",
    )(open_ends, *v_planes, *edges, new_re, new_im)


def swap_near(value):
    return lax.ppermute(value, "z", [(i, i ^ 1) for i in range(lax.axis_size("z"))])


def swap_far(value):
    count = lax.axis_size("z")
    return lax.ppermute(value, "z", [(i, (i - 1) % count if i % 2 == 0 else (i + 1) % count) for i in range(count)])


def swap_edges(to_mate, to_other, same_on_orb=False):
    count = lax.axis_size("slab")
    pairs = []
    for y in range(SIDES):
        for slab in range(count):
            other = (slab - 1) % count if slab % 2 == 0 else (slab + 1) % count
            crossing = slab * 2 // count != other * 2 // count
            side = (y + 1) % SIDES if crossing and same_on_orb else y
            pairs.append((y * count + slab, side * count + other))
    from_mate = lax.ppermute(to_mate, "slab", [(i, i ^ 1) for i in range(count)])
    from_other = lax.ppermute(to_other, ("y", "slab"), pairs)
    return from_mate, from_other


def after(value, *others):
    return lax.optimization_barrier((value,) + others)[0]


def sum_over_ring(first, second, pieces, beside):
    s0, s1, s2, s3, s5, s6, s7 = pieces
    half = first.shape[1]
    near, far = swap_near(first), swap_far(second)
    near = jnp.concatenate([s5[:, :half] + near, s5[:, half:]], axis=1)
    far = jnp.concatenate([s3[:, :half], s3[:, half:] + far], axis=1)
    near, far = swap_far(near), swap_near(far)
    near, far = after(near, *beside[0]), after(far, *beside[0])
    near, far = swap_near(near + s2), swap_far(far + s6)
    near, far = after(near, *beside[1]), after(far, *beside[1])
    near, far = swap_far(near + s7), swap_near(far + s1)
    return add_shares(s0, near, far)


def gather_over_ring(block, beside, early):
    half = block.shape[0] // 2
    near1, far1 = swap_near(block), swap_far(block)
    near1, far1 = after(near1, *beside[0]), after(far1, *beside[0])
    near2, far2 = swap_near(far1), swap_far(near1)
    near2, far2 = after(near2, *beside[1]), after(far2, *beside[1])
    near3, far3 = swap_near(far2), swap_far(near2)
    near3, far3 = after(near3, *beside[2]), after(far3, *beside[2])
    near4, far4 = swap_near(far3[:half]), swap_far(near3[half:])
    made = early([block, near1, near2, near3, far3, far2, far1])
    return made, (after(near4, *made), far4)


def across(value):
    return lax.all_to_all(value, ("slab", "y"), split_axis=0, concat_axis=0, tiled=True)


def on_device(psi_re, psi_im, v_local, n_ground):
    total_orbs = psi_re.shape[0] * lax.axis_size("y") * lax.axis_size("z")
    planes, ny, nx = v_local.shape
    nz = planes * lax.axis_size("slab")
    y_table, x_table, z_table = cas_table(ny), cas_table(nx), cas_table(nz)

    rho, rows, first, second, to_mate, to_other = density(psi_re, psi_im, n_ground, y_table, total_orbs)
    s3, s5 = shares((3, 5), rho, rows, "shares_a")
    s0, s1, s2, s6, s7 = shares((0, 1, 2, 6, 7), rho, rows, "shares_b")
    pieces = (s0, s1, s2, s3, s5, s6, s7)
    near = (psi_re[0], psi_im[0])
    edges = swap_edges(to_mate, to_other)

    middle = planes // 2
    once_groups = [list(range(1, middle)), list(range(middle, planes - 1)), [-1, 0, planes - 1, planes]]
    base_groups = [list(range(middle)), list(range(middle, planes))]
    sides = neighbour_matrix(nx)
    onces = [
        once(sides, near, (), once_groups[0], "once_a"),
        once(sides, near, (), once_groups[1], "once_b"),
        once(sides, near, edges, once_groups[2], "once_c"),
    ]
    bases = [
        base(sides, near, onces, once_groups, group, name) for group, name in zip(base_groups, ("base_a", "base_b"))
    ]
    share = sum_over_ring(first, second, pieces, [[onces[0]], [onces[1]]])
    pencils = across(share).reshape(SIDES * nz, nx)
    (early, tail), late = gather_over_ring(
        across(solve(pencils, x_table, z_table, ny, planes)),
        [[onces[2]], [bases[0]], [bases[1]]],
        functools.partial(early_potential, v_local, y_table),
    )
    v_other, v_mate = outer_potential(early, tail, late)
    v_planes = swap_edges(v_mate, v_other, same_on_orb=True)
    new_re, new_im, open_ends = inner_update(
        sides, early, tail, late, near, onces, once_groups, bases, base_groups
    )
    return tuple(close_ends(new_re, new_im, open_ends, v_planes, edges))


def solution(mesh):
    orbs, slabs = mesh.devices.shape
    mesh = Mesh(mesh.devices.reshape(SIDES, orbs // SIDES, slabs), ("y", "z", "slab"))
    orb = ("y", "z")
    placed = (
        P(orb, "slab", None, None),
        P(orb, "slab", None, None),
        P("slab", None, None),
        P("slab", orb, None),
    )
    return jax.shard_map(
        on_device,
        mesh=mesh,
        in_specs=placed,
        out_specs=(P(orb, "slab", None, None), P(orb, "slab", None, None)),
        check_vma=False,
    )
```
